256 devices in a mesh: atom: 32 (over x, y, core), aux: 8 (over z).
Axes of the slice: x: 4, y: 4, z: 8, core: 2. Of those that a mesh axis runs over, the one named last changes fastest.
Arguments:
- integrals: bfloat16 [64, 8192, 512], P('aux', 'atom'), may hold values from -0.25 to 0.25
- coeffs: bfloat16 [8192, 2, 384], P('atom'), may hold values from -6 to 6
- metric: bfloat16 [64, 8], P('aux'), may hold values from -0.84852814 to 1.4, as said below
- atom_sizes: int32 [32, 32], P('atom'), may hold values from 1 to 16, 256 in all within a row
- pair_device: int32 [1024, 1], P('atom'), may hold values from 0 to 31; in each aligned block of 32 rows (0 to 31, 32 to 63, ...) at most 2 rows name the same one
- pair_atom: int32 [1024], P('atom'), may hold values from 0 to 31
Outputs:
- exchange_term: float32 [8192, 2, 384], P('atom', None, 'aux')
The draws below stay inside these ranges and needn't reach their ends.
Inputs may be any that keep to these rules, and one draw needn't show every extreme that they name: `metric`: within each block of 8 rows, entry (q, p) is zero where q % 8 > p. `atom_sizes`: each row sums to 256. `pair_device`: rows 2k and 2k + 1 are the two ends of pair k, owned by the device that holds them; among the (32) rows of one device, at most 2 name the same block. A pair may name one atom twice, and a pair may repeat; every entry counts.
All inputs are finite; a program needn't handle non-finite values.
Results may differ from the reference program's by a relative error of at most 0.0061.
Values may be sent and summed in bfloat16 or wider, within the bound.
No kernel may reach another device: no remote copies, remote signals or barrier semaphores. Data moves between devices by JAX's collectives and lax.ppermute only.
A program may use at most 128 MiB of HBM per device.

```python
import math
import jax
import jax.numpy as jnp
import numpy as np
from jax import lax

OCC = 384
MAXBF = 16
HALO = 128
ATOM_DEV = 32
AUX_DEV = 8
BAS_DEV = 256
PAIR_DEV = 16
CAP = 2
BLOCKS = 32
NBAS = 8192
NAUX = 64
REFS = 1024
WINDOW = 512
N_AUX = 8


def draw_metric(key, part):
    key = jax.random.fold_in(key, 11)
    diag_key, off_key = jax.random.split(key)
    diagonal = jax.random.uniform(diag_key, (NAUX, AUX_DEV), jnp.float32, 0.6, 1.4)
    spread = jnp.clip(jax.random.normal(off_key, (NAUX, AUX_DEV), jnp.float32), -4.0, 4.0) * (0.6 / math.sqrt(AUX_DEV))
    row_pos = jnp.arange(NAUX)[:, None] % AUX_DEV
    col_pos = jnp.arange(AUX_DEV)[None, :]
    filled = jnp.where(row_pos == col_pos, diagonal, jnp.where(row_pos < col_pos, spread, 0.0))
    return filled.astype(jnp.bfloat16)


def place_ends(values, own_key, smallest, largest):
    place = [jax.random.randint(jax.random.fold_in(own_key, axis), (), 0, length) for axis, length in enumerate(values.shape)]
    main_axis = values.shape.index(max(values.shape))
    next_to = place[:main_axis] + [(place[main_axis] + 1) % values.shape[main_axis]] + place[main_axis + 1:]
    return values.at[tuple(place)].set(smallest).at[tuple(next_to)].set(largest)


def levels(stream_key, dims, cuts, low, largest):
    def one(position, parts):
        draws = jax.random.uniform(jax.random.fold_in(jax.random.fold_in(stream_key, 6), position), (parts,), jnp.float32, low / len(cuts), largest / len(cuts))
        return jnp.repeat(jnp.exp(draws), dims[position] // parts).reshape((-1,) + (1,) * (len(dims) - position - 1))

    loudness = one(*cuts[0])
    for cut in cuts[1:]:
        loudness = loudness * one(*cut)
    return loudness


def length_profile(count, total, reach, skew):
    weights = [(1 << 20) // math.isqrt(grade ** skew) + 1 for grade in range(2, count + 1)]
    surplus, holding = total - reach - (count - 1), [1] * (count - 1)
    while surplus > 0:
        movable = [i for i in range(count - 1) if holding[i] < reach]
        whole, left = sum([weights[i] for i in movable]), surplus
        for i in movable:
            addition = min(reach - holding[i], max(1, left * weights[i] // whole), surplus)
            holding[i] = holding[i] + addition
            surplus = surplus - addition
    return np.array([reach] + holding)


def ragged(rng, count, total, bound, skew):
    if count == 2:
        one = jax.random.randint(rng, (), max(1, total - bound), min(bound, total - 1) + 1)
        return jnp.stack([one, total - one])
    sizes = jnp.asarray(length_profile(count, total, bound, skew), jnp.int32)
    couples = (count - 1) // 2
    source_of, sink = sizes[1:1 + 2 * couples:2], sizes[2:2 + 2 * couples:2]
    room = jnp.minimum(source_of - 1, bound - sink)
    shifted = jax.random.randint(jax.random.fold_in(rng, 1), (couples,), 0, 1 << 20) % (room + 1)
    sizes = sizes.at[1:1 + 2 * couples:2].set(source_of - shifted).at[2:2 + 2 * couples:2].set(sink + shifted)
    return sizes[jax.random.permutation(jax.random.fold_in(rng, 2), count)]


def routed_block(stream_key, own, number, rows, amount, top, limit, skew):
    order = jax.random.permutation(stream_key, amount)
    packed, ordinary = portions_of(amount, rows * top, limit, skew, True), portions_of(amount, rows * top, limit, skew, False)
    places = jnp.arange(amount)

    def named(sizes, offset_by):
        used = int((sizes > 0).sum())
        fixed = max(1, used // 4)
        shifted = fixed + (places - fixed + offset_by * (used - fixed)) % max(1, amount - fixed)
        return jnp.zeros((amount,), jnp.int32).at[order[jnp.where(places < fixed, places, shifted)]].set(jnp.asarray(sizes, jnp.int32))

    sizes = jnp.where(number % 4 == 0, named(packed, number // 4), named(ordinary, number - number // 4 - 1))
    mixed = jax.random.permutation(jax.random.fold_in(own, 3), amount)
    source_of, sink = mixed[0:amount // 2 * 2:2], mixed[1:amount // 2 * 2:2]
    margin = jnp.minimum(sizes[source_of] - 1, limit - sizes[sink]) // 2
    margin = jnp.where((source_of == order[0]) | (sink == order[0]) | (sizes[sink] == 0), 0, jnp.maximum(margin, 0))
    shifted = jax.random.randint(jax.random.fold_in(own, 4), (amount // 2,), 0, 1 << 20) % (margin + 1)
    sizes = sizes.at[source_of].add(-shifted).at[sink].add(shifted)
    members = jnp.searchsorted(jnp.cumsum(sizes), jnp.arange(rows * top), side="right").astype(jnp.int32)
    listing = members.reshape(top, rows).T
    listing = listing[jax.random.permutation(jax.random.fold_in(own, 1), rows)]
    offset_by = jax.random.randint(jax.random.fold_in(own, 2), (rows, 1), 0, top)
    return jnp.take_along_axis(listing, (jnp.arange(top)[None, :] + offset_by) % top, axis=1)


def portions_of(count, total, bound, lean, full):
    weights = [(1 << 20) // math.isqrt(rank ** lean) + 1 for rank in range(1, count + 1)]
    largest = bound if full else min(bound, max(-(-total // count), total * weights[0] // sum(weights)))
    least = 1 if total - largest >= count - 1 else 0
    given, rest = [largest] + [least] * (count - 1), total - largest - least * (count - 1)
    while rest > 0:
        movable = [i for i in range(1, count) if given[i] < largest] or [i for i in range(1, count) if given[i] < bound]
        mass, left = sum([weights[i] for i in movable]), rest
        for i in movable:
            extra = min(bound - given[i], max(1, left * weights[i] // mass), rest)
            given[i] = given[i] + extra
            rest = rest - extra
    return np.array(given)


def noise(stream_key, extent, scale, reach, cuts=(), kind=jnp.bfloat16):
    values = jax.random.normal(stream_key, extent, jnp.float32) * scale
    if len(cuts) > 0:
        values = levels(stream_key, extent, cuts, -0.22, 0.18) * values
    return jnp.clip(values, min=-reach, max=reach).astype(kind)


def setup_inputs(seed: int = 0) -> dict:
    key_of = jax.random.split(jax.random.key(seed), 7)
    integrals = noise(key_of[0], (NAUX, NBAS, WINDOW), WINDOW ** -0.5, 0.25, ((0, 8), (1, 32)))
    coeffs = noise(key_of[1], (NBAS, 2, OCC), 1.0, 6.0, ((0, 32),))
    metric = draw_metric(jax.random.fold_in(key_of[6], 71), 0)
    atom_sizes = jax.vmap(lambda own: ragged(own, ATOM_DEV, BAS_DEV, MAXBF, 1))(jax.random.split(key_of[3], BLOCKS)).reshape((BLOCKS, ATOM_DEV)).astype(jnp.int32)
    pair_device_keys = jax.random.split(jax.random.fold_in(key_of[4], 1), REFS // (2 * PAIR_DEV))
    pair_device_turns = jax.random.permutation(jax.random.fold_in(key_of[4], 3), REFS // (2 * PAIR_DEV))
    pair_device = jax.vmap(lambda own, number: routed_block(jax.random.fold_in(key_of[4], 2), own, number, 2 * PAIR_DEV, BLOCKS, 1, CAP, 2))(pair_device_keys, pair_device_turns).reshape((REFS, 1))
    pair_atom = place_ends(jax.random.randint(key_of[5], (REFS,), 0, ATOM_DEV), jax.random.fold_in(key_of[5], 1), 0, ATOM_DEV - 1).astype(jnp.int32)
    return dict(integrals=integrals, coeffs=coeffs, metric=metric, atom_sizes=atom_sizes, pair_device=pair_device, pair_atom=pair_atom)


def reference(integrals, coeffs, metric, atom_sizes, pair_device, pair_atom):
    window_len = BAS_DEV + 2 * HALO
    coef_rows = coeffs.reshape(NBAS, 2 * OCC)
    padded = jnp.pad(coef_rows, ((HALO, HALO), (0, 0)))
    factor = metric.reshape(N_AUX, AUX_DEV, AUX_DEV).astype(jnp.float32)

    def fit_block(block_index):
        row_start = (block_index * BAS_DEV).astype(jnp.int32)
        window_rows = lax.dynamic_slice_in_dim(padded, row_start, window_len, 0)
        local_ints = lax.dynamic_slice_in_dim(integrals, row_start, BAS_DEV, 1)
        half_block = jnp.dot(local_ints.reshape(NAUX * BAS_DEV, window_len), window_rows, preferred_element_type=jnp.float32).astype(jnp.bfloat16)
        grouped = half_block.reshape(N_AUX, AUX_DEV, BAS_DEV * 2 * OCC).astype(jnp.float32)
        fitted_block = jnp.einsum('kqp,kqr->kpr', factor, grouped)
        return fitted_block.astype(jnp.bfloat16).reshape(NAUX, BAS_DEV, 2 * OCC)
    fitted = lax.map(fit_block, jnp.arange(BLOCKS, dtype=jnp.int32))
    starts = jnp.cumsum(atom_sizes, axis=1) - atom_sizes
    offsets = jnp.arange(MAXBF, dtype=jnp.int32)
    devices = pair_device[:, 0].reshape(-1, 2)
    atom_index = pair_atom.reshape(-1, 2)
    pair_scale = 1.0 / math.sqrt(2 * OCC * NAUX * MAXBF)
    zero_half = jnp.zeros((), jnp.bfloat16)

    def atom_rows(device, atom_id):
        row_first = starts[device, atom_id]
        row_count = atom_sizes[device, atom_id]
        row_ids = jnp.minimum(row_first + offsets, BAS_DEV - 1).astype(jnp.int32)
        is_valid = offsets < row_count
        block_rows = jnp.take(fitted[device], row_ids, axis=1)
        block_rows = jnp.where(is_valid[None, :, None], block_rows, zero_half)
        global_rows = (device * BAS_DEV + row_ids).astype(jnp.int32)
        coef_block = jnp.where(is_valid[:, None], jnp.take(coef_rows, global_rows, axis=0), zero_half)
        return (block_rows, coef_block, global_rows)

    def add_pair(accumulated, pair_item):
        device, atom_id = pair_item
        first_rows, first_coef, first_index = atom_rows(device[0], atom_id[0])
        second_rows, second_coef, second_index = atom_rows(device[1], atom_id[1])
        turned = jnp.concatenate([-second_rows[..., OCC:], second_rows[..., :OCC]], axis=-1)
        left_rows = first_rows.astype(jnp.float32)
        real_k = jnp.einsum('qaj,qbj->ab', left_rows, second_rows.astype(jnp.float32))
        imag_k = jnp.einsum('qaj,qbj->ab', left_rows, turned.astype(jnp.float32))
        real_k = (real_k * pair_scale).astype(jnp.bfloat16)
        imag_k = (imag_k * pair_scale).astype(jnp.bfloat16)
        real_on_second = jnp.dot(real_k, second_coef, preferred_element_type=jnp.float32).reshape(MAXBF, 2, OCC)
        imag_on_second = jnp.dot(imag_k, second_coef, preferred_element_type=jnp.float32).reshape(MAXBF, 2, OCC)
        first_gain = jnp.stack([real_on_second[:, 0] - imag_on_second[:, 1], real_on_second[:, 1] + imag_on_second[:, 0]], axis=1)
        real_on_first = jnp.dot(real_k.T, first_coef, preferred_element_type=jnp.float32).reshape(MAXBF, 2, OCC)
        imag_on_first = jnp.dot(imag_k.T, first_coef, preferred_element_type=jnp.float32).reshape(MAXBF, 2, OCC)
        second_gain = jnp.stack([real_on_first[:, 0] + imag_on_first[:, 1], real_on_first[:, 1] - imag_on_first[:, 0]], axis=1)
        accumulated = accumulated.at[first_index].add(first_gain)
        accumulated = accumulated.at[second_index].add(second_gain)
        return (accumulated, None)
    result, _ = lax.scan(add_pair, jnp.zeros((NBAS, 2, OCC), jnp.float32), (devices, atom_index))
    return result
```

```python
import math

import jax
import jax.numpy as jnp
from jax import lax
from jax.experimental import pallas as pl
from jax.experimental.pallas import tpu as pltpu
from jax.sharding import PartitionSpec as P

MAXBF = 16
ROWBLK = 32
PACKED = ROWBLK + ROWBLK // 2
MIB = 1 << 20


def iota(shape, dim):
    return lax.broadcasted_iota(jnp.int32, shape, dim)


def dot(a, b):
    return jnp.dot(a, b, preferred_element_type=jnp.float32)


def dot_nt(a, b):
    return lax.dot_general(a, b, (((1,), (1,)), ((), ())), preferred_element_type=jnp.float32)


def dot_tn(a, b):
    return lax.dot_general(a, b, (((0,), (0,)), ((), ())), preferred_element_type=jnp.float32)


def fit_kernel(ints_ref, low_ref, own_ref, high_ref, mix_ref, out_ref, window_ref):
    @pl.when(pl.program_id(0) == 0)
    def _():
        window_ref[0:128] = low_ref[...]
        window_ref[128:384] = own_ref[...]
        window_ref[384:512] = high_ref[...]

    aux_dev = ints_ref.shape[0]
    half = dot(ints_ref[...].reshape(aux_dev * ROWBLK, ints_ref.shape[2]), window_ref[...])
    fitted = dot(mix_ref[...], half.astype(jnp.bfloat16))
    left = iota((ROWBLK // 2, 128), 1) < 64
    for p in range(aux_dev):
        rows = fitted[p * ROWBLK : (p + 1) * ROWBLK]
        for k in range(4):
            out_ref[p * 4 + k, 0, 0:ROWBLK] = rows[:, k * 128 : (k + 1) * 128].astype(jnp.bfloat16)
        for k in range(2):
            shared = rows[:, 512 + k * 128 : 640 + k * 128]
            top, bottom = shared[: ROWBLK // 2], shared[ROWBLK // 2 :]
            even = jnp.where(left, top, pltpu.roll(bottom, 64, 1))
            odd = jnp.where(left, pltpu.roll(top, 64, 1), bottom)
            out_ref[p * 4 + 2 * k, 0, ROWBLK:PACKED] = even.astype(jnp.bfloat16)
            out_ref[p * 4 + 2 * k + 1, 0, ROWBLK:PACKED] = odd.astype(jnp.bfloat16)


def pair_kernel(row_ref, got_ref, out_ref, main_ref, side_ref, first_ref, second_ref):
    groups, _, _, _ = got_ref.shape
    blocks = got_ref.shape[1]
    left = iota((ROWBLK // 2, 128), 1) < 64

    def unpack(b, carry):
        for i in range(blocks):
            base = pl.multiple_of(b * (blocks * ROWBLK) + i * ROWBLK, ROWBLK)
            main_ref[pl.ds(base, ROWBLK)] = got_ref[b, i, 0:ROWBLK].astype(jnp.float32)
            shared = got_ref[b, i, ROWBLK:PACKED].astype(jnp.float32)
            side_ref[pl.ds(base, ROWBLK // 2)] = jnp.where(left, shared, 0.0)
            side_ref[pl.ds(base + ROWBLK // 2, ROWBLK // 2)] = jnp.where(
                left, pltpu.roll(shared, 64, 1), 0.0
            )
        return carry

    lax.fori_loop(0, groups, unpack, 0)
    tail = groups * blocks * ROWBLK
    main_ref[tail : tail + MAXBF] = jnp.zeros((MAXBF, 128), jnp.float32)
    side_ref[tail : tail + MAXBF] = jnp.zeros((MAXBF, 128), jnp.float32)

    u, v = iota((256, 256), 0), iota((256, 256), 1)
    span = jnp.where(v < 128, 64, 32)
    is_real = (v < 64) | ((v >= 128) & (v < 160))
    source = jnp.where(is_real, v + span, v - span)
    turn = jnp.where((u == source) & (v < 192), jnp.where(is_real, -1.0, 1.0), 0.0)
    turn = turn.astype(jnp.bfloat16)
    same = iota((MAXBF, MAXBF, 256), 0) == iota((MAXBF, MAXBF, 256), 2) // MAXBF

    def group(g, carry):
        for j in range(2 * MAXBF):
            row = row_ref[g * (2 * MAXBF) + j]
            dest = first_ref if j % 2 == 0 else second_ref
            place = (j // 2) * MAXBF
            dest[place : place + MAXBF, 0:128] = main_ref[pl.ds(row, MAXBF)].astype(jnp.bfloat16)
            dest[place : place + MAXBF, 128:256] = side_ref[pl.ds(row, MAXBF)].astype(jnp.bfloat16)
        first = first_ref[...]
        second = second_ref[...]
        real = dot_nt(first, second)
        imag = dot_nt(first, dot(second, turn).astype(jnp.bfloat16))
        for c, value in ((0, real), (1, imag)):
            value = jnp.where(same, value.reshape(MAXBF, MAXBF, 256), 0.0)
            out_ref[g, c * MAXBF : (c + 1) * MAXBF] = jnp.sum(value, axis=0)
        return carry

    lax.fori_loop(0, groups, group, 0)


def slot_kernel(scale, place_ref, parts_ref, out_ref, tile_ref):
    total = parts_ref[0]
    for z in range(1, parts_ref.shape[0]):
        total = total + parts_ref[z]
    kernel = (total * scale).astype(jnp.bfloat16)
    same = iota((256, 256), 0) // MAXBF == iota((256, 256), 1) // MAXBF
    u, v = iota((256, 128), 0), iota((256, 128), 1)
    spot = v % 64 - (v // 64) * MAXBF
    first = jnp.zeros((256, 128), jnp.float32)
    for c in range(2):
        half = kernel[c * MAXBF : (c + 1) * MAXBF].astype(jnp.float32)
        wide = jnp.concatenate([half] * MAXBF, axis=0)
        wide = jnp.where(same, wide, 0.0).astype(jnp.bfloat16)
        fold = jnp.where(spot == c * 32 + u % MAXBF, 1.0, 0.0).astype(jnp.bfloat16)
        first = first + dot(wide, fold)
    u, v = iota((32, 128), 0), iota((32, 128), 1)
    spot = v % 64 - (v // 64) * MAXBF
    fold = jnp.where(spot == (u // MAXBF) * 32 + u % MAXBF, jnp.where(u < MAXBF, 1.0, -1.0), 0.0)
    tile_ref[0:256] = first
    tile_ref[256:512] = dot_tn(kernel, fold.astype(jnp.bfloat16))
    tile_ref[512:528] = jnp.zeros((MAXBF, 128), jnp.float32)
    for d in range(out_ref.shape[0]):
        one = tile_ref[pl.ds(pl.multiple_of(place_ref[2 * d], MAXBF), MAXBF)]
        two = tile_ref[pl.ds(pl.multiple_of(place_ref[2 * d + 1], MAXBF), MAXBF)]
        both = one + pltpu.roll(two, 64, 1)
        out_ref[d] = both[:, 0:64].astype(jnp.bfloat16)


def coef_kernel(row_ref, count_ref, coef_ref, out_ref):
    u, v = iota((96, 96), 0), iota((96, 96), 1)
    turn = jnp.where(u == (v + 48) % 96, jnp.where(v < 48, -1.0, 1.0), 0.0).astype(jnp.bfloat16)
    row_id = iota((MAXBF, 96), 0)

    def owner(g, carry):
        picked = []
        for r in range(2):
            row = row_ref[2 * g + r]
            base = pl.multiple_of((row // 16) * 16, 16)
            wide = coef_ref[pl.ds(base, 32)].astype(jnp.float32)
            rows = pltpu.roll(wide, 32 - (row - base), 0)[0:MAXBF]
            picked.append(jnp.where(row_id < count_ref[2 * g + r], rows, 0.0))
        rows = jnp.concatenate(picked, axis=0).astype(jnp.bfloat16)
        out_ref[g, 0:32] = rows
        out_ref[g, 32:64] = dot(rows, turn).astype(jnp.bfloat16)
        return carry

    lax.fori_loop(0, out_ref.shape[0], owner, 0)


def gain_kernel(row_ref, count_ref, slot_ref, coef_ref, out_ref, sum_ref):
    sum_ref[...] = jnp.zeros(sum_ref.shape, jnp.float32)
    lane = iota((MAXBF, 64), 1) % 32
    row_id = iota((MAXBF, 96), 0)
    for g in range(slot_ref.shape[0]):
        tile = slot_ref[g].astype(jnp.float32)
        upper = jnp.where(lane < MAXBF, tile, 0.0)
        lower = jnp.where(lane >= MAXBF, tile, 0.0)
        both = jnp.concatenate([upper, lower], axis=0).astype(jnp.bfloat16)
        gains = dot(both, coef_ref[g])
        for r in range(2):
            part = gains[r * MAXBF : (r + 1) * MAXBF]
            part = jnp.where(row_id < count_ref[2 * g + r], part, 0.0)
            where = pl.ds(row_ref[2 * g + r], MAXBF)
            sum_ref[where, 0:96] = sum_ref[where, 0:96] + part
    out_ref[...] = sum_ref[0:256].T[0:96]


def vmem_spec():
    return pl.BlockSpec(memory_space=pltpu.VMEM)


def smem_spec():
    return pl.BlockSpec(memory_space=pltpu.SMEM)


def limit(mib):
    return pltpu.CompilerParams(vmem_limit_bytes=mib * MIB)


def fit(integrals, low, own, high, mix):
    aux_dev, bas_dev, window = integrals.shape
    width = own.shape[1]
    steps = bas_dev // ROWBLK
    return pl.pallas_call(
        fit_kernel,
        grid=(steps,),
        in_specs=[
            pl.BlockSpec((aux_dev, ROWBLK, window), lambda i: (0, i, 0)),
            pl.BlockSpec(low.shape, lambda i: (0, 0)),
            pl.BlockSpec(own.shape, lambda i: (0, 0)),
            pl.BlockSpec(high.shape, lambda i: (0, 0)),
            pl.BlockSpec(mix.shape, lambda i: (0, 0)),
        ],
        out_specs=pl.BlockSpec((4 * aux_dev, 1, PACKED, 128), lambda i: (0, i, 0, 0)),
        out_shape=jax.ShapeDtypeStruct((4 * aux_dev, steps, PACKED, 128), jnp.bfloat16),
        scratch_shapes=[pltpu.VMEM((window, width), jnp.bfloat16)],
        compiler_params=limit(32),
        cost_estimate=pl.CostEstimate(
            flops=2 * aux_dev * bas_dev * width * (window + 256),
            bytes_accessed=6 * MIB,
            transcendentals=0,
        ),
        name="fit",
    )(integrals, low, own, high, mix)


def pair_sums(end_rows, got):
    groups, steps, _, _ = got.shape
    rows = groups * steps * ROWBLK + MAXBF
    return pl.pallas_call(
        pair_kernel,
        in_specs=[smem_spec(), vmem_spec()],
        out_specs=vmem_spec(),
        out_shape=jax.ShapeDtypeStruct((groups, 2 * MAXBF, 256), jnp.float32),
        scratch_shapes=[
            pltpu.VMEM((rows, 128), jnp.float32),
            pltpu.VMEM((rows, 128), jnp.float32),
            pltpu.VMEM((256, 256), jnp.bfloat16),
            pltpu.VMEM((256, 256), jnp.bfloat16),
        ],
        compiler_params=limit(40),
        name="pair_sums",
    )(end_rows, got)


def make_slots(scale, places, parts, groups):
    def body(*refs):
        slot_kernel(scale, *refs)

    return pl.pallas_call(
        body,
        in_specs=[smem_spec(), vmem_spec()],
        out_specs=vmem_spec(),
        out_shape=jax.ShapeDtypeStruct((groups, MAXBF, 64), jnp.bfloat16),
        scratch_shapes=[pltpu.VMEM((528, 128), jnp.float32)],
        compiler_params=limit(16),
        name="make_slots",
    )(places, parts)


def partner_coef(rows, counts, coef, groups):
    return pl.pallas_call(
        coef_kernel,
        in_specs=[smem_spec(), smem_spec(), vmem_spec()],
        out_specs=vmem_spec(),
        out_shape=jax.ShapeDtypeStruct((groups, 64, coef.shape[1]), jnp.bfloat16),
        compiler_params=limit(16),
        name="partner_coef",
    )(rows, counts, coef)


def add_gains(rows, counts, slots, partner, bas_dev):
    return pl.pallas_call(
        gain_kernel,
        in_specs=[smem_spec(), smem_spec(), vmem_spec(), vmem_spec()],
        out_specs=vmem_spec(),
        out_shape=jax.ShapeDtypeStruct((partner.shape[2], bas_dev), jnp.float32),
        scratch_shapes=[pltpu.VMEM((bas_dev + MAXBF, 128), jnp.float32)],
        compiler_params=limit(16),
        name="add_gains",
    )(rows, counts, slots, partner)


def pick(hit, values):
    return jnp.sum(jnp.where(hit, values, 0), axis=-1)


def per_device(integrals, coeffs, metric, atom_sizes, pair_device, pair_atom):
    aux_dev, bas_dev, window = integrals.shape
    occ = coeffs.shape[2]
    groups = lax.axis_size("atom")
    aux_count = lax.axis_size("aux")
    occ_part = occ // aux_count
    atom_count = atom_sizes.shape[1]
    ref_count = pair_atom.shape[0]
    halo = (window - bas_dev) // 2
    scale = 1.0 / math.sqrt(2 * occ * aux_dev * aux_count * MAXBF)
    me = lax.axis_index("atom")

    wide = coeffs[:, :, :256].reshape(bas_dev, 2, 4, 64).transpose(0, 2, 1, 3)
    narrow = coeffs[:, :, 256:].reshape(bas_dev, 2, 4, 32).transpose(0, 2, 1, 3)
    own = jnp.concatenate([wide.reshape(bas_dev, 512), narrow.reshape(bas_dev, 256)], axis=1)
    forward = [(i, i + 1) for i in range(groups - 1)]
    backward = [(i + 1, i) for i in range(groups - 1)]
    low = lax.ppermute(own[bas_dev - halo :], "atom", forward)
    high = lax.ppermute(own[:halo], "atom", backward)

    meta = jnp.concatenate([atom_sizes[0], pair_device[:, 0], pair_atom]).astype(jnp.bfloat16)
    coef_part = lax.dynamic_slice_in_dim(
        coeffs, lax.axis_index("aux") * occ_part, occ_part, 2
    ).reshape(bas_dev, 2 * occ_part)
    meta_rows = jnp.pad(meta[None], ((0, 15), (0, 0)))
    sent = jnp.concatenate([coef_part, meta_rows], axis=0)
    block_rows = bas_dev + 16
    all_coef = lax.all_gather(sent, "atom", axis=0, tiled=True)

    mix = metric.T[:, None, :, None] * jnp.eye(ROWBLK, dtype=jnp.bfloat16)[None, :, None, :]
    mix = mix.reshape(aux_dev * ROWBLK, aux_dev * ROWBLK)
    packed = fit(integrals, low, own, high, mix)
    got = lax.all_to_all(packed, "atom", split_axis=0, concat_axis=0, tiled=True)

    all_meta = all_coef.reshape(groups, block_rows, 2 * occ_part)[:, bas_dev].astype(jnp.int32)
    sizes = all_meta[:, :atom_count]
    devices = all_meta[:, atom_count : atom_count + ref_count]
    atoms = all_meta[:, atom_count + ref_count :]
    starts = jnp.cumsum(sizes, axis=1) - sizes
    atom_range = jnp.arange(atom_count, dtype=jnp.int32)
    block_range = jnp.arange(groups, dtype=jnp.int32)
    flat_dev, flat_atom = devices.reshape(-1), atoms.reshape(-1)
    both = (starts * 32 + sizes).astype(jnp.int32)
    hit = (flat_dev[:, None, None] == block_range[None, :, None]) & (
        flat_atom[:, None, None] == atom_range[None, None, :]
    )
    found = jnp.sum(jnp.where(hit, both[None], 0), axis=(1, 2))
    end_start = found // 32
    end_size = found % 32
    end_rows = flat_dev * bas_dev + end_start

    here = devices == me
    rank = jnp.cumsum(here.astype(jnp.int32), axis=1) - 1
    slot = here[:, None, :] & (rank[:, None, :] == jnp.arange(2, dtype=jnp.int32)[None, :, None])
    end_start, end_size = end_start.reshape(groups, ref_count), end_size.reshape(groups, ref_count)

    def partner(x):
        return x.reshape(groups, ref_count // 2, 2)[:, :, ::-1].reshape(groups, ref_count)

    gather_rows = devices * block_rows + end_start
    slot_start = pick(slot, end_start[:, None, :]).reshape(-1)
    slot_size = pick(slot, end_size[:, None, :]).reshape(-1)
    other_row = pick(slot, partner(gather_rows)[:, None, :]).reshape(-1)
    other_size = pick(slot, partner(end_size)[:, None, :]).reshape(-1)

    targets = pair_device[:, 0]
    order = jnp.arange(ref_count, dtype=jnp.int32)
    earlier = (targets[:, None] == targets[None, :]) & (order[None, :] < order[:, None])
    ranks = jnp.sum(earlier.astype(jnp.int32), axis=1)
    asked = targets * 2 + ranks
    place = (order % 2) * 256 + (order // 2) * MAXBF
    asked_hit = asked[None, :] == jnp.arange(2 * groups, dtype=jnp.int32)[:, None]
    places = 512 + pick(asked_hit, place[None, :] - 512)

    partial_sums = pair_sums(end_rows, got)
    owned = lax.all_to_all(partial_sums, "atom", split_axis=0, concat_axis=0, tiled=True)
    partner_rows = partner_coef(other_row, other_size, all_coef, groups)
    owned = jnp.sum(owned, axis=0)
    shared = jnp.broadcast_to(owned[None], (aux_count,) + owned.shape)
    parts = lax.all_to_all(shared, "aux", split_axis=0, concat_axis=0, tiled=True)
    slots = make_slots(scale, places, parts, groups)
    slots = lax.all_to_all(slots, "atom", split_axis=0, concat_axis=0, tiled=True)
    gains = add_gains(slot_start, slot_size, slots, partner_rows, bas_dev)
    return gains.reshape(2, occ_part, bas_dev).transpose(2, 0, 1)


def solution(mesh):
    placed = (
        P("aux", "atom", None),
        P("atom", None, None),
        P("aux", None),
        P("atom", None),
        P("atom", None),
        P("atom"),
    )
    return jax.shard_map(
        per_device, mesh=mesh, in_specs=placed, out_specs=P("atom", None, "aux"), check_vma=False
    )
```

```python
import math

import jax
import jax.numpy as jnp
import numpy as np
from jax import lax
from jax.experimental import pallas as pl
from jax.experimental.pallas import tpu as pltpu
from jax.sharding import PartitionSpec as P

MAXBF = 16
ROWBLK = 32
PACKED = ROWBLK + ROWBLK // 2
BATCH = 8
MIB = 1 << 20


def iota(shape, dim):
    return lax.broadcasted_iota(jnp.int32, shape, dim)


def dot(a, b):
    return jnp.dot(a, b, preferred_element_type=jnp.float32)


def dot_nt(a, b):
    return lax.dot_general(a, b, (((1,), (1,)), ((), ())), preferred_element_type=jnp.float32)


def dot_tn(a, b):
    return lax.dot_general(a, b, (((0,), (0,)), ((), ())), preferred_element_type=jnp.float32)


def fit_kernel(
    ints_ref, low_ref, own_ref, high_ref, order_ref, mix_ref, meta_ref, out_ref,
    window_ref, packed_ref, sem_ref,
):
    at = 0
    for part_ref in (low_ref, own_ref, high_ref):
        rows = part_ref.shape[0]
        window_ref[at : at + rows] = dot(part_ref[...], order_ref[...]).astype(jnp.bfloat16)
        at += rows
    aux_dev, bas_dev, span = ints_ref.shape
    blocks = bas_dev // ROWBLK
    left = iota((ROWBLK // 2, 128), 1) < 64
    copies = []
    for u in range(blocks):
        ints = ints_ref[:, u * ROWBLK : (u + 1) * ROWBLK].reshape(aux_dev * ROWBLK, span)
        half = dot(ints, window_ref[...]).astype(jnp.bfloat16)
        fitted = dot(mix_ref[...], half)
        main = slice(u * PACKED, u * PACKED + ROWBLK)
        side = slice(u * PACKED + ROWBLK, (u + 1) * PACKED)
        for p in range(aux_dev):
            rows = fitted[p * ROWBLK : (p + 1) * ROWBLK]
            for k in range(4):
                tile = rows[:, k * 128 : (k + 1) * 128]
                packed_ref[p * 4 + k, main] = tile.astype(jnp.bfloat16)
            for k in range(2):
                shared = rows[:, 512 + k * 128 : 640 + k * 128]
                top, bottom = shared[: ROWBLK // 2], shared[ROWBLK // 2 :]
                even = jnp.where(left, top, pltpu.roll(bottom, 64, 1))
                odd = jnp.where(left, pltpu.roll(top, 64, 1), bottom)
                packed_ref[p * 4 + 2 * k, side] = even.astype(jnp.bfloat16)
                packed_ref[p * 4 + 2 * k + 1, side] = odd.astype(jnp.bfloat16)
        if u == blocks - 1:
            for d in range(4 * aux_dev):
                packed_ref[d, blocks * PACKED : blocks * PACKED + 16] = meta_ref[...]
        if u % 2 == 1:
            first = (u - 1) * PACKED
            span_rows = pl.ds(first, 2 * PACKED + (16 if u == blocks - 1 else 0))
            copies.append(
                pltpu.make_async_copy(
                    packed_ref.at[:, span_rows], out_ref.at[:, span_rows], sem_ref.at[u // 2]
                )
            )
            copies[-1].start()
    for copy in copies:
        copy.wait()


def pair_kernel(row_ref, got_ref, out_ref, real_ref, imag_ref, sums_ref, sem_ref, *sides):
    groups, blocks = got_ref.shape[0], got_ref.shape[1] // PACKED
    lane = iota((ROWBLK // 2, 128), 1)
    left, valid = lane < 64, lane < 96

    def unpack(b, carry):
        for i in range(blocks):
            base = pl.multiple_of(b * (blocks * ROWBLK) + i * ROWBLK, ROWBLK)
            shared = got_ref[b, i * PACKED + ROWBLK : (i + 1) * PACKED].astype(jnp.float32)
            for h in range(2):
                at = i * PACKED + h * 16
                main = got_ref[b, at : at + 16].astype(jnp.float32)
                real = shared if h else pltpu.roll(shared, 64, 1)
                imag = pltpu.roll(shared, 96 if h else 32, 1)
                real = jnp.where(left, main, jnp.where(valid, real, 0.0))
                imag = jnp.where(left, pltpu.roll(main, 64, 1), jnp.where(valid, imag, 0.0))
                real_ref[pl.ds(base + h * 16, 16)] = real
                imag_ref[pl.ds(base + h * 16, 16)] = imag
        return carry

    lax.fori_loop(0, groups, unpack, 0, unroll=2)
    tail = groups * blocks * ROWBLK
    real_ref[tail : tail + MAXBF] = jnp.zeros((MAXBF, 128), jnp.float32)
    imag_ref[tail : tail + MAXBF] = jnp.zeros((MAXBF, 128), jnp.float32)
    lane_pair = lane // MAXBF
    batch = len(sides) // 4

    def group(step, carry):
        for u in range(batch):
            g = step * batch + u
            for h in range(2):
                first_ref, second_ref = sides[u * 4 + h * 2], sides[u * 4 + h * 2 + 1]
                for j in range(16):
                    row = row_ref[g * (2 * MAXBF) + h * 16 + j]
                    dest = second_ref if j % 2 else first_ref
                    place = (j // 2) * MAXBF
                    dest[place : place + 16] = real_ref[pl.ds(row, 16)].astype(jnp.bfloat16)
                    dest[128 + place : 144 + place] = imag_ref[pl.ds(row, 16)].astype(jnp.bfloat16)
                value = dot_nt(first_ref[...], second_ref[...])
                parts = []
                for top in (0, 128):
                    for at in (0, 128):
                        part = value[top : top + 16, at : at + 128]
                        for j in range(1, 8):
                            here = value[top + j * 16 : top + j * 16 + 16, at : at + 128]
                            part = jnp.where(lane_pair == j, here, part)
                        parts.append(part)
                sums_ref[g, 0:16, h * 128 : (h + 1) * 128] = parts[0] + parts[3]
                sums_ref[g, 16:32, h * 128 : (h + 1) * 128] = parts[2] - parts[1]
        send(step).start()
        return carry

    def send(step):
        done = pl.ds(step * batch, batch)
        return pltpu.make_async_copy(sums_ref.at[done], out_ref.at[done], sem_ref.at[step])

    lax.fori_loop(0, groups // batch, group, 0)
    for step in range(groups // batch):
        send(step).wait()


def slot_kernel(scale, place_ref, parts_ref, out_ref, tile_ref):
    total = parts_ref[0].astype(jnp.float32)
    for z in range(1, parts_ref.shape[0]):
        total = total + parts_ref[z].astype(jnp.float32)
    kernel = (total * scale).astype(jnp.bfloat16)
    same = iota((256, 256), 0) // MAXBF == iota((256, 256), 1) // MAXBF
    u, v = iota((256, 128), 0), iota((256, 128), 1)
    spot = v % 64 - (v // 64) * MAXBF
    first = jnp.zeros((256, 128), jnp.float32)
    for c in range(2):
        half = kernel[c * MAXBF : (c + 1) * MAXBF].astype(jnp.float32)
        wide = jnp.concatenate([half] * MAXBF, axis=0)
        wide = jnp.where(same, wide, 0.0).astype(jnp.bfloat16)
        fold = jnp.where(spot == c * 32 + u % MAXBF, 1.0, 0.0).astype(jnp.bfloat16)
        first = first + dot(wide, fold)
    u, v = iota((32, 128), 0), iota((32, 128), 1)
    spot = v % 64 - (v // 64) * MAXBF
    fold = jnp.where(spot == (u // MAXBF) * 32 + u % MAXBF, jnp.where(u < MAXBF, 1.0, -1.0), 0.0)
    tile_ref[0:256] = first
    tile_ref[256:512] = dot_tn(kernel, fold.astype(jnp.bfloat16))
    tile_ref[512:528] = jnp.zeros((MAXBF, 128), jnp.float32)
    left = iota((8, 128), 1) < 64
    for d in range(out_ref.shape[0]):
        one = tile_ref[pl.ds(pl.multiple_of(place_ref[2 * d], MAXBF), MAXBF)]
        two = tile_ref[pl.ds(pl.multiple_of(place_ref[2 * d + 1], MAXBF), MAXBF)]
        both = one + pltpu.roll(two, 64, 1)
        out_ref[d] = jnp.where(left, both[0:8], pltpu.roll(both[8:16], 64, 1))


def coef_kernel(row_ref, count_ref, coef_ref, out_ref):
    u, v = iota((96, 96), 0), iota((96, 96), 1)
    turn = jnp.where(u == (v + 48) % 96, jnp.where(v < 48, -1.0, 1.0), 0.0).astype(jnp.bfloat16)
    row_id = iota((MAXBF, 96), 0)

    def owner(g, carry):
        picked = []
        for r in range(2):
            row = row_ref[2 * g + r]
            base = jnp.minimum((row // 16) * 16, coef_ref.shape[0] - 32)
            base = pl.multiple_of(base, 16)
            wide = coef_ref[pl.ds(base, 32)].astype(jnp.float32)
            rows = pltpu.roll(wide, lax.rem(32 - (row - base), 32), 0)[0:MAXBF]
            picked.append(jnp.where(row_id < count_ref[2 * g + r], rows, 0.0))
        rows = jnp.concatenate(picked, axis=0).astype(jnp.bfloat16)
        out_ref[g, 0:32] = rows
        out_ref[g, 32:64] = dot(rows, turn).astype(jnp.bfloat16)
        return carry

    lax.fori_loop(0, out_ref.shape[0], owner, 0)


def gain_kernel(row_ref, count_ref, slot_ref, coef_ref, out_ref, sum_ref):
    sum_ref[...] = jnp.zeros(sum_ref.shape, jnp.float32)
    lane = iota((MAXBF, 64), 1) % 32
    row_id = iota((MAXBF, 96), 0)
    for g in range(slot_ref.shape[0]):
        pair = slot_ref[g]
        tile = jnp.concatenate([pair, pltpu.roll(pair, 64, 1)], axis=0)[:, 0:64]
        upper = jnp.where(lane < MAXBF, tile, 0.0)
        lower = jnp.where(lane >= MAXBF, tile, 0.0)
        both = jnp.concatenate([upper, lower], axis=0).astype(jnp.bfloat16)
        gains = dot(both, coef_ref[g])
        for r in range(2):
            part = gains[r * MAXBF : (r + 1) * MAXBF]
            part = jnp.where(row_id < count_ref[2 * g + r], part, 0.0)
            where = pl.ds(row_ref[2 * g + r], MAXBF)
            sum_ref[where, 0:96] = sum_ref[where, 0:96] + part
    out_ref[...] = sum_ref[0:256].T[0:96]


def vmem_spec():
    return pl.BlockSpec(memory_space=pltpu.VMEM)


def smem_spec():
    return pl.BlockSpec(memory_space=pltpu.SMEM)


def limit(mib):
    return pltpu.CompilerParams(vmem_limit_bytes=mib * MIB)


def fit(integrals, low, own, high, order, mix, meta):
    aux_dev, bas_dev, window = integrals.shape
    width = own.shape[1]
    blocks = bas_dev // ROWBLK
    shape = (4 * aux_dev, blocks * PACKED + 16, 128)
    return pl.pallas_call(
        fit_kernel,
        in_specs=[vmem_spec()] * 7,
        out_specs=pl.BlockSpec(memory_space=pltpu.HBM),
        out_shape=jax.ShapeDtypeStruct(shape, jnp.bfloat16),
        scratch_shapes=[
            pltpu.VMEM((window, width), jnp.bfloat16),
            pltpu.VMEM(shape, jnp.bfloat16),
            pltpu.SemaphoreType.DMA((blocks // 2,)),
        ],
        compiler_params=limit(32),
        cost_estimate=pl.CostEstimate(
            flops=2 * aux_dev * bas_dev * width * (window + 256),
            bytes_accessed=6 * MIB,
            transcendentals=0,
        ),
        name="fit",
    )(integrals, low, own, high, order, mix, meta)


def pair_sums(end_rows, got):
    groups = got.shape[0]
    rows = groups * (got.shape[1] // PACKED) * ROWBLK + MAXBF
    return pl.pallas_call(
        pair_kernel,
        in_specs=[smem_spec(), vmem_spec()],
        out_specs=pl.BlockSpec(memory_space=pltpu.HBM),
        out_shape=jax.ShapeDtypeStruct((groups, 2 * MAXBF, 256), jnp.float32),
        scratch_shapes=[
            pltpu.VMEM((rows, 128), jnp.float32),
            pltpu.VMEM((rows, 128), jnp.float32),
            pltpu.VMEM((groups, 2 * MAXBF, 256), jnp.float32),
            pltpu.SemaphoreType.DMA((groups // BATCH,)),
        ]
        + [pltpu.VMEM((256, 128), jnp.bfloat16)] * (4 * BATCH),
        compiler_params=limit(40),
        name="pair_sums",
    )(end_rows, got)


def make_slots(scale, places, parts, groups):
    def body(*refs):
        slot_kernel(scale, *refs)

    return pl.pallas_call(
        body,
        in_specs=[smem_spec(), vmem_spec()],
        out_specs=vmem_spec(),
        out_shape=jax.ShapeDtypeStruct((groups, 8, 128), jnp.float32),
        scratch_shapes=[pltpu.VMEM((528, 128), jnp.float32)],
        compiler_params=limit(16),
        name="make_slots",
    )(places, parts)


def partner_coef(rows, counts, coef, groups):
    return pl.pallas_call(
        coef_kernel,
        in_specs=[smem_spec(), smem_spec(), vmem_spec()],
        out_specs=vmem_spec(),
        out_shape=jax.ShapeDtypeStruct((groups, 64, coef.shape[1]), jnp.bfloat16),
        compiler_params=limit(16),
        name="partner_coef",
    )(rows, counts, coef)


def add_gains(rows, counts, slots, partner, bas_dev):
    return pl.pallas_call(
        gain_kernel,
        in_specs=[smem_spec(), smem_spec(), vmem_spec(), vmem_spec()],
        out_specs=vmem_spec(),
        out_shape=jax.ShapeDtypeStruct((partner.shape[2], bas_dev), jnp.float32),
        scratch_shapes=[pltpu.VMEM((bas_dev + MAXBF, 128), jnp.float32)],
        compiler_params=limit(16),
        name="add_gains",
    )(rows, counts, slots, partner)


def pick(hit, values):
    return jnp.sum(jnp.where(hit, values, 0), axis=-1)


def column_order(occ):
    order = np.zeros((2 * occ, 2 * occ), np.float32)
    spot = 0
    for first, count in ((0, 64), (4 * 64, 32)):
        for k in range(4):
            for c in range(2):
                for i in range(count):
                    order[c * occ + first + k * count + i, spot] = 1.0
                    spot += 1
    return order.astype(jnp.bfloat16)


def per_device(integrals, coeffs, metric, atom_sizes, pair_device, pair_atom):
    aux_dev, bas_dev, window = integrals.shape
    occ = coeffs.shape[2]
    groups = lax.axis_size("atom")
    aux_count = lax.axis_size("aux")
    occ_part = occ // aux_count
    atom_count = atom_sizes.shape[1]
    ref_count = pair_atom.shape[0]
    halo = (window - bas_dev) // 2
    scale = 1.0 / math.sqrt(2 * occ * aux_dev * aux_count * MAXBF)
    me = lax.axis_index("atom")

    own = coeffs.reshape(bas_dev, 2 * occ)
    forward = [(i, i + 1) for i in range(groups - 1)]
    backward = [(i + 1, i) for i in range(groups - 1)]
    low = lax.ppermute(own[bas_dev - halo :], "atom", forward)
    high = lax.ppermute(own[:halo], "atom", backward)

    meta = jnp.concatenate([atom_sizes[0], pair_device[:, 0], pair_atom]).astype(jnp.bfloat16)
    meta = jnp.pad(meta[None], ((0, 15), (0, 128 - meta.shape[0])))
    mix = metric.T[:, None, :, None] * jnp.eye(ROWBLK, dtype=jnp.bfloat16)[None, :, None, :]
    mix = mix.reshape(aux_dev * ROWBLK, aux_dev * ROWBLK)
    packed = fit(integrals, low, own, high, jnp.asarray(column_order(occ)), mix, meta)
    coef_part, packed = lax.optimization_barrier((coeffs, packed))
    got = lax.all_to_all(packed, "atom", split_axis=0, concat_axis=0, tiled=True)
    coef_part = lax.dynamic_slice_in_dim(
        coef_part, lax.axis_index("aux") * occ_part, occ_part, 2
    ).reshape(bas_dev, 2 * occ_part)
    all_coef = lax.all_gather(coef_part, "atom", axis=0, tiled=True)

    all_meta = got[:, got.shape[1] - 16, : 2 * occ_part].astype(jnp.int32)
    sizes = all_meta[:, :atom_count]
    devices = all_meta[:, atom_count : atom_count + ref_count]
    atoms = all_meta[:, atom_count + ref_count :]
    starts = jnp.cumsum(sizes, axis=1) - sizes
    atom_range = jnp.arange(atom_count, dtype=jnp.int32)
    block_range = jnp.arange(groups, dtype=jnp.int32)
    flat_dev, flat_atom = devices.reshape(-1), atoms.reshape(-1)
    both = (starts * 32 + sizes).astype(jnp.int32)
    hit = (flat_dev[:, None, None] == block_range[None, :, None]) & (
        flat_atom[:, None, None] == atom_range[None, None, :]
    )
    found = jnp.sum(jnp.where(hit, both[None], 0), axis=(1, 2))
    end_start = found // 32
    end_size = found % 32
    end_rows = flat_dev * bas_dev + end_start

    here = devices == me
    rank = jnp.cumsum(here.astype(jnp.int32), axis=1) - 1
    slot = here[:, None, :] & (rank[:, None, :] == jnp.arange(2, dtype=jnp.int32)[None, :, None])
    end_start, end_size = end_start.reshape(groups, ref_count), end_size.reshape(groups, ref_count)

    def partner(x):
        return x.reshape(groups, ref_count // 2, 2)[:, :, ::-1].reshape(groups, ref_count)

    gather_rows = devices * bas_dev + end_start
    slot_start = pick(slot, end_start[:, None, :]).reshape(-1)
    slot_size = pick(slot, end_size[:, None, :]).reshape(-1)
    other_row = pick(slot, partner(gather_rows)[:, None, :]).reshape(-1)
    other_size = pick(slot, partner(end_size)[:, None, :]).reshape(-1)

    targets = pair_device[:, 0]
    order = jnp.arange(ref_count, dtype=jnp.int32)
    earlier = (targets[:, None] == targets[None, :]) & (order[None, :] < order[:, None])
    ranks = jnp.sum(earlier.astype(jnp.int32), axis=1)
    asked = targets * 2 + ranks
    place = (order % 2) * 256 + (order // 2) * MAXBF
    asked_hit = asked[None, :] == jnp.arange(2 * groups, dtype=jnp.int32)[:, None]
    places = 512 + pick(asked_hit, place[None, :] - 512)

    partial_sums = pair_sums(end_rows, got)
    owned = lax.all_to_all(partial_sums, "atom", split_axis=0, concat_axis=0, tiled=True)
    partner_rows = partner_coef(other_row, other_size, all_coef, groups)
    owned = jnp.sum(owned, axis=0).astype(jnp.bfloat16)
    shared = jnp.broadcast_to(owned[None], (aux_count,) + owned.shape)
    parts = lax.all_to_all(shared, "aux", split_axis=0, concat_axis=0, tiled=True)
    slots = make_slots(scale, places, parts, groups)
    slots = lax.all_to_all(slots, "atom", split_axis=0, concat_axis=0, tiled=True)
    gains = add_gains(slot_start, slot_size, slots, partner_rows, bas_dev)
    return gains.reshape(2, occ_part, bas_dev).transpose(2, 0, 1)


def solution(mesh):
    placed = (
        P("aux", "atom", None),
        P("atom", None, None),
        P("aux", None),
        P("atom", None),
        P("atom", None),
        P("atom"),
    )
    return jax.shard_map(
        per_device, mesh=mesh, in_specs=placed, out_specs=P("atom", None, "aux"), check_vma=False
    )
```

```python
import math

import jax
import jax.numpy as jnp
import numpy as np
from jax import lax
from jax.experimental import pallas as pl
from jax.experimental.pallas import tpu as pltpu
from jax.sharding import PartitionSpec as P

MAXBF = 16
ROWBLK = 32
PACKED = ROWBLK + ROWBLK // 2
BATCH = 8
MIB = 1 << 20


def iota(shape, dim):
    return lax.broadcasted_iota(jnp.int32, shape, dim)


def dot(a, b):
    return jnp.dot(a, b, preferred_element_type=jnp.float32)


def dot_nt(a, b):
    return lax.dot_general(a, b, (((1,), (1,)), ((), ())), preferred_element_type=jnp.float32)


def dot_tn(a, b):
    return lax.dot_general(a, b, (((0,), (0,)), ((), ())), preferred_element_type=jnp.float32)


def fit_kernel(
    ints_ref, low_ref, own_ref, high_ref, order_ref, mix_ref, meta_ref, out_ref,
    window_ref, packed_ref, sem_ref,
):
    at = 0
    for part_ref in (low_ref, own_ref, high_ref):
        rows = part_ref.shape[0]
        window_ref[at : at + rows] = dot(part_ref[...], order_ref[...]).astype(jnp.bfloat16)
        at += rows
    aux_dev, bas_dev, span = ints_ref.shape
    blocks = bas_dev // ROWBLK
    left = iota((ROWBLK // 2, 128), 1) < 64
    copies = []
    for u in range(blocks):
        ints = ints_ref[:, u * ROWBLK : (u + 1) * ROWBLK].reshape(aux_dev * ROWBLK, span)
        half = dot(ints, window_ref[...]).astype(jnp.bfloat16)
        fitted = dot(mix_ref[...], half)
        main = slice(u * PACKED, u * PACKED + ROWBLK)
        side = slice(u * PACKED + ROWBLK, (u + 1) * PACKED)
        for p in range(aux_dev):
            rows = fitted[p * ROWBLK : (p + 1) * ROWBLK]
            for k in range(4):
                tile = rows[:, k * 128 : (k + 1) * 128]
                packed_ref[p * 4 + k, main] = tile.astype(jnp.bfloat16)
            for k in range(2):
                shared = rows[:, 512 + k * 128 : 640 + k * 128]
                top, bottom = shared[: ROWBLK // 2], shared[ROWBLK // 2 :]
                even = jnp.where(left, top, pltpu.roll(bottom, 64, 1))
                odd = jnp.where(left, pltpu.roll(top, 64, 1), bottom)
                packed_ref[p * 4 + 2 * k, side] = even.astype(jnp.bfloat16)
                packed_ref[p * 4 + 2 * k + 1, side] = odd.astype(jnp.bfloat16)
        if u == blocks - 1:
            for d in range(4 * aux_dev):
                packed_ref[d, blocks * PACKED : blocks * PACKED + 16] = meta_ref[...]
        if u % 2 == 1:
            first = (u - 1) * PACKED
            span_rows = pl.ds(first, 2 * PACKED + (16 if u == blocks - 1 else 0))
            copies.append(
                pltpu.make_async_copy(
                    packed_ref.at[:, span_rows], out_ref.at[:, span_rows], sem_ref.at[u // 2]
                )
            )
            copies[-1].start()
    for copy in copies:
        copy.wait()


def pair_kernel(
    row_ref, start_ref, count_ref, coef_ref, got_ref, out_ref,
    real_ref, imag_ref, rows_ref, sums_ref, sem_ref, *sides,
):
    groups, blocks = got_ref.shape[0], got_ref.shape[1] // PACKED
    lane = iota((ROWBLK // 2, 128), 1)
    left, valid = lane < 64, lane < 96

    def unpack(b, carry):
        for i in range(blocks):
            base = pl.multiple_of(b * (blocks * ROWBLK) + i * ROWBLK, ROWBLK)
            shared = got_ref[b, i * PACKED + ROWBLK : (i + 1) * PACKED].astype(jnp.float32)
            for h in range(2):
                at = i * PACKED + h * 16
                main = got_ref[b, at : at + 16].astype(jnp.float32)
                real = shared if h else pltpu.roll(shared, 64, 1)
                imag = pltpu.roll(shared, 96 if h else 32, 1)
                real = jnp.where(left, main, jnp.where(valid, real, 0.0))
                imag = jnp.where(left, pltpu.roll(main, 64, 1), jnp.where(valid, imag, 0.0))
                real_ref[pl.ds(base + h * 16, 16)] = real
                imag_ref[pl.ds(base + h * 16, 16)] = imag
        return carry

    lax.fori_loop(0, groups, unpack, 0, unroll=2)
    tail = groups * blocks * ROWBLK
    real_ref[tail : tail + MAXBF] = jnp.zeros((MAXBF, 128), jnp.float32)
    imag_ref[tail : tail + MAXBF] = jnp.zeros((MAXBF, 128), jnp.float32)
    bas_dev, width = coef_ref.shape
    rows_ref[...] = jnp.zeros(rows_ref.shape, jnp.float32)
    rows_ref[0:bas_dev, 0:width] = coef_ref[...].astype(jnp.float32)
    row_id = iota((MAXBF, 128), 0)
    lane_pair = lane // MAXBF
    batch = len(sides) // 4

    def group(step, carry):
        for u in range(batch):
            g = step * batch + u
            for h in range(2):
                first_ref, second_ref = sides[u * 4 + h * 2], sides[u * 4 + h * 2 + 1]
                for j in range(16):
                    row = row_ref[g * (2 * MAXBF) + h * 16 + j]
                    dest = second_ref if j % 2 else first_ref
                    place = (j // 2) * MAXBF
                    dest[place : place + 16] = real_ref[pl.ds(row, 16)].astype(jnp.bfloat16)
                    dest[128 + place : 144 + place] = imag_ref[pl.ds(row, 16)].astype(jnp.bfloat16)
                value = dot_nt(first_ref[...], second_ref[...])
                parts = []
                for top in (0, 128):
                    for at in (0, 128):
                        part = value[top : top + 16, at : at + 128]
                        for j in range(1, 8):
                            here = value[top + j * 16 : top + j * 16 + 16, at : at + 128]
                            part = jnp.where(lane_pair == j, here, part)
                        parts.append(part)
                real, imag = parts[0] + parts[3], parts[2] - parts[1]
                sums_ref[g, h * 32 : h * 32 + 16] = real.astype(jnp.bfloat16)
                sums_ref[g, h * 32 + 16 : h * 32 + 32] = imag.astype(jnp.bfloat16)
                rows = rows_ref[pl.ds(start_ref[2 * g + h], MAXBF)]
                rows = jnp.where(row_id < count_ref[2 * g + h], rows, 0.0)
                sums_ref[g, 64 + h * 16 : 80 + h * 16] = rows.astype(jnp.bfloat16)
        send(step).start()
        return carry

    def send(step):
        done = pl.ds(step * batch, batch)
        return pltpu.make_async_copy(sums_ref.at[done], out_ref.at[done], sem_ref.at[step])

    lax.fori_loop(0, groups // batch, group, 0)
    for step in range(groups // batch):
        send(step).wait()


def gain_kernel(
    scale, target_ref, rank_ref, place_ref, parts_ref, got_ref, out_ref,
    first_ref, second_ref, gain_ref,
):
    total = parts_ref[0]
    for z in range(1, parts_ref.shape[0]):
        total = total + parts_ref[z]
    kernel = (total * scale).astype(jnp.bfloat16).astype(jnp.float32)
    for e in range(2 * MAXBF):
        dest = second_ref if e % 2 else first_ref
        at = pl.multiple_of(64 + rank_ref[e] * MAXBF, MAXBF)
        place = (e // 2) * MAXBF
        dest[place : place + MAXBF] = got_ref[target_ref[e], pl.ds(at, MAXBF)]
    u, v = iota((128, 128), 0), iota((128, 128), 1)
    turn = jnp.where((v < 48) & (u == v + 48), -1.0, 0.0)
    turn = jnp.where((v >= 48) & (v < 96) & (u == v - 48), 1.0, turn).astype(jnp.bfloat16)
    same = u // MAXBF == v // MAXBF
    for h in range(2):
        rows = slice(h * 128, (h + 1) * 128)
        first, second = first_ref[rows], second_ref[rows]
        wide = []
        for c in range(2):
            tile = kernel[h * 32 + c * MAXBF : h * 32 + (c + 1) * MAXBF]
            tile = jnp.concatenate([tile] * 8, axis=0)
            wide.append(jnp.where(same, tile, 0.0).astype(jnp.bfloat16))
        turned = dot(second, turn).astype(jnp.bfloat16)
        gain_ref[rows] = dot(wide[0], second) + dot(wide[1], turned)
        turned = dot(first, turn).astype(jnp.bfloat16)
        gain_ref[256 + h * 128 : 384 + h * 128] = dot_tn(wide[0], first) - dot_tn(wide[1], turned)
    gain_ref[512:528] = jnp.zeros((MAXBF, 128), jnp.float32)
    for s in range(2 * out_ref.shape[0]):
        at = pl.ds(pl.multiple_of(place_ref[s], MAXBF), MAXBF)
        out_ref[s // 2, (s % 2) * MAXBF : (s % 2 + 1) * MAXBF] = gain_ref[at]


def add_kernel(start_ref, count_ref, gain_ref, out_ref, sum_ref):
    sum_ref[...] = jnp.zeros(sum_ref.shape, jnp.float32)
    row_id = iota((MAXBF, 128), 0)
    for s in range(2 * gain_ref.shape[0]):
        part = gain_ref[s // 2, (s % 2) * MAXBF : (s % 2 + 1) * MAXBF]
        where = pl.ds(start_ref[s], MAXBF)
        sum_ref[where] = sum_ref[where] + jnp.where(row_id < count_ref[s], part, 0.0)
    out_ref[...] = sum_ref[0 : out_ref.shape[1]].T[0 : out_ref.shape[0]]


def vmem_spec():
    return pl.BlockSpec(memory_space=pltpu.VMEM)


def smem_spec():
    return pl.BlockSpec(memory_space=pltpu.SMEM)


def limit(mib):
    return pltpu.CompilerParams(vmem_limit_bytes=mib * MIB)


def fit(integrals, low, own, high, order, mix, meta):
    aux_dev, bas_dev, window = integrals.shape
    width = own.shape[1]
    blocks = bas_dev // ROWBLK
    shape = (4 * aux_dev, blocks * PACKED + 16, 128)
    return pl.pallas_call(
        fit_kernel,
        in_specs=[vmem_spec()] * 7,
        out_specs=pl.BlockSpec(memory_space=pltpu.HBM),
        out_shape=pltpu.HBM(shape, jnp.bfloat16),
        scratch_shapes=[
            pltpu.VMEM((window, width), jnp.bfloat16),
            pltpu.VMEM(shape, jnp.bfloat16),
            pltpu.SemaphoreType.DMA((blocks // 2,)),
        ],
        compiler_params=limit(32),
        cost_estimate=pl.CostEstimate(
            flops=2 * aux_dev * bas_dev * width * (window + 256),
            bytes_accessed=6 * MIB,
            transcendentals=0,
        ),
        name="fit",
    )(integrals, low, own, high, order, mix, meta)


def pair_sums(end_rows, starts, counts, coef, got):
    groups = got.shape[0]
    rows = groups * (got.shape[1] // PACKED) * ROWBLK + MAXBF
    shape = (groups, 6 * MAXBF, 128)
    return pl.pallas_call(
        pair_kernel,
        in_specs=[smem_spec()] * 3 + [vmem_spec()] * 2,
        out_specs=pl.BlockSpec(memory_space=pltpu.HBM),
        out_shape=pltpu.HBM(shape, jnp.bfloat16),
        scratch_shapes=[
            pltpu.VMEM((rows, 128), jnp.float32),
            pltpu.VMEM((rows, 128), jnp.float32),
            pltpu.VMEM((coef.shape[0] + MAXBF, 128), jnp.float32),
            pltpu.VMEM(shape, jnp.bfloat16),
            pltpu.SemaphoreType.DMA((groups // BATCH,)),
        ]
        + [pltpu.VMEM((256, 128), jnp.bfloat16)] * (4 * BATCH),
        compiler_params=limit(40),
        name="pair_sums",
    )(end_rows, starts, counts, coef, got)


def make_gains(scale, targets, ranks, places, parts, got):
    def body(*refs):
        gain_kernel(scale, *refs)

    return pl.pallas_call(
        body,
        in_specs=[smem_spec()] * 3 + [vmem_spec()] * 2,
        out_specs=vmem_spec(),
        out_shape=jax.ShapeDtypeStruct((got.shape[0], 2 * MAXBF, 128), jnp.float32),
        scratch_shapes=[
            pltpu.VMEM((256, 128), jnp.bfloat16),
            pltpu.VMEM((256, 128), jnp.bfloat16),
            pltpu.VMEM((528, 128), jnp.float32),
        ],
        compiler_params=limit(16),
        name="make_gains",
    )(targets, ranks, places, parts, got)


def add_gains(starts, counts, gains, width, bas_dev):
    return pl.pallas_call(
        add_kernel,
        in_specs=[smem_spec()] * 2 + [vmem_spec()],
        out_specs=vmem_spec(),
        out_shape=jax.ShapeDtypeStruct((width, bas_dev), jnp.float32),
        scratch_shapes=[pltpu.VMEM((bas_dev + MAXBF, 128), jnp.float32)],
        compiler_params=limit(16),
        name="add_gains",
    )(starts, counts, gains)


def pick(hit, values):
    return jnp.sum(jnp.where(hit, values, 0), axis=-1)


def column_order(occ):
    order = np.zeros((2 * occ, 2 * occ), np.float32)
    spot = 0
    for first, count in ((0, 64), (4 * 64, 32)):
        for k in range(4):
            for c in range(2):
                for i in range(count):
                    order[c * occ + first + k * count + i, spot] = 1.0
                    spot += 1
    return order.astype(jnp.bfloat16)


def per_device(integrals, coeffs, metric, atom_sizes, pair_device, pair_atom):
    aux_dev, bas_dev, window = integrals.shape
    occ = coeffs.shape[2]
    groups = lax.axis_size("atom")
    aux_count = lax.axis_size("aux")
    occ_part = occ // aux_count
    atom_count = atom_sizes.shape[1]
    ref_count = pair_atom.shape[0]
    halo = (window - bas_dev) // 2
    scale = 1.0 / math.sqrt(2 * occ * aux_dev * aux_count * MAXBF)
    me = lax.axis_index("atom")

    own = coeffs.reshape(bas_dev, 2 * occ)
    forward = [(i, i + 1) for i in range(groups - 1)]
    backward = [(i + 1, i) for i in range(groups - 1)]
    low = lax.ppermute(own[bas_dev - halo :], "atom", forward)
    high = lax.ppermute(own[:halo], "atom", backward)

    meta = jnp.concatenate([atom_sizes[0], pair_device[:, 0], pair_atom]).astype(jnp.bfloat16)
    meta = jnp.pad(meta[None], ((0, 15), (0, 128 - meta.shape[0])))
    mix = metric.T[:, None, :, None] * jnp.eye(ROWBLK, dtype=jnp.bfloat16)[None, :, None, :]
    mix = mix.reshape(aux_dev * ROWBLK, aux_dev * ROWBLK)
    packed = fit(integrals, low, own, high, jnp.asarray(column_order(occ)), mix, meta)
    got = lax.all_to_all(packed, "atom", split_axis=0, concat_axis=0, tiled=True)
    coef_part = lax.dynamic_slice_in_dim(
        coeffs, lax.axis_index("aux") * occ_part, occ_part, 2
    ).reshape(bas_dev, 2 * occ_part)

    all_meta = got[:, got.shape[1] - 16, : 2 * occ_part].astype(jnp.int32)
    sizes = all_meta[:, :atom_count]
    devices = all_meta[:, atom_count : atom_count + ref_count]
    atoms = all_meta[:, atom_count + ref_count :]
    starts = jnp.cumsum(sizes, axis=1) - sizes
    atom_range = jnp.arange(atom_count, dtype=jnp.int32)
    block_range = jnp.arange(groups, dtype=jnp.int32)
    flat_dev, flat_atom = devices.reshape(-1), atoms.reshape(-1)
    both = (starts * 32 + sizes).astype(jnp.int32)
    hit = (flat_dev[:, None, None] == block_range[None, :, None]) & (
        flat_atom[:, None, None] == atom_range[None, None, :]
    )
    found = jnp.sum(jnp.where(hit, both[None], 0), axis=(1, 2))
    end_start = found // 32
    end_size = found % 32
    end_rows = flat_dev * bas_dev + end_start

    here = devices == me
    rank = jnp.cumsum(here.astype(jnp.int32), axis=1) - 1
    slot = here[:, None, :] & (rank[:, None, :] == jnp.arange(2, dtype=jnp.int32)[None, :, None])
    end_start, end_size = end_start.reshape(groups, ref_count), end_size.reshape(groups, ref_count)

    slot_start = pick(slot, end_start[:, None, :]).reshape(-1)
    slot_size = pick(slot, end_size[:, None, :]).reshape(-1)

    targets = pair_device[:, 0]
    order = jnp.arange(ref_count, dtype=jnp.int32)
    earlier = (targets[:, None] == targets[None, :]) & (order[None, :] < order[:, None])
    ranks = jnp.sum(earlier.astype(jnp.int32), axis=1)
    asked = targets * 2 + ranks
    place = (order % 2) * 256 + (order // 2) * MAXBF
    asked_hit = asked[None, :] == jnp.arange(2 * groups, dtype=jnp.int32)[:, None]
    places = 512 + pick(asked_hit, place[None, :] - 512)

    sent = pair_sums(end_rows, slot_start, slot_size, coef_part, got)
    owned = lax.all_to_all(sent, "atom", split_axis=0, concat_axis=0, tiled=True)
    own_sums = jnp.sum(owned[:, : 4 * MAXBF].astype(jnp.float32), axis=0)
    shared = jnp.broadcast_to(own_sums[None], (aux_count,) + own_sums.shape)
    parts = lax.all_to_all(shared, "aux", split_axis=0, concat_axis=0, tiled=True)
    gains = make_gains(scale, targets, ranks, places, parts, owned)
    gains = lax.all_to_all(gains, "atom", split_axis=0, concat_axis=0, tiled=True)
    result = add_gains(slot_start, slot_size, gains, 2 * occ_part, bas_dev)
    return result.reshape(2, occ_part, bas_dev).transpose(2, 0, 1)


def solution(mesh):
    placed = (
        P("aux", "atom", None),
        P("atom", None, None),
        P("aux", None),
        P("atom", None),
        P("atom", None),
        P("atom"),
    )
    return jax.shard_map(
        per_device, mesh=mesh, in_specs=placed, out_specs=P("atom", None, "aux"), check_vma=False
    )
```

```python
import math

import jax
import jax.numpy as jnp
from jax import lax
from jax.experimental import pallas as pl
from jax.experimental.pallas import tpu as pltpu
from jax.sharding import PartitionSpec as P

MAXBF = 16
ROWBLK = 32
PACKED = ROWBLK + ROWBLK // 2
BATCH = 8
MIB = 1 << 20


def iota(shape, dim):
    return lax.broadcasted_iota(jnp.int32, shape, dim)


def dot(a, b):
    return jnp.dot(a, b, preferred_element_type=jnp.float32)


def dot_nt(a, b):
    return lax.dot_general(a, b, (((1,), (1,)), ((), ())), preferred_element_type=jnp.float32)


def dot_tn(a, b):
    return lax.dot_general(a, b, (((0,), (0,)), ((), ())), preferred_element_type=jnp.float32)


def fit_kernel(
    ints_ref, low_ref, own_ref, high_ref, metric_ref, size_ref, dev_ref, atom_ref, out_ref,
    window_ref, packed_ref, meta_ref, sem_ref,
):
    u, v = iota((256, 256), 0), iota((256, 256), 1)
    main_order = u == ((v % 128) // 64) * 128 + (v // 128) * 64 + v % 64
    side_order = u == ((v % 64) // 32) * 128 + (v // 64) * 32 + v % 32
    main_order = jnp.where(main_order, 1.0, 0.0).astype(jnp.bfloat16)
    side_order = jnp.where(side_order, 1.0, 0.0).astype(jnp.bfloat16)
    at = 0
    for part_ref in (low_ref, own_ref, high_ref):
        rows = part_ref.shape[0]
        half = part_ref.shape[1] // 2
        for t in range(3):
            real = part_ref[:, t * 128 : (t + 1) * 128]
            imag = part_ref[:, half + t * 128 : half + (t + 1) * 128]
            order = side_order if t == 2 else main_order
            value = dot(jnp.concatenate([real, imag], axis=1), order)
            window_ref[at : at + rows, t * 256 : (t + 1) * 256] = value.astype(jnp.bfloat16)
        at += rows
    member = iota((256, 8), 0) // ROWBLK == iota((256, 8), 1)
    member = jnp.where(member, 1.0, 0.0).astype(jnp.bfloat16)
    mix = dot_nt(dot_nt(member, metric_ref[...]).astype(jnp.bfloat16), member)
    mix = jnp.where(u % ROWBLK == v % ROWBLK, mix, 0.0).astype(jnp.bfloat16)
    meta_ref[...] = jnp.zeros(meta_ref.shape, jnp.float32)
    for row, value_ref in enumerate((size_ref, dev_ref, atom_ref)):
        meta_ref[row : row + 1, 0 : value_ref.shape[1]] = value_ref[...].astype(jnp.float32)
    aux_dev, bas_dev, span = ints_ref.shape
    blocks = bas_dev // ROWBLK
    left = iota((ROWBLK // 2, 128), 1) < 64
    copies = []
    for u in range(blocks):
        ints = ints_ref[:, u * ROWBLK : (u + 1) * ROWBLK].reshape(aux_dev * ROWBLK, span)
        half = dot(ints, window_ref[...]).astype(jnp.bfloat16)
        fitted = dot(mix, half)
        main = slice(u * PACKED, u * PACKED + ROWBLK)
        side = slice(u * PACKED + ROWBLK, (u + 1) * PACKED)
        for p in range(aux_dev):
            rows = fitted[p * ROWBLK : (p + 1) * ROWBLK]
            for k in range(4):
                tile = rows[:, k * 128 : (k + 1) * 128]
                packed_ref[p * 4 + k, main] = tile.astype(jnp.bfloat16)
            for k in range(2):
                shared = rows[:, 512 + k * 128 : 640 + k * 128]
                top, bottom = shared[: ROWBLK // 2], shared[ROWBLK // 2 :]
                even = jnp.where(left, top, pltpu.roll(bottom, 64, 1))
                odd = jnp.where(left, pltpu.roll(top, 64, 1), bottom)
                packed_ref[p * 4 + 2 * k, side] = even.astype(jnp.bfloat16)
                packed_ref[p * 4 + 2 * k + 1, side] = odd.astype(jnp.bfloat16)
        if u == blocks - 1:
            for d in range(4 * aux_dev):
                packed_ref[d, blocks * PACKED : blocks * PACKED + 16] = meta_ref[...].astype(
                    jnp.bfloat16
                )
        if u % 2 == 1:
            first = (u - 1) * PACKED
            span_rows = pl.ds(first, 2 * PACKED + (16 if u == blocks - 1 else 0))
            copies.append(
                pltpu.make_async_copy(
                    packed_ref.at[:, span_rows], out_ref.at[:, span_rows], sem_ref.at[u // 2]
                )
            )
            copies[-1].start()
    for copy in copies:
        copy.wait()


def pair_kernel(row_ref, got_ref, out_ref, real_ref, imag_ref, sums_ref, sem_ref, *sides):
    groups, blocks = got_ref.shape[0], got_ref.shape[1] // PACKED
    lane = iota((ROWBLK // 2, 128), 1)
    left, valid = lane < 64, lane < 96

    def unpack(b, carry):
        for i in range(blocks):
            base = pl.multiple_of(b * (blocks * ROWBLK) + i * ROWBLK, ROWBLK)
            shared = got_ref[b, i * PACKED + ROWBLK : (i + 1) * PACKED].astype(jnp.float32)
            for h in range(2):
                at = i * PACKED + h * 16
                main = got_ref[b, at : at + 16].astype(jnp.float32)
                real = shared if h else pltpu.roll(shared, 64, 1)
                imag = pltpu.roll(shared, 96 if h else 32, 1)
                real = jnp.where(left, main, jnp.where(valid, real, 0.0))
                imag = jnp.where(left, pltpu.roll(main, 64, 1), jnp.where(valid, imag, 0.0))
                real_ref[pl.ds(base + h * 16, 16)] = real
                imag_ref[pl.ds(base + h * 16, 16)] = imag
        return carry

    lax.fori_loop(0, groups, unpack, 0, unroll=2)
    tail = groups * blocks * ROWBLK
    real_ref[tail : tail + MAXBF] = jnp.zeros((MAXBF, 128), jnp.float32)
    imag_ref[tail : tail + MAXBF] = jnp.zeros((MAXBF, 128), jnp.float32)
    lane_pair = lane // MAXBF
    batch = len(sides) // 4

    def group(step, carry):
        for u in range(batch):
            g = step * batch + u
            for h in range(2):
                first_ref, second_ref = sides[u * 4 + h * 2], sides[u * 4 + h * 2 + 1]
                for j in range(16):
                    row = row_ref[g * (2 * MAXBF) + h * 16 + j]
                    dest = second_ref if j % 2 else first_ref
                    place = (j // 2) * MAXBF
                    dest[place : place + 16] = real_ref[pl.ds(row, 16)].astype(jnp.bfloat16)
                    dest[128 + place : 144 + place] = imag_ref[pl.ds(row, 16)].astype(jnp.bfloat16)
                value = dot_nt(first_ref[...], second_ref[...])
                parts = []
                for top in (0, 128):
                    for at in (0, 128):
                        part = value[top : top + 16, at : at + 128]
                        for j in range(1, 8):
                            here = value[top + j * 16 : top + j * 16 + 16, at : at + 128]
                            part = jnp.where(lane_pair == j, here, part)
                        parts.append(part)
                real, imag = parts[0] + parts[3], parts[2] - parts[1]
                sums_ref[g, h * 32 : h * 32 + 16] = real.astype(jnp.bfloat16)
                sums_ref[g, h * 32 + 16 : h * 32 + 32] = imag.astype(jnp.bfloat16)
        send(step).start()
        return carry

    def send(step):
        done = pl.ds(step * batch, batch)
        return pltpu.make_async_copy(sums_ref.at[done], out_ref.at[done], sem_ref.at[step])

    lax.fori_loop(0, groups // batch, group, 0)
    for step in range(groups // batch):
        send(step).wait()


def slot_kernel(scale, place_ref, parts_ref, out_ref, tile_ref):
    total = parts_ref[0].astype(jnp.float32)
    for z in range(1, parts_ref.shape[0]):
        total = total + parts_ref[z].astype(jnp.float32)
    kernel = (total * scale).astype(jnp.bfloat16)
    u, v = iota((128, 128), 0), iota((128, 128), 1)
    same = u // MAXBF == v // MAXBF
    spot = v % 64 - (v // 64) * MAXBF
    folds = [jnp.where(spot == c * 32 + u % MAXBF, 1.0, 0.0).astype(jnp.bfloat16) for c in range(2)]
    u, v = iota((32, 128), 0), iota((32, 128), 1)
    spot = v % 64 - (v // 64) * MAXBF
    turned = jnp.where(spot == (u // MAXBF) * 32 + u % MAXBF, jnp.where(u < MAXBF, 1.0, -1.0), 0.0)
    turned = turned.astype(jnp.bfloat16)
    for h in range(2):
        block = kernel[h * 32 : (h + 1) * 32]
        first = jnp.zeros((128, 128), jnp.float32)
        for c in range(2):
            tile = block[c * MAXBF : (c + 1) * MAXBF].astype(jnp.float32)
            wide = jnp.where(same, jnp.concatenate([tile] * 8, axis=0), 0.0)
            first = first + dot(wide.astype(jnp.bfloat16), folds[c])
        tile_ref[h * 128 : (h + 1) * 128] = first
        tile_ref[256 + h * 128 : 384 + h * 128] = dot_tn(block, turned)
    tile_ref[512:528] = jnp.zeros((MAXBF, 128), jnp.float32)
    left = iota((8, 128), 1) < 64
    for d in range(out_ref.shape[0]):
        one = tile_ref[pl.ds(pl.multiple_of(place_ref[2 * d], MAXBF), MAXBF)]
        two = tile_ref[pl.ds(pl.multiple_of(place_ref[2 * d + 1], MAXBF), MAXBF)]
        both = one + pltpu.roll(two, 64, 1)
        out_ref[d] = jnp.where(left, both[0:8], pltpu.roll(both[8:16], 64, 1))


def coef_kernel(block_ref, start_ref, count_ref, coef_ref, out_ref):
    width, bas_dev = coef_ref.shape[1:]
    u, v = iota((width, width), 0), iota((width, width), 1)
    half = width // 2
    turn = jnp.where(u == (v + half) % width, jnp.where(v < half, -1.0, 1.0), 0.0)
    turn = turn.astype(jnp.bfloat16)
    row, spot = iota((MAXBF, bas_dev), 0), iota((MAXBF, bas_dev), 1)

    def owner(g, carry):
        picked = []
        for r in range(2):
            s = 2 * g + r
            hit = (spot == start_ref[s] + row) & (row < count_ref[s])
            hit = jnp.where(hit, 1.0, 0.0).astype(jnp.bfloat16)
            picked.append(dot_nt(hit, coef_ref[block_ref[s]]))
        rows = jnp.concatenate(picked, axis=0).astype(jnp.bfloat16)
        out_ref[g, 0:32] = rows
        out_ref[g, 32:64] = dot(rows, turn).astype(jnp.bfloat16)
        return carry

    lax.fori_loop(0, out_ref.shape[0], owner, 0, unroll=4)


def gain_kernel(row_ref, count_ref, slot_ref, coef_ref, out_ref, sum_ref):
    sum_ref[...] = jnp.zeros(sum_ref.shape, jnp.float32)
    lane = iota((MAXBF, 64), 1) % 32
    row_id = iota((MAXBF, 96), 0)
    for g in range(slot_ref.shape[0]):
        pair = slot_ref[g]
        tile = jnp.concatenate([pair, pltpu.roll(pair, 64, 1)], axis=0)[:, 0:64]
        upper = jnp.where(lane < MAXBF, tile, 0.0)
        lower = jnp.where(lane >= MAXBF, tile, 0.0)
        both = jnp.concatenate([upper, lower], axis=0).astype(jnp.bfloat16)
        gains = dot(both, coef_ref[g])
        for r in range(2):
            part = gains[r * MAXBF : (r + 1) * MAXBF]
            part = jnp.where(row_id < count_ref[2 * g + r], part, 0.0)
            where = pl.ds(row_ref[2 * g + r], MAXBF)
            sum_ref[where, 0:96] = sum_ref[where, 0:96] + part
    out_ref[...] = sum_ref[0 : out_ref.shape[1]].T[0 : out_ref.shape[0]]


def vmem_spec():
    return pl.BlockSpec(memory_space=pltpu.VMEM)


def smem_spec():
    return pl.BlockSpec(memory_space=pltpu.SMEM)


def limit(mib):
    return pltpu.CompilerParams(vmem_limit_bytes=mib * MIB)


def fit(integrals, low, own, high, metric, sizes, devices, atoms):
    aux_dev, bas_dev, window = integrals.shape
    width = own.shape[1]
    blocks = bas_dev // ROWBLK
    shape = (4 * aux_dev, blocks * PACKED + 16, 128)
    return pl.pallas_call(
        fit_kernel,
        in_specs=[vmem_spec()] * 8,
        out_specs=pl.BlockSpec(memory_space=pltpu.HBM),
        out_shape=pltpu.HBM(shape, jnp.bfloat16),
        scratch_shapes=[
            pltpu.VMEM((window, width), jnp.bfloat16),
            pltpu.VMEM(shape, jnp.bfloat16),
            pltpu.VMEM((16, 128), jnp.float32),
            pltpu.SemaphoreType.DMA((blocks // 2,)),
        ],
        compiler_params=limit(32),
        cost_estimate=pl.CostEstimate(
            flops=2 * aux_dev * bas_dev * width * (window + 256),
            bytes_accessed=6 * MIB,
            transcendentals=0,
        ),
        name="fit",
    )(integrals, low, own, high, metric, sizes, devices, atoms)


def pair_sums(end_rows, got):
    groups = got.shape[0]
    rows = groups * (got.shape[1] // PACKED) * ROWBLK + MAXBF
    shape = (groups, 4 * MAXBF, 128)
    return pl.pallas_call(
        pair_kernel,
        in_specs=[smem_spec(), vmem_spec()],
        out_specs=pl.BlockSpec(memory_space=pltpu.HBM),
        out_shape=pltpu.HBM(shape, jnp.bfloat16),
        scratch_shapes=[
            pltpu.VMEM((rows, 128), jnp.float32),
            pltpu.VMEM((rows, 128), jnp.float32),
            pltpu.VMEM(shape, jnp.bfloat16),
            pltpu.SemaphoreType.DMA((groups // BATCH,)),
        ]
        + [pltpu.VMEM((256, 128), jnp.bfloat16)] * (4 * BATCH),
        compiler_params=limit(40),
        name="pair_sums",
    )(end_rows, got)


def make_slots(scale, places, parts, groups):
    def body(*refs):
        slot_kernel(scale, *refs)

    return pl.pallas_call(
        body,
        in_specs=[smem_spec(), vmem_spec()],
        out_specs=vmem_spec(),
        out_shape=jax.ShapeDtypeStruct((groups, 8, 128), jnp.float32),
        scratch_shapes=[pltpu.VMEM((528, 128), jnp.float32)],
        compiler_params=limit(16),
        name="make_slots",
    )(places, parts)


def partner_coef(blocks, starts, counts, coef):
    groups, width, _ = coef.shape
    return pl.pallas_call(
        coef_kernel,
        in_specs=[smem_spec()] * 3 + [vmem_spec()],
        out_specs=vmem_spec(),
        out_shape=jax.ShapeDtypeStruct((groups, 64, width), jnp.bfloat16),
        compiler_params=limit(16),
        cost_estimate=pl.CostEstimate(flops=1 << 30, bytes_accessed=2 * MIB, transcendentals=0),
        name="partner_coef",
    )(blocks, starts, counts, coef)


def add_gains(rows, counts, slots, partner, bas_dev):
    return pl.pallas_call(
        gain_kernel,
        in_specs=[smem_spec()] * 2 + [vmem_spec()] * 2,
        out_specs=vmem_spec(),
        out_shape=jax.ShapeDtypeStruct((partner.shape[2], bas_dev), jnp.float32),
        scratch_shapes=[pltpu.VMEM((bas_dev + MAXBF, 128), jnp.float32)],
        compiler_params=limit(16),
        name="add_gains",
    )(rows, counts, slots, partner)


def pick(hit, values):
    return jnp.sum(jnp.where(hit, values, 0), axis=-1)


def per_device(integrals, coeffs, metric, atom_sizes, pair_device, pair_atom):
    aux_dev, bas_dev, window = integrals.shape
    occ = coeffs.shape[2]
    groups = lax.axis_size("atom")
    aux_count = lax.axis_size("aux")
    occ_part = occ // aux_count
    atom_count = atom_sizes.shape[1]
    ref_count = pair_atom.shape[0]
    halo = (window - bas_dev) // 2
    scale = 1.0 / math.sqrt(2 * occ * aux_dev * aux_count * MAXBF)
    me = lax.axis_index("atom")

    own = coeffs.reshape(bas_dev, 2 * occ)
    forward = [(i, i + 1) for i in range(groups - 1)]
    backward = [(i + 1, i) for i in range(groups - 1)]
    low = lax.ppermute(own[bas_dev - halo :], "atom", forward)
    high = lax.ppermute(own[:halo], "atom", backward)

    coef_part = lax.dynamic_slice_in_dim(
        coeffs, lax.axis_index("aux") * occ_part, occ_part, 2
    )
    coef_part = coef_part.transpose(1, 2, 0).reshape(1, 2 * occ_part, bas_dev)
    all_coef = lax.all_gather(coef_part, "atom", axis=0, tiled=True)

    packed = fit(
        integrals, low, own, high, metric, atom_sizes, pair_device.T, pair_atom[None]
    )
    got = lax.all_to_all(packed, "atom", split_axis=0, concat_axis=0, tiled=True)

    all_meta = got[:, got.shape[1] - 16 : got.shape[1] - 13, :32].astype(jnp.int32)
    sizes, devices, atoms = all_meta[:, 0, :atom_count], all_meta[:, 1], all_meta[:, 2]
    starts = jnp.cumsum(sizes, axis=1) - sizes
    atom_range = jnp.arange(atom_count, dtype=jnp.int32)
    block_range = jnp.arange(groups, dtype=jnp.int32)
    flat_dev, flat_atom = devices.reshape(-1), atoms.reshape(-1)
    both = (starts * 32 + sizes).astype(jnp.int32)
    hit = (flat_dev[:, None, None] == block_range[None, :, None]) & (
        flat_atom[:, None, None] == atom_range[None, None, :]
    )
    found = jnp.sum(jnp.where(hit, both[None], 0), axis=(1, 2))
    end_start = found // 32
    end_size = found % 32
    end_rows = flat_dev * bas_dev + end_start

    here = devices == me
    rank = jnp.cumsum(here.astype(jnp.int32), axis=1) - 1
    slot = here[:, None, :] & (rank[:, None, :] == jnp.arange(2, dtype=jnp.int32)[None, :, None])
    end_start, end_size = end_start.reshape(groups, ref_count), end_size.reshape(groups, ref_count)

    slot_start = pick(slot, end_start[:, None, :]).reshape(-1)
    slot_size = pick(slot, end_size[:, None, :]).reshape(-1)

    packed_end = (devices * 256 + end_start) * 32 + end_size
    other = packed_end.reshape(groups, ref_count // 2, 2)[:, :, ::-1].reshape(groups, ref_count)
    other = pick(slot, other[:, None, :]).reshape(-1)
    other_block, other_start, other_size = other // 8192, other // 32 % 256, other % 32

    targets = pair_device[:, 0]
    order = jnp.arange(ref_count, dtype=jnp.int32)
    earlier = (targets[:, None] == targets[None, :]) & (order[None, :] < order[:, None])
    ranks = jnp.sum(earlier.astype(jnp.int32), axis=1)
    asked = targets * 2 + ranks
    place = (order % 2) * 256 + (order // 2) * MAXBF
    asked_hit = asked[None, :] == jnp.arange(2 * groups, dtype=jnp.int32)[:, None]
    places = 512 + pick(asked_hit, place[None, :] - 512)

    sent = pair_sums(end_rows, got)
    owned = lax.all_to_all(sent, "atom", split_axis=0, concat_axis=0, tiled=True)
    own_sums = jnp.sum(owned.astype(jnp.float32), axis=0).astype(jnp.bfloat16)
    shared = jnp.broadcast_to(own_sums[None], (aux_count,) + own_sums.shape)
    parts = lax.all_to_all(shared, "aux", split_axis=0, concat_axis=0, tiled=True)
    partner = partner_coef(other_block, other_start, other_size, all_coef)
    slots = make_slots(scale, places, parts, groups)
    slots = lax.all_to_all(slots, "atom", split_axis=0, concat_axis=0, tiled=True)
    result = add_gains(slot_start, slot_size, slots, partner, bas_dev)
    return result.reshape(2, occ_part, bas_dev).transpose(2, 0, 1)


def solution(mesh):
    placed = (
        P("aux", "atom", None),
        P("atom", None, None),
        P("aux", None),
        P("atom", None),
        P("atom", None),
        P("atom"),
    )
    return jax.shard_map(
        per_device, mesh=mesh, in_specs=placed, out_specs=P("atom", None, "aux"), check_vma=False
    )
```

```python
import math

import jax
import jax.numpy as jnp
from jax import lax
from jax.experimental import pallas as pl
from jax.experimental.pallas import tpu as pltpu
from jax.sharding import PartitionSpec as P

MAXBF = 16
ROWBLK = 32
PACKED = ROWBLK + ROWBLK // 2
BATCH = 8
MIB = 1 << 20


def iota(shape, dim):
    return lax.broadcasted_iota(jnp.int32, shape, dim)


def dot(a, b):
    return jnp.dot(a, b, preferred_element_type=jnp.float32)


def dot_nt(a, b):
    return lax.dot_general(a, b, (((1,), (1,)), ((), ())), preferred_element_type=jnp.float32)


def dot_tn(a, b):
    return lax.dot_general(a, b, (((0,), (0,)), ((), ())), preferred_element_type=jnp.float32)


def fit_kernel(
    low_ref, own_ref, high_ref, ints_hbm, metric_hbm, size_hbm, dev_hbm, atom_hbm, out_ref,
    ints_ref, metric_ref, size_ref, dev_ref, atom_ref, window_ref, packed_ref, meta_ref,
    in_sem, out_sem,
):
    small = [(metric_hbm, metric_ref), (size_hbm, size_ref), (dev_hbm, dev_ref), (atom_hbm, atom_ref)]
    fetches = [pltpu.make_async_copy(a, b, in_sem.at[i]) for i, (a, b) in enumerate(small)]
    aux_dev, bas_dev, span = ints_ref.shape
    blocks = bas_dev // ROWBLK
    for u in range(blocks // 2):
        rows = pl.ds(2 * u * ROWBLK, 2 * ROWBLK)
        fetches.append(
            pltpu.make_async_copy(ints_hbm.at[:, rows], ints_ref.at[:, rows], in_sem.at[4 + u])
        )
    for fetch in fetches:
        fetch.start()
    u, v = iota((256, 256), 0), iota((256, 256), 1)
    main_order = u == ((v % 128) // 64) * 128 + (v // 128) * 64 + v % 64
    side_order = u == ((v % 64) // 32) * 128 + (v // 64) * 32 + v % 32
    main_order = jnp.where(main_order, 1.0, 0.0).astype(jnp.bfloat16)
    side_order = jnp.where(side_order, 1.0, 0.0).astype(jnp.bfloat16)
    at = 0
    for part_ref in (low_ref, own_ref, high_ref):
        rows = part_ref.shape[0]
        half = part_ref.shape[1] // 2
        for t in range(3):
            real = part_ref[:, t * 128 : (t + 1) * 128]
            imag = part_ref[:, half + t * 128 : half + (t + 1) * 128]
            order = side_order if t == 2 else main_order
            value = dot(jnp.concatenate([real, imag], axis=1), order)
            window_ref[at : at + rows, t * 256 : (t + 1) * 256] = value.astype(jnp.bfloat16)
        at += rows
    for fetch in fetches[:4]:
        fetch.wait()
    member = iota((256, 8), 0) // ROWBLK == iota((256, 8), 1)
    member = jnp.where(member, 1.0, 0.0).astype(jnp.bfloat16)
    mix = dot_nt(dot_nt(member, metric_ref[...]).astype(jnp.bfloat16), member)
    mix = jnp.where(u % ROWBLK == v % ROWBLK, mix, 0.0).astype(jnp.bfloat16)
    meta_ref[...] = jnp.zeros(meta_ref.shape, jnp.float32)
    for row, value_ref in enumerate((size_ref, dev_ref, atom_ref)):
        meta_ref[row : row + 1, 0 : value_ref.shape[1]] = value_ref[...].astype(jnp.float32)
    left = iota((ROWBLK // 2, 128), 1) < 64
    copies = []
    for u in range(blocks):
        if u % 2 == 0:
            fetches[4 + u // 2].wait()
        ints = ints_ref[:, u * ROWBLK : (u + 1) * ROWBLK].reshape(aux_dev * ROWBLK, span)
        half = dot(ints, window_ref[...]).astype(jnp.bfloat16)
        fitted = dot(mix, half)
        main = slice(u * PACKED, u * PACKED + ROWBLK)
        side = slice(u * PACKED + ROWBLK, (u + 1) * PACKED)
        for p in range(aux_dev):
            rows = fitted[p * ROWBLK : (p + 1) * ROWBLK]
            for k in range(4):
                tile = rows[:, k * 128 : (k + 1) * 128]
                packed_ref[p * 4 + k, main] = tile.astype(jnp.bfloat16)
            for k in range(2):
                shared = rows[:, 512 + k * 128 : 640 + k * 128]
                top, bottom = shared[: ROWBLK // 2], shared[ROWBLK // 2 :]
                even = jnp.where(left, top, pltpu.roll(bottom, 64, 1))
                odd = jnp.where(left, pltpu.roll(top, 64, 1), bottom)
                packed_ref[p * 4 + 2 * k, side] = even.astype(jnp.bfloat16)
                packed_ref[p * 4 + 2 * k + 1, side] = odd.astype(jnp.bfloat16)
        if u == blocks - 1:
            for d in range(4 * aux_dev):
                packed_ref[d, blocks * PACKED : blocks * PACKED + 16] = meta_ref[...].astype(
                    jnp.bfloat16
                )
        if u % 2 == 1:
            first = (u - 1) * PACKED
            span_rows = pl.ds(first, 2 * PACKED + (16 if u == blocks - 1 else 0))
            copies.append(
                pltpu.make_async_copy(
                    packed_ref.at[:, span_rows], out_ref.at[:, span_rows], out_sem.at[u // 2]
                )
            )
            copies[-1].start()
    for copy in copies:
        copy.wait()


def end_table(me, got_ref, size_ref, dev_ref, atom_ref):
    groups, at = got_ref.shape[0], got_ref.shape[1] - 16
    for d in range(groups):
        rows = got_ref[d, at : at + 16].astype(jnp.float32)
        for i, dest in enumerate((size_ref, dev_ref, atom_ref)):
            dest[d : d + 1] = rows[i : i + 1]
    before = jnp.where(iota((128, 128), 0) < iota((128, 128), 1), 1.0, 0.0).astype(jnp.bfloat16)
    sizes = size_ref[...]
    packed = dot(sizes.astype(jnp.bfloat16), before) * 32.0 + sizes
    devices = dev_ref[...].astype(jnp.int32)
    atoms = atom_ref[...].astype(jnp.int32)
    found = jnp.zeros(packed.shape, jnp.float32)
    for d in range(groups):
        row = jnp.broadcast_to(packed[d : d + 1], packed.shape)
        found = jnp.where(devices == d, jnp.take_along_axis(row, atoms, axis=1), found)
    found = found.astype(jnp.int32)
    starts, counts = found // 32, found % 32
    lane = iota(found.shape, 1)
    here = (devices == me) & (lane < 32)
    rank = dot(jnp.where(here, 1.0, 0.0).astype(jnp.bfloat16), before)
    table = jnp.where(lane < 32, devices * 256 + starts, 0)
    for i, value in enumerate((starts, counts)):
        value = value.astype(jnp.float32)
        for r in range(2):
            one = jnp.sum(jnp.where(here & (rank == r), value, 0.0), axis=1, keepdims=True)
            table = jnp.where(lane == 32 + 2 * i + r, one.astype(jnp.int32), table)
    return table


def pair_kernel(
    me_ref, coef_ref, got_ref, table_ref, out_ref, real_ref, imag_ref, rows_ref, sums_ref,
    size_ref, dev_ref, atom_ref, row_ref, table_sem, sem_ref, *sides,
):
    table_ref[...] = end_table(me_ref[0], got_ref, size_ref, dev_ref, atom_ref)
    fetch = pltpu.make_async_copy(table_ref, row_ref, table_sem)
    fetch.start()
    groups, blocks = got_ref.shape[0], got_ref.shape[1] // PACKED
    lane = iota((ROWBLK // 2, 128), 1)
    left, valid = lane < 64, lane < 96

    def unpack(b, carry):
        for i in range(blocks):
            base = pl.multiple_of(b * (blocks * ROWBLK) + i * ROWBLK, ROWBLK)
            shared = got_ref[b, i * PACKED + ROWBLK : (i + 1) * PACKED].astype(jnp.float32)
            for h in range(2):
                at = i * PACKED + h * 16
                main = got_ref[b, at : at + 16].astype(jnp.float32)
                real = shared if h else pltpu.roll(shared, 64, 1)
                imag = pltpu.roll(shared, 96 if h else 32, 1)
                real = jnp.where(left, main, jnp.where(valid, real, 0.0))
                imag = jnp.where(left, pltpu.roll(main, 64, 1), jnp.where(valid, imag, 0.0))
                real_ref[pl.ds(base + h * 16, 16)] = real
                imag_ref[pl.ds(base + h * 16, 16)] = imag
        return carry

    lax.fori_loop(0, groups, unpack, 0, unroll=2)
    tail = groups * blocks * ROWBLK
    real_ref[tail : tail + MAXBF] = jnp.zeros((MAXBF, 128), jnp.float32)
    imag_ref[tail : tail + MAXBF] = jnp.zeros((MAXBF, 128), jnp.float32)
    bas_dev, width = coef_ref.shape
    rows_ref[...] = jnp.zeros(rows_ref.shape, jnp.float32)
    rows_ref[0:bas_dev, 0:width] = coef_ref[...].astype(jnp.float32)
    row_id = iota((MAXBF, 128), 0)
    lane_pair = lane // MAXBF
    batch = len(sides) // 4
    fetch.wait()

    def group(step, carry):
        for u in range(batch):
            g = step * batch + u
            for h in range(2):
                first_ref, second_ref = sides[u * 4 + h * 2], sides[u * 4 + h * 2 + 1]
                for j in range(16):
                    row = row_ref[g, h * 16 + j]
                    dest = second_ref if j % 2 else first_ref
                    place = (j // 2) * MAXBF
                    dest[place : place + 16] = real_ref[pl.ds(row, 16)].astype(jnp.bfloat16)
                    dest[128 + place : 144 + place] = imag_ref[pl.ds(row, 16)].astype(jnp.bfloat16)
                value = dot_nt(first_ref[...], second_ref[...])
                parts = []
                for top in (0, 128):
                    for at in (0, 128):
                        part = value[top : top + 16, at : at + 128]
                        for j in range(1, 8):
                            here = value[top + j * 16 : top + j * 16 + 16, at : at + 128]
                            part = jnp.where(lane_pair == j, here, part)
                        parts.append(part)
                real, imag = parts[0] + parts[3], parts[2] - parts[1]
                sums_ref[g, h * 32 : h * 32 + 16] = real.astype(jnp.bfloat16)
                sums_ref[g, h * 32 + 16 : h * 32 + 32] = imag.astype(jnp.bfloat16)
                rows = rows_ref[pl.ds(row_ref[g, 32 + h], MAXBF)]
                rows = jnp.where(row_id < row_ref[g, 34 + h], rows, 0.0)
                sums_ref[g, 64 + h * 16 : 80 + h * 16] = rows.astype(jnp.bfloat16)
        send(step).start()
        return carry

    def send(step):
        done = pl.ds(step * batch, batch)
        return pltpu.make_async_copy(sums_ref.at[done], out_ref.at[done], sem_ref.at[step])

    lax.fori_loop(0, groups // batch, group, 0)
    for step in range(groups // batch):
        send(step).wait()


def slot_kernel(scale, target_ref, rank_ref, place_ref, parts_ref, got_ref, out_ref, tile_ref):
    total = parts_ref[0].astype(jnp.float32)
    for z in range(1, parts_ref.shape[0]):
        total = total + parts_ref[z].astype(jnp.float32)
    kernel = (total * scale).astype(jnp.bfloat16)
    u, v = iota((128, 128), 0), iota((128, 128), 1)
    same = u // MAXBF == v // MAXBF
    folds = [jnp.where(v == 96 + c * 16 + u % 16, 1.0, 0.0).astype(jnp.bfloat16) for c in range(2)]
    u, v = iota((32, 128), 0), iota((32, 128), 1)
    turned = jnp.where(v == 96 + u, jnp.where(u < MAXBF, 1.0, -1.0), 0.0).astype(jnp.bfloat16)

    def coef(e):
        at = pl.multiple_of(64 + rank_ref[e] * MAXBF, MAXBF)
        return got_ref[target_ref[e], pl.ds(at, MAXBF)].astype(jnp.float32)

    for h in range(2):
        block = kernel[h * 32 : (h + 1) * 32]
        first = jnp.zeros((128, 128), jnp.float32)
        for c in range(2):
            tile = block[c * MAXBF : (c + 1) * MAXBF].astype(jnp.float32)
            wide = jnp.where(same, jnp.concatenate([tile] * 8, axis=0), 0.0)
            first = first + dot(wide.astype(jnp.bfloat16), folds[c])
        second = dot_tn(block, turned)
        for j in range(8):
            pair, rows = h * 8 + j, slice(j * MAXBF, (j + 1) * MAXBF)
            at = pair * MAXBF
            tile_ref[at : at + MAXBF] = first[rows] + coef(2 * pair + 1)
            tile_ref[256 + at : 256 + at + MAXBF] = second[rows] + coef(2 * pair)
    tile_ref[512:528] = jnp.zeros((MAXBF, 128), jnp.float32)
    for s in range(2 * out_ref.shape[0]):
        rows = tile_ref[pl.ds(pl.multiple_of(place_ref[s], MAXBF), MAXBF)]
        out_ref[s // 2, (s % 2) * MAXBF : (s % 2 + 1) * MAXBF] = rows.astype(jnp.bfloat16)


def gain_kernel(row_ref, count_ref, slot_ref, out_ref, plain_ref, turned_ref):
    plain_ref[...] = jnp.zeros(plain_ref.shape, jnp.float32)
    turned_ref[...] = jnp.zeros(turned_ref.shape, jnp.float32)
    lane, row_id = iota((MAXBF, 128), 1), iota((MAXBF, 128), 0)
    masks = [lane < MAXBF, (lane >= MAXBF) & (lane < 2 * MAXBF)]
    for g in range(slot_ref.shape[0]):
        slots = slot_ref[g]
        wide = slots.astype(jnp.float32)
        tiles = []
        for c in range(2):
            for r in range(2):
                tile = wide[r * MAXBF : (r + 1) * MAXBF]
                tile = pltpu.roll(tile, 32 + 16 * (r - c), 1)
                tiles.append(jnp.where(masks[r], tile, 0.0))
        tiles = jnp.concatenate(tiles, axis=0)[:, 0:32].astype(jnp.bfloat16)
        gains = dot(tiles, slots)
        for c, sum_ref in enumerate((plain_ref, turned_ref)):
            for r in range(2):
                at = (2 * c + r) * MAXBF
                part = jnp.where(row_id < count_ref[2 * g + r], gains[at : at + MAXBF], 0.0)
                where = pl.ds(row_ref[2 * g + r], MAXBF)
                sum_ref[where] = sum_ref[where] + part
    width, bas_dev = out_ref.shape
    half = width // 2
    plain = plain_ref[0:bas_dev].T
    turned = turned_ref[0:bas_dev].T
    out_ref[0:half] = plain[0:half] - turned[half:width]
    out_ref[half:width] = plain[half:width] + turned[0:half]


def vmem_spec():
    return pl.BlockSpec(memory_space=pltpu.VMEM)


def smem_spec():
    return pl.BlockSpec(memory_space=pltpu.SMEM)


def limit(mib):
    return pltpu.CompilerParams(vmem_limit_bytes=mib * MIB)


def in_hbm(array):
    return pltpu.with_memory_space_constraint(array, pltpu.HBM)


def fit(low, own, high, *fetched):
    aux_dev, bas_dev, window = fetched[0].shape
    width = own.shape[1]
    blocks = bas_dev // ROWBLK
    shape = (4 * aux_dev, blocks * PACKED + 16, 128)
    return pl.pallas_call(
        fit_kernel,
        in_specs=[vmem_spec()] * 3 + [pl.BlockSpec(memory_space=pltpu.HBM)] * len(fetched),
        out_specs=pl.BlockSpec(memory_space=pltpu.HBM),
        out_shape=pltpu.HBM(shape, jnp.bfloat16),
        scratch_shapes=[pltpu.VMEM(x.shape, x.dtype) for x in fetched]
        + [
            pltpu.VMEM((window, width), jnp.bfloat16),
            pltpu.VMEM(shape, jnp.bfloat16),
            pltpu.VMEM((16, 128), jnp.float32),
            pltpu.SemaphoreType.DMA((4 + blocks // 2,)),
            pltpu.SemaphoreType.DMA((blocks // 2,)),
        ],
        compiler_params=limit(32),
        cost_estimate=pl.CostEstimate(
            flops=2 * aux_dev * bas_dev * width * (window + 256),
            bytes_accessed=6 * MIB,
            transcendentals=0,
        ),
        name="fit",
    )(low, own, high, *[in_hbm(x) for x in fetched])


def pair_sums(me, coef, got):
    groups = got.shape[0]
    rows = groups * (got.shape[1] // PACKED) * ROWBLK + MAXBF
    shape = (groups, 6 * MAXBF, 128)
    return pl.pallas_call(
        pair_kernel,
        in_specs=[smem_spec(), vmem_spec(), vmem_spec()],
        out_specs=[vmem_spec(), pl.BlockSpec(memory_space=pltpu.HBM)],
        out_shape=[
            jax.ShapeDtypeStruct((groups, 128), jnp.int32),
            pltpu.HBM(shape, jnp.bfloat16),
        ],
        scratch_shapes=[
            pltpu.VMEM((rows, 128), jnp.float32),
            pltpu.VMEM((rows, 128), jnp.float32),
            pltpu.VMEM((coef.shape[0] + MAXBF, 128), jnp.float32),
            pltpu.VMEM(shape, jnp.bfloat16),
            pltpu.VMEM((groups, 128), jnp.float32),
            pltpu.VMEM((groups, 128), jnp.float32),
            pltpu.VMEM((groups, 128), jnp.float32),
            pltpu.SMEM((groups, 128), jnp.int32),
            pltpu.SemaphoreType.DMA,
            pltpu.SemaphoreType.DMA((groups // BATCH,)),
        ]
        + [pltpu.VMEM((256, 128), jnp.bfloat16)] * (4 * BATCH),
        compiler_params=limit(40),
        name="pair_sums",
    )(me, coef, got)


def make_slots(scale, targets, ranks, places, parts, got):
    def body(*refs):
        slot_kernel(scale, *refs)

    return pl.pallas_call(
        body,
        in_specs=[smem_spec()] * 3 + [vmem_spec()] * 2,
        out_specs=vmem_spec(),
        out_shape=jax.ShapeDtypeStruct((got.shape[0], 2 * MAXBF, 128), jnp.bfloat16),
        scratch_shapes=[pltpu.VMEM((528, 128), jnp.float32)],
        compiler_params=limit(16),
        name="make_slots",
    )(targets, ranks, places, parts, got)


def add_gains(rows, counts, slots, width, bas_dev):
    return pl.pallas_call(
        gain_kernel,
        in_specs=[smem_spec()] * 2 + [vmem_spec()],
        out_specs=vmem_spec(),
        out_shape=jax.ShapeDtypeStruct((width, bas_dev), jnp.float32),
        scratch_shapes=[pltpu.VMEM((bas_dev + MAXBF, 128), jnp.float32)] * 2,
        compiler_params=limit(16),
        name="add_gains",
    )(rows, counts, slots)


def pick(hit, values):
    return jnp.sum(jnp.where(hit, values, 0), axis=-1)


def per_device(integrals, coeffs, metric, atom_sizes, pair_device, pair_atom):
    aux_dev, bas_dev, window = integrals.shape
    occ = coeffs.shape[2]
    groups = lax.axis_size("atom")
    aux_count = lax.axis_size("aux")
    occ_part = occ // aux_count
    ref_count = pair_atom.shape[0]
    halo = (window - bas_dev) // 2
    scale = 1.0 / math.sqrt(2 * occ * aux_dev * aux_count * MAXBF)
    me = lax.axis_index("atom")

    own = coeffs.reshape(bas_dev, 2 * occ)
    forward = [(i, i + 1) for i in range(groups - 1)]
    backward = [(i + 1, i) for i in range(groups - 1)]
    low = lax.ppermute(own[bas_dev - halo :], "atom", forward)
    high = lax.ppermute(own[:halo], "atom", backward)

    packed = fit(
        low, own, high, integrals, metric, atom_sizes, pair_device.T, pair_atom[None]
    )
    got = lax.all_to_all(packed, "atom", split_axis=0, concat_axis=0, tiled=True)
    coef_part = lax.dynamic_slice_in_dim(
        coeffs, lax.axis_index("aux") * occ_part, occ_part, 2
    ).reshape(bas_dev, 2 * occ_part)
    me = jnp.full((1,), lax.axis_index("atom"), jnp.int32)

    targets = pair_device[:, 0]
    order = jnp.arange(ref_count, dtype=jnp.int32)
    earlier = (targets[:, None] == targets[None, :]) & (order[None, :] < order[:, None])
    ranks = jnp.sum(earlier.astype(jnp.int32), axis=1)
    asked = targets * 2 + ranks
    place = (order % 2) * 256 + (order // 2) * MAXBF
    asked_hit = asked[None, :] == jnp.arange(2 * groups, dtype=jnp.int32)[:, None]
    places = 512 + pick(asked_hit, place[None, :] - 512)

    table, sent = pair_sums(me, coef_part, got)
    owned = lax.all_to_all(sent, "atom", split_axis=0, concat_axis=0, tiled=True)
    own_sums = jnp.sum(owned[:, : 4 * MAXBF].astype(jnp.float32), axis=0).astype(jnp.bfloat16)
    shared = jnp.broadcast_to(own_sums[None], (aux_count,) + own_sums.shape)
    parts = lax.all_to_all(shared, "aux", split_axis=0, concat_axis=0, tiled=True)
    slots = make_slots(scale, targets, ranks, places, parts, owned)
    slots = lax.all_to_all(slots, "atom", split_axis=0, concat_axis=0, tiled=True)
    rows, counts = table[:, 32:34].reshape(-1), table[:, 34:36].reshape(-1)
    result = add_gains(rows, counts, slots, 2 * occ_part, bas_dev)
    return result.reshape(2, occ_part, bas_dev).transpose(2, 0, 1)


def solution(mesh):
    placed = (
        P("aux", "atom", None),
        P("atom", None, None),
        P("aux", None),
        P("atom", None),
        P("atom", None),
        P("atom"),
    )
    return jax.shard_map(
        per_device, mesh=mesh, in_specs=placed, out_specs=P("atom", None, "aux"), check_vma=False
    )
```

```python
import math

import jax
import jax.numpy as jnp
from jax import lax
from jax.experimental import pallas as pl
from jax.experimental.pallas import tpu as pltpu
from jax.sharding import PartitionSpec as P

MAXBF = 16
ROWBLK = 32
PACKED = ROWBLK + ROWBLK // 2
BATCH = 8
MIB = 1 << 20


def iota(shape, dim):
    return lax.broadcasted_iota(jnp.int32, shape, dim)


def dot(a, b):
    return jnp.dot(a, b, preferred_element_type=jnp.float32)


def dot_nt(a, b):
    return lax.dot_general(a, b, (((1,), (1,)), ((), ())), preferred_element_type=jnp.float32)


def dot_tn(a, b):
    return lax.dot_general(a, b, (((0,), (0,)), ((), ())), preferred_element_type=jnp.float32)


def ordered(part_ref, order_ref, window_ref, at):
    rows = part_ref.shape[0]
    half = part_ref.shape[1] // 2
    for t in range(3):
        real = part_ref[:, t * 128 : (t + 1) * 128]
        imag = part_ref[:, half + t * 128 : half + (t + 1) * 128]
        value = dot(jnp.concatenate([real, imag], axis=1), order_ref[t // 2])
        window_ref[at : at + rows, t * 256 : (t + 1) * 256] = value.astype(jnp.bfloat16)


def stage_kernel(
    own_ref, ints_hbm, metric_hbm, size_hbm, dev_hbm, atom_hbm,
    ints_ref, window_ref, order_ref, mix_ref, meta_ref,
    metric_ref, size_ref, dev_ref, atom_ref, rows_ref, sem_ref,
):
    sources = (ints_hbm, metric_hbm, size_hbm, dev_hbm, atom_hbm)
    targets = (ints_ref, metric_ref, size_ref, dev_ref, atom_ref)
    fetches = [
        pltpu.make_async_copy(a, b, sem_ref.at[i]) for i, (a, b) in enumerate(zip(sources, targets))
    ]
    for fetch in fetches:
        fetch.start()
    u, v = iota((256, 256), 0), iota((256, 256), 1)
    main_order = u == ((v % 128) // 64) * 128 + (v // 128) * 64 + v % 64
    side_order = u == ((v % 64) // 32) * 128 + (v // 64) * 32 + v % 32
    order_ref[0] = jnp.where(main_order, 1.0, 0.0).astype(jnp.bfloat16)
    order_ref[1] = jnp.where(side_order, 1.0, 0.0).astype(jnp.bfloat16)
    ordered(own_ref, order_ref, window_ref, 0)
    for fetch in fetches[1:]:
        fetch.wait()
    member = iota((256, 8), 0) // ROWBLK == iota((256, 8), 1)
    member = jnp.where(member, 1.0, 0.0).astype(jnp.bfloat16)
    mix = dot_nt(dot_nt(member, metric_ref[...]).astype(jnp.bfloat16), member)
    mix_ref[...] = jnp.where(u % ROWBLK == v % ROWBLK, mix, 0.0).astype(jnp.bfloat16)
    rows_ref[...] = jnp.zeros(rows_ref.shape, jnp.float32)
    for row, value_ref in enumerate((size_ref, dev_ref, atom_ref)):
        rows_ref[row : row + 1, 0 : value_ref.shape[1]] = value_ref[...].astype(jnp.float32)
    meta_ref[...] = rows_ref[...].astype(jnp.bfloat16)
    fetches[0].wait()


def fit_kernel(
    low_ref, high_ref, own_ref, ints_ref, order_ref, mix_ref, meta_ref, out_ref,
    window_ref, packed_ref, out_sem,
):
    aux_dev, bas_dev, span = ints_ref.shape
    blocks = bas_dev // ROWBLK
    halo = low_ref.shape[0]
    ordered(low_ref, order_ref, window_ref, 0)
    window_ref[halo : halo + bas_dev] = own_ref[...]
    ordered(high_ref, order_ref, window_ref, halo + bas_dev)
    mix = mix_ref[...]
    left = iota((ROWBLK // 2, 128), 1) < 64
    copies = []
    for u in range(blocks):
        if u % 4 == 0:
            ints = ints_ref[:, u * ROWBLK : (u + 4) * ROWBLK].reshape(-1, span)
            wide = dot(ints, window_ref[...]).astype(jnp.bfloat16)
            wide = wide.reshape(aux_dev, 4 * ROWBLK, -1)
        at = (u % 4) * ROWBLK
        half = wide[:, at : at + ROWBLK].reshape(aux_dev * ROWBLK, -1)
        fitted = dot(mix, half)
        main = slice(u * PACKED, u * PACKED + ROWBLK)
        side = slice(u * PACKED + ROWBLK, (u + 1) * PACKED)
        for p in range(aux_dev):
            rows = fitted[p * ROWBLK : (p + 1) * ROWBLK]
            for k in range(4):
                tile = rows[:, k * 128 : (k + 1) * 128]
                packed_ref[p * 4 + k, main] = tile.astype(jnp.bfloat16)
            for k in range(2):
                shared = rows[:, 512 + k * 128 : 640 + k * 128]
                top, bottom = shared[: ROWBLK // 2], shared[ROWBLK // 2 :]
                even = jnp.where(left, top, pltpu.roll(bottom, 64, 1))
                odd = jnp.where(left, pltpu.roll(top, 64, 1), bottom)
                packed_ref[p * 4 + 2 * k, side] = even.astype(jnp.bfloat16)
                packed_ref[p * 4 + 2 * k + 1, side] = odd.astype(jnp.bfloat16)
        if u == blocks - 1:
            for d in range(4 * aux_dev):
                packed_ref[d, blocks * PACKED : blocks * PACKED + 16] = meta_ref[...]
        if u % 2 == 1:
            first = (u - 1) * PACKED
            span_rows = pl.ds(first, 2 * PACKED + (16 if u == blocks - 1 else 0))
            copies.append(
                pltpu.make_async_copy(
                    packed_ref.at[:, span_rows], out_ref.at[:, span_rows], out_sem.at[u // 2]
                )
            )
            copies[-1].start()
    for copy in copies:
        copy.wait()


def end_table(me, got_ref, size_ref, dev_ref, atom_ref):
    groups, at = got_ref.shape[0], got_ref.shape[1] - 16
    for d in range(groups):
        rows = got_ref[d, at : at + 16].astype(jnp.float32)
        for i, dest in enumerate((size_ref, dev_ref, atom_ref)):
            dest[d : d + 1] = rows[i : i + 1]
    before = jnp.where(iota((128, 128), 0) < iota((128, 128), 1), 1.0, 0.0).astype(jnp.bfloat16)
    sizes = size_ref[...]
    packed = dot(sizes.astype(jnp.bfloat16), before) * 32.0 + sizes
    devices = dev_ref[...].astype(jnp.int32)
    atoms = atom_ref[...].astype(jnp.int32)
    found = jnp.zeros(packed.shape, jnp.float32)
    for d in range(groups):
        row = jnp.broadcast_to(packed[d : d + 1], packed.shape)
        found = jnp.where(devices == d, jnp.take_along_axis(row, atoms, axis=1), found)
    found = found.astype(jnp.int32)
    starts, counts = found // 32, found % 32
    lane = iota(found.shape, 1)
    here = (devices == me) & (lane < 32)
    rank = dot(jnp.where(here, 1.0, 0.0).astype(jnp.bfloat16), before)
    table = jnp.where(lane < 32, devices * 256 + starts, 0)
    for i, value in enumerate((starts, counts)):
        value = value.astype(jnp.float32)
        for r in range(2):
            one = jnp.sum(jnp.where(here & (rank == r), value, 0.0), axis=1, keepdims=True)
            table = jnp.where(lane == 32 + 2 * i + r, one.astype(jnp.int32), table)
    return table


def pair_kernel(
    me_ref, coef_ref, got_ref, table_ref, out_ref, real_ref, imag_ref, rows_ref, sums_ref,
    size_ref, dev_ref, atom_ref, row_ref, table_sem, sem_ref, *sides,
):
    table_ref[...] = end_table(me_ref[0], got_ref, size_ref, dev_ref, atom_ref)
    fetch = pltpu.make_async_copy(table_ref, row_ref, table_sem)
    fetch.start()
    groups, blocks = got_ref.shape[0], got_ref.shape[1] // PACKED
    lane = iota((ROWBLK // 2, 128), 1)
    left, valid = lane < 64, lane < 96

    def unpack(b, carry):
        for i in range(blocks):
            base = pl.multiple_of(b * (blocks * ROWBLK) + i * ROWBLK, ROWBLK)
            shared = got_ref[b, i * PACKED + ROWBLK : (i + 1) * PACKED].astype(jnp.float32)
            for h in range(2):
                at = i * PACKED + h * 16
                main = got_ref[b, at : at + 16].astype(jnp.float32)
                real = shared if h else pltpu.roll(shared, 64, 1)
                imag = pltpu.roll(shared, 96 if h else 32, 1)
                real = jnp.where(left, main, jnp.where(valid, real, 0.0))
                imag = jnp.where(left, pltpu.roll(main, 64, 1), jnp.where(valid, imag, 0.0))
                real_ref[pl.ds(base + h * 16, 16)] = real
                imag_ref[pl.ds(base + h * 16, 16)] = imag
        return carry

    lax.fori_loop(0, groups, unpack, 0, unroll=4)
    tail = groups * blocks * ROWBLK
    real_ref[tail : tail + MAXBF] = jnp.zeros((MAXBF, 128), jnp.float32)
    imag_ref[tail : tail + MAXBF] = jnp.zeros((MAXBF, 128), jnp.float32)
    bas_dev, width = coef_ref.shape
    rows_ref[...] = jnp.zeros(rows_ref.shape, jnp.float32)
    rows_ref[0:bas_dev, 0:width] = coef_ref[...].astype(jnp.float32)
    row_id = iota((MAXBF, 128), 0)
    lane_pair = lane // MAXBF
    batch = len(sides) // 4
    fetch.wait()

    def group(step, carry):
        for u in range(batch):
            g = step * batch + u
            for h in range(2):
                first_ref, second_ref = sides[u * 4 + h * 2], sides[u * 4 + h * 2 + 1]
                for j in range(16):
                    row = pl.ds(row_ref[g, h * 16 + j], 16)
                    place = (j // 2) * MAXBF
                    real, imag = real_ref[row], imag_ref[row]
                    if j % 2:
                        second_ref[place : place + 16, 0:128] = real.astype(jnp.bfloat16)
                        second_ref[place : place + 16, 128:256] = imag.astype(jnp.bfloat16)
                    else:
                        first_ref[place : place + 16, 0:128] = real.astype(jnp.bfloat16)
                        first_ref[place : place + 16, 128:256] = imag.astype(jnp.bfloat16)
                        place += 128
                        first_ref[place : place + 16, 0:128] = imag.astype(jnp.bfloat16)
                        first_ref[place : place + 16, 128:256] = (-real).astype(jnp.bfloat16)
                value = dot_nt(first_ref[...], second_ref[...])
                for c in range(2):
                    part = value[c * 128 : c * 128 + 16]
                    for j in range(1, 8):
                        here = value[c * 128 + j * 16 : c * 128 + j * 16 + 16]
                        part = jnp.where(lane_pair == j, here, part)
                    at = h * 32 + c * 16
                    sums_ref[g, at : at + 16] = part.astype(jnp.bfloat16)
                rows = rows_ref[pl.ds(row_ref[g, 32 + h], MAXBF)]
                rows = jnp.where(row_id < row_ref[g, 34 + h], rows, 0.0)
                sums_ref[g, 64 + h * 16 : 80 + h * 16] = rows.astype(jnp.bfloat16)
        send(step).start()
        return carry

    def send(step):
        done = pl.ds(step * batch, batch)
        return pltpu.make_async_copy(sums_ref.at[done], out_ref.at[done], sem_ref.at[step])

    lax.fori_loop(0, groups // batch, group, 0)
    for step in range(groups // batch):
        send(step).wait()


def slot_kernel(scale, target_ref, rank_ref, place_ref, parts_ref, got_ref, out_ref, tile_ref):
    total = parts_ref[0].astype(jnp.float32)
    for z in range(1, parts_ref.shape[0]):
        total = total + parts_ref[z].astype(jnp.float32)
    kernel = (total * scale).astype(jnp.bfloat16)
    u, v = iota((128, 128), 0), iota((128, 128), 1)
    same = u // MAXBF == v // MAXBF
    folds = [jnp.where(v == 96 + c * 16 + u % 16, 1.0, 0.0).astype(jnp.bfloat16) for c in range(2)]
    u, v = iota((32, 128), 0), iota((32, 128), 1)
    turned = jnp.where(v == 96 + u, jnp.where(u < MAXBF, 1.0, -1.0), 0.0).astype(jnp.bfloat16)

    def coef(e):
        at = pl.multiple_of(64 + rank_ref[e] * MAXBF, MAXBF)
        return got_ref[target_ref[e], pl.ds(at, MAXBF)].astype(jnp.float32)

    for h in range(2):
        block = kernel[h * 32 : (h + 1) * 32]
        first = jnp.zeros((128, 128), jnp.float32)
        for c in range(2):
            tile = block[c * MAXBF : (c + 1) * MAXBF].astype(jnp.float32)
            wide = jnp.where(same, jnp.concatenate([tile] * 8, axis=0), 0.0)
            first = first + dot(wide.astype(jnp.bfloat16), folds[c])
        second = dot_tn(block, turned)
        for j in range(8):
            pair, rows = h * 8 + j, slice(j * MAXBF, (j + 1) * MAXBF)
            at = pair * MAXBF
            tile_ref[at : at + MAXBF] = first[rows] + coef(2 * pair + 1)
            tile_ref[256 + at : 256 + at + MAXBF] = second[rows] + coef(2 * pair)
    tile_ref[512:528] = jnp.zeros((MAXBF, 128), jnp.float32)
    for s in range(2 * out_ref.shape[0]):
        rows = tile_ref[pl.ds(pl.multiple_of(place_ref[s], MAXBF), MAXBF)]
        out_ref[s // 2, (s % 2) * MAXBF : (s % 2 + 1) * MAXBF] = rows.astype(jnp.bfloat16)


def gain_kernel(row_ref, count_ref, slot_ref, out_ref, plain_ref, turned_ref):
    plain_ref[...] = jnp.zeros(plain_ref.shape, jnp.float32)
    turned_ref[...] = jnp.zeros(turned_ref.shape, jnp.float32)
    lane, row_id = iota((MAXBF, 128), 1), iota((MAXBF, 128), 0)
    masks = [lane < MAXBF, (lane >= MAXBF) & (lane < 2 * MAXBF)]
    for g in range(slot_ref.shape[0]):
        slots = slot_ref[g]
        wide = slots.astype(jnp.float32)
        tiles = []
        for c in range(2):
            for r in range(2):
                tile = wide[r * MAXBF : (r + 1) * MAXBF]
                tile = pltpu.roll(tile, 32 + 16 * (r - c), 1)
                tiles.append(jnp.where(masks[r], tile, 0.0))
        tiles = jnp.concatenate(tiles, axis=0)[:, 0:32].astype(jnp.bfloat16)
        gains = dot(tiles, slots)
        for c, sum_ref in enumerate((plain_ref, turned_ref)):
            for r in range(2):
                at = (2 * c + r) * MAXBF
                part = jnp.where(row_id < count_ref[2 * g + r], gains[at : at + MAXBF], 0.0)
                where = pl.ds(row_ref[2 * g + r], MAXBF)
                sum_ref[where] = sum_ref[where] + part
    width, bas_dev = out_ref.shape
    half = width // 2
    plain = plain_ref[0:bas_dev].T
    turned = turned_ref[0:bas_dev].T
    out_ref[0:half] = plain[0:half] - turned[half:width]
    out_ref[half:width] = plain[half:width] + turned[0:half]


def vmem_spec():
    return pl.BlockSpec(memory_space=pltpu.VMEM)


def smem_spec():
    return pl.BlockSpec(memory_space=pltpu.SMEM)


def limit(mib):
    return pltpu.CompilerParams(vmem_limit_bytes=mib * MIB)


def in_hbm(array):
    return pltpu.with_memory_space_constraint(array, pltpu.HBM)


def stage(own, *fetched):
    shapes = [fetched[0].shape, own.shape, (2, 256, 256), (256, 256), (16, 128)]
    return pl.pallas_call(
        stage_kernel,
        in_specs=[vmem_spec()] + [pl.BlockSpec(memory_space=pltpu.HBM)] * len(fetched),
        out_specs=[vmem_spec()] * len(shapes),
        out_shape=[pltpu.VMEM(shape, jnp.bfloat16) for shape in shapes],
        scratch_shapes=[pltpu.VMEM(x.shape, x.dtype) for x in fetched[1:]]
        + [pltpu.VMEM((16, 128), jnp.float32), pltpu.SemaphoreType.DMA((len(fetched),))],
        compiler_params=limit(16),
        cost_estimate=pl.CostEstimate(flops=1 << 28, bytes_accessed=5 * MIB, transcendentals=0),
        name="stage",
    )(own, *[in_hbm(x) for x in fetched])


def fit(low, high, window_rows, ints, order, mix, meta):
    aux_dev, bas_dev, window = ints.shape
    width = low.shape[1]
    blocks = bas_dev // ROWBLK
    shape = (4 * aux_dev, blocks * PACKED + 16, 128)
    return pl.pallas_call(
        fit_kernel,
        in_specs=[vmem_spec()] * 7,
        out_specs=pl.BlockSpec(memory_space=pltpu.HBM),
        out_shape=pltpu.HBM(shape, jnp.bfloat16),
        scratch_shapes=[
            pltpu.VMEM((window, width), jnp.bfloat16),
            pltpu.VMEM(shape, jnp.bfloat16),
            pltpu.SemaphoreType.DMA((blocks // 2,)),
        ],
        compiler_params=limit(32),
        cost_estimate=pl.CostEstimate(
            flops=2 * aux_dev * bas_dev * width * (window + 256),
            bytes_accessed=6 * MIB,
            transcendentals=0,
        ),
        name="fit",
    )(low, high, window_rows, ints, order, mix, meta)


def pair_sums(me, coef, got):
    groups = got.shape[0]
    rows = groups * (got.shape[1] // PACKED) * ROWBLK + MAXBF
    shape = (groups, 6 * MAXBF, 128)
    return pl.pallas_call(
        pair_kernel,
        in_specs=[smem_spec(), vmem_spec(), vmem_spec()],
        out_specs=[vmem_spec(), pl.BlockSpec(memory_space=pltpu.HBM)],
        out_shape=[
            jax.ShapeDtypeStruct((groups, 128), jnp.int32),
            pltpu.HBM(shape, jnp.bfloat16),
        ],
        scratch_shapes=[
            pltpu.VMEM((rows, 128), jnp.float32),
            pltpu.VMEM((rows, 128), jnp.float32),
            pltpu.VMEM((coef.shape[0] + MAXBF, 128), jnp.float32),
            pltpu.VMEM(shape, jnp.bfloat16),
            pltpu.VMEM((groups, 128), jnp.float32),
            pltpu.VMEM((groups, 128), jnp.float32),
            pltpu.VMEM((groups, 128), jnp.float32),
            pltpu.SMEM((groups, 128), jnp.int32),
            pltpu.SemaphoreType.DMA,
            pltpu.SemaphoreType.DMA((groups // BATCH,)),
        ]
        + [pltpu.VMEM((256, 256), jnp.bfloat16), pltpu.VMEM((128, 256), jnp.bfloat16)] * (2 * BATCH),
        compiler_params=limit(40),
        name="pair_sums",
    )(me, coef, got)


def make_slots(scale, targets, ranks, places, parts, got):
    def body(*refs):
        slot_kernel(scale, *refs)

    return pl.pallas_call(
        body,
        in_specs=[smem_spec()] * 3 + [vmem_spec()] * 2,
        out_specs=vmem_spec(),
        out_shape=jax.ShapeDtypeStruct((got.shape[0], 2 * MAXBF, 128), jnp.bfloat16),
        scratch_shapes=[pltpu.VMEM((528, 128), jnp.float32)],
        compiler_params=limit(16),
        name="make_slots",
    )(targets, ranks, places, parts, got)


def add_gains(rows, counts, slots, width, bas_dev):
    return pl.pallas_call(
        gain_kernel,
        in_specs=[smem_spec()] * 2 + [vmem_spec()],
        out_specs=vmem_spec(),
        out_shape=jax.ShapeDtypeStruct((width, bas_dev), jnp.float32),
        scratch_shapes=[pltpu.VMEM((bas_dev + MAXBF, 128), jnp.float32)] * 2,
        compiler_params=limit(16),
        name="add_gains",
    )(rows, counts, slots)


def pick(hit, values):
    return jnp.sum(jnp.where(hit, values, 0), axis=-1)


def per_device(integrals, coeffs, metric, atom_sizes, pair_device, pair_atom):
    aux_dev, bas_dev, window = integrals.shape
    occ = coeffs.shape[2]
    groups = lax.axis_size("atom")
    aux_count = lax.axis_size("aux")
    occ_part = occ // aux_count
    ref_count = pair_atom.shape[0]
    halo = (window - bas_dev) // 2
    scale = 1.0 / math.sqrt(2 * occ * aux_dev * aux_count * MAXBF)
    me = lax.axis_index("atom")

    own = coeffs.reshape(bas_dev, 2 * occ)
    forward = [(i, i + 1) for i in range(groups - 1)]
    backward = [(i + 1, i) for i in range(groups - 1)]
    low = lax.ppermute(own[bas_dev - halo :], "atom", forward)
    high = lax.ppermute(own[:halo], "atom", backward)

    ints, window_rows, order, mix, meta = stage(
        own, integrals, metric, atom_sizes, pair_device.T, pair_atom[None]
    )
    packed = fit(low, high, window_rows, ints, order, mix, meta)
    got = lax.all_to_all(packed, "atom", split_axis=0, concat_axis=0, tiled=True)
    coef_part = lax.dynamic_slice_in_dim(
        coeffs, lax.axis_index("aux") * occ_part, occ_part, 2
    ).reshape(bas_dev, 2 * occ_part)
    me = jnp.full((1,), lax.axis_index("atom"), jnp.int32)

    targets = pair_device[:, 0]
    order = jnp.arange(ref_count, dtype=jnp.int32)
    earlier = (targets[:, None] == targets[None, :]) & (order[None, :] < order[:, None])
    ranks = jnp.sum(earlier.astype(jnp.int32), axis=1)
    asked = targets * 2 + ranks
    place = (order % 2) * 256 + (order // 2) * MAXBF
    asked_hit = asked[None, :] == jnp.arange(2 * groups, dtype=jnp.int32)[:, None]
    places = 512 + pick(asked_hit, place[None, :] - 512)

    table, sent = pair_sums(me, coef_part, got)
    owned = lax.all_to_all(sent, "atom", split_axis=0, concat_axis=0, tiled=True)
    own_sums = jnp.sum(owned[:, : 4 * MAXBF].astype(jnp.float32), axis=0).astype(jnp.bfloat16)
    shared = jnp.broadcast_to(own_sums[None], (aux_count,) + own_sums.shape)
    parts = lax.all_to_all(shared, "aux", split_axis=0, concat_axis=0, tiled=True)
    slots = make_slots(scale, targets, ranks, places, parts, owned)
    slots = lax.all_to_all(slots, "atom", split_axis=0, concat_axis=0, tiled=True)
    rows, counts = table[:, 32:34].reshape(-1), table[:, 34:36].reshape(-1)
    result = add_gains(rows, counts, slots, 2 * occ_part, bas_dev)
    return result.reshape(2, occ_part, bas_dev).transpose(2, 0, 1)


def solution(mesh):
    placed = (
        P("aux", "atom", None),
        P("atom", None, None),
        P("aux", None),
        P("atom", None),
        P("atom", None),
        P("atom"),
    )
    return jax.shard_map(
        per_device, mesh=mesh, in_specs=placed, out_specs=P("atom", None, "aux"), check_vma=False
    )
```

```python
import math

import jax
import jax.numpy as jnp
from jax import lax
from jax.experimental import pallas as pl
from jax.experimental.pallas import tpu as pltpu
from jax.sharding import PartitionSpec as P

MAXBF = 16
ROWBLK = 32
PACKED = ROWBLK + ROWBLK // 2
BATCH = 8
MIB = 1 << 20


def iota(shape, dim):
    return lax.broadcasted_iota(jnp.int32, shape, dim)


def dot(a, b):
    return jnp.dot(a, b, preferred_element_type=jnp.float32)


def dot_nt(a, b):
    return lax.dot_general(a, b, (((1,), (1,)), ((), ())), preferred_element_type=jnp.float32)


def dot_tn(a, b):
    return lax.dot_general(a, b, (((0,), (0,)), ((), ())), preferred_element_type=jnp.float32)


def ordered(part_ref, order_ref, window_ref, at):
    rows = part_ref.shape[0]
    half = part_ref.shape[1] // 2
    for t in range(3):
        real = part_ref[:, t * 128 : (t + 1) * 128]
        imag = part_ref[:, half + t * 128 : half + (t + 1) * 128]
        value = dot(jnp.concatenate([real, imag], axis=1), order_ref[t // 2])
        place = pl.ds(at if isinstance(at, int) else pl.multiple_of(at, 128), rows)
        window_ref[place, t * 256 : (t + 1) * 256] = value.astype(jnp.bfloat16)


def stage_kernel(
    own_ref, ints_hbm, metric_hbm, size_hbm, dev_hbm, atom_hbm,
    ints_ref, window_ref, order_ref, mix_ref, meta_ref,
    metric_ref, size_ref, dev_ref, atom_ref, rows_ref, sem_ref,
):
    sources = (ints_hbm, metric_hbm, size_hbm, dev_hbm, atom_hbm)
    targets = (ints_ref, metric_ref, size_ref, dev_ref, atom_ref)
    fetches = [
        pltpu.make_async_copy(a, b, sem_ref.at[i]) for i, (a, b) in enumerate(zip(sources, targets))
    ]
    for fetch in fetches:
        fetch.start()
    u, v = iota((256, 256), 0), iota((256, 256), 1)
    main_order = u == ((v % 128) // 64) * 128 + (v // 128) * 64 + v % 64
    side_order = u == ((v % 64) // 32) * 128 + (v // 64) * 32 + v % 32
    order_ref[0] = jnp.where(main_order, 1.0, 0.0).astype(jnp.bfloat16)
    order_ref[1] = jnp.where(side_order, 1.0, 0.0).astype(jnp.bfloat16)
    ordered(own_ref, order_ref, window_ref, 0)
    for fetch in fetches[1:]:
        fetch.wait()
    member = iota((256, 8), 0) // ROWBLK == iota((256, 8), 1)
    member = jnp.where(member, 1.0, 0.0).astype(jnp.bfloat16)
    mix = dot_nt(dot_nt(member, metric_ref[...]).astype(jnp.bfloat16), member)
    mix_ref[...] = jnp.where(u % ROWBLK == v % ROWBLK, mix, 0.0).astype(jnp.bfloat16)
    rows_ref[...] = jnp.zeros(rows_ref.shape, jnp.float32)
    for row, value_ref in enumerate((size_ref, dev_ref, atom_ref)):
        rows_ref[row : row + 1, 0 : value_ref.shape[1]] = value_ref[...].astype(jnp.float32)
    meta_ref[...] = rows_ref[...].astype(jnp.bfloat16)
    fetches[0].wait()


def fit_kernel(
    odd_ref, near_ref, far_ref, own_ref, ints_ref, order_ref, mix_ref, meta_ref, out_ref,
    window_ref, packed_ref, out_sem,
):
    aux_dev, bas_dev, span = ints_ref.shape
    blocks = bas_dev // ROWBLK
    halo = near_ref.shape[0]
    far_at = odd_ref[0] * (halo + bas_dev)
    ordered(near_ref, order_ref, window_ref, halo + bas_dev - far_at)
    window_ref[halo : halo + bas_dev] = own_ref[...]
    ordered(far_ref, order_ref, window_ref, far_at)
    mix = mix_ref[...]
    left = iota((ROWBLK // 2, 128), 1) < 64
    copies = []
    for u in range(blocks):
        if u % 4 == 0:
            ints = ints_ref[:, u * ROWBLK : (u + 4) * ROWBLK].reshape(-1, span)
            wide = dot(ints, window_ref[...]).astype(jnp.bfloat16)
            wide = wide.reshape(aux_dev, 4 * ROWBLK, -1)
        at = (u % 4) * ROWBLK
        half = wide[:, at : at + ROWBLK].reshape(aux_dev * ROWBLK, -1)
        fitted = dot(mix, half)
        main = slice(u * PACKED, u * PACKED + ROWBLK)
        side = slice(u * PACKED + ROWBLK, (u + 1) * PACKED)
        for p in range(aux_dev):
            rows = fitted[p * ROWBLK : (p + 1) * ROWBLK]
            for k in range(4):
                tile = rows[:, k * 128 : (k + 1) * 128]
                packed_ref[p * 4 + k, main] = tile.astype(jnp.bfloat16)
            for k in range(2):
                shared = rows[:, 512 + k * 128 : 640 + k * 128]
                top, bottom = shared[: ROWBLK // 2], shared[ROWBLK // 2 :]
                even = jnp.where(left, top, pltpu.roll(bottom, 64, 1))
                odd = jnp.where(left, pltpu.roll(top, 64, 1), bottom)
                packed_ref[p * 4 + 2 * k, side] = even.astype(jnp.bfloat16)
                packed_ref[p * 4 + 2 * k + 1, side] = odd.astype(jnp.bfloat16)
        if u == blocks - 1:
            for d in range(4 * aux_dev):
                packed_ref[d, blocks * PACKED : blocks * PACKED + 16] = meta_ref[...]
        if u % 2 == 1:
            first = (u - 1) * PACKED
            span_rows = pl.ds(first, 2 * PACKED + (16 if u == blocks - 1 else 0))
            copies.append(
                pltpu.make_async_copy(
                    packed_ref.at[:, span_rows], out_ref.at[:, span_rows], out_sem.at[u // 2]
                )
            )
            copies[-1].start()
    for copy in copies:
        copy.wait()


def end_table(me, got_ref, size_ref, dev_ref, atom_ref):
    groups, at = got_ref.shape[0], got_ref.shape[1] - 16
    for d in range(groups):
        rows = got_ref[d, at : at + 16].astype(jnp.float32)
        for i, dest in enumerate((size_ref, dev_ref, atom_ref)):
            dest[d : d + 1] = rows[i : i + 1]
    before = jnp.where(iota((128, 128), 0) < iota((128, 128), 1), 1.0, 0.0).astype(jnp.bfloat16)
    sizes = size_ref[...]
    packed = dot(sizes.astype(jnp.bfloat16), before) * 32.0 + sizes
    devices = dev_ref[...].astype(jnp.int32)
    atoms = atom_ref[...].astype(jnp.int32)
    found = jnp.zeros(packed.shape, jnp.float32)
    for d in range(groups):
        row = jnp.broadcast_to(packed[d : d + 1], packed.shape)
        found = jnp.where(devices == d, jnp.take_along_axis(row, atoms, axis=1), found)
    found = found.astype(jnp.int32)
    starts, counts = found // 32, found % 32
    lane = iota(found.shape, 1)
    here = (devices == me) & (lane < 32)
    rank = dot(jnp.where(here, 1.0, 0.0).astype(jnp.bfloat16), before)
    table = jnp.where(lane < 32, devices * 256 + starts, 0)
    for i, value in enumerate((starts, counts)):
        value = value.astype(jnp.float32)
        for r in range(2):
            one = jnp.sum(jnp.where(here & (rank == r), value, 0.0), axis=1, keepdims=True)
            table = jnp.where(lane == 32 + 2 * i + r, one.astype(jnp.int32), table)
    return table


def pair_kernel(
    me_ref, coef_ref, got_ref, table_ref, out_ref, real_ref, imag_ref, rows_ref, sums_ref,
    size_ref, dev_ref, atom_ref, row_ref, table_sem, sem_ref, *sides,
):
    table_ref[...] = end_table(me_ref[0], got_ref, size_ref, dev_ref, atom_ref)
    fetch = pltpu.make_async_copy(table_ref, row_ref, table_sem)
    fetch.start()
    groups, blocks = got_ref.shape[0], got_ref.shape[1] // PACKED
    lane = iota((ROWBLK // 2, 128), 1)
    left, valid = lane < 64, lane < 96

    def unpack(b, carry):
        for i in range(blocks):
            base = pl.multiple_of(b * (blocks * ROWBLK) + i * ROWBLK, ROWBLK)
            shared = got_ref[b, i * PACKED + ROWBLK : (i + 1) * PACKED].astype(jnp.float32)
            for h in range(2):
                at = i * PACKED + h * 16
                main = got_ref[b, at : at + 16].astype(jnp.float32)
                real = shared if h else pltpu.roll(shared, 64, 1)
                imag = pltpu.roll(shared, 96 if h else 32, 1)
                real = jnp.where(left, main, jnp.where(valid, real, 0.0))
                imag = jnp.where(left, pltpu.roll(main, 64, 1), jnp.where(valid, imag, 0.0))
                real_ref[pl.ds(base + h * 16, 16)] = real
                imag_ref[pl.ds(base + h * 16, 16)] = imag
        return carry

    lax.fori_loop(0, groups, unpack, 0, unroll=4)
    tail = groups * blocks * ROWBLK
    real_ref[tail : tail + MAXBF] = jnp.zeros((MAXBF, 128), jnp.float32)
    imag_ref[tail : tail + MAXBF] = jnp.zeros((MAXBF, 128), jnp.float32)
    bas_dev, width = coef_ref.shape
    rows_ref[...] = jnp.zeros(rows_ref.shape, jnp.float32)
    rows_ref[0:bas_dev, 0:width] = coef_ref[...].astype(jnp.float32)
    row_id = iota((MAXBF, 128), 0)
    lane_pair = lane // MAXBF
    batch = len(sides) // 4
    fetch.wait()

    def group(step, carry):
        for u in range(batch):
            g = step * batch + u
            for h in range(2):
                first_ref, second_ref = sides[u * 4 + h * 2], sides[u * 4 + h * 2 + 1]
                for j in range(16):
                    row = pl.ds(row_ref[g, h * 16 + j], 16)
                    place = (j // 2) * MAXBF
                    real, imag = real_ref[row], imag_ref[row]
                    if j % 2:
                        second_ref[place : place + 16, 0:128] = real.astype(jnp.bfloat16)
                        second_ref[place : place + 16, 128:256] = imag.astype(jnp.bfloat16)
                    else:
                        first_ref[place : place + 16, 0:128] = real.astype(jnp.bfloat16)
                        first_ref[place : place + 16, 128:256] = imag.astype(jnp.bfloat16)
                        place += 128
                        first_ref[place : place + 16, 0:128] = imag.astype(jnp.bfloat16)
                        first_ref[place : place + 16, 128:256] = (-real).astype(jnp.bfloat16)
                value = dot_nt(first_ref[...], second_ref[...])
                for c in range(2):
                    part = value[c * 128 : c * 128 + 16]
                    for j in range(1, 8):
                        here = value[c * 128 + j * 16 : c * 128 + j * 16 + 16]
                        part = jnp.where(lane_pair == j, here, part)
                    at = h * 32 + c * 16
                    sums_ref[g, at : at + 16] = part.astype(jnp.bfloat16)
                rows = rows_ref[pl.ds(row_ref[g, 32 + h], MAXBF)]
                rows = jnp.where(row_id < row_ref[g, 34 + h], rows, 0.0)
                sums_ref[g, 64 + h * 16 : 80 + h * 16] = rows.astype(jnp.bfloat16)
        send(step).start()
        return carry

    def send(step):
        done = pl.ds(step * batch, batch)
        return pltpu.make_async_copy(sums_ref.at[done], out_ref.at[done], sem_ref.at[step])

    lax.fori_loop(0, groups // batch, group, 0)
    for step in range(groups // batch):
        send(step).wait()


def slot_kernel(scale, target_ref, rank_ref, place_ref, parts_ref, got_ref, out_ref, tile_ref):
    total = parts_ref[0].astype(jnp.float32)
    for z in range(1, parts_ref.shape[0]):
        total = total + parts_ref[z].astype(jnp.float32)
    kernel = (total * scale).astype(jnp.bfloat16)
    u, v = iota((128, 128), 0), iota((128, 128), 1)
    same = u // MAXBF == v // MAXBF
    folds = [jnp.where(v == 96 + c * 16 + u % 16, 1.0, 0.0).astype(jnp.bfloat16) for c in range(2)]
    u, v = iota((32, 128), 0), iota((32, 128), 1)
    turned = jnp.where(v == 96 + u, jnp.where(u < MAXBF, 1.0, -1.0), 0.0).astype(jnp.bfloat16)

    def coef(e):
        at = pl.multiple_of(64 + rank_ref[e] * MAXBF, MAXBF)
        return got_ref[target_ref[e], pl.ds(at, MAXBF)].astype(jnp.float32)

    for h in range(2):
        block = kernel[h * 32 : (h + 1) * 32]
        first = jnp.zeros((128, 128), jnp.float32)
        for c in range(2):
            tile = block[c * MAXBF : (c + 1) * MAXBF].astype(jnp.float32)
            wide = jnp.where(same, jnp.concatenate([tile] * 8, axis=0), 0.0)
            first = first + dot(wide.astype(jnp.bfloat16), folds[c])
        second = dot_tn(block, turned)
        for j in range(8):
            pair, rows = h * 8 + j, slice(j * MAXBF, (j + 1) * MAXBF)
            at = pair * MAXBF
            tile_ref[at : at + MAXBF] = first[rows] + coef(2 * pair + 1)
            tile_ref[256 + at : 256 + at + MAXBF] = second[rows] + coef(2 * pair)
    tile_ref[512:528] = jnp.zeros((MAXBF, 128), jnp.float32)
    for s in range(2 * out_ref.shape[0]):
        rows = tile_ref[pl.ds(pl.multiple_of(place_ref[s], MAXBF), MAXBF)]
        out_ref[s // 2, (s % 2) * MAXBF : (s % 2 + 1) * MAXBF] = rows.astype(jnp.bfloat16)


def gain_kernel(row_ref, count_ref, slot_ref, out_ref, sum_ref, turned_ref):
    groups, rows, _ = slot_ref.shape
    width, bas_dev = out_ref.shape
    half = width // 2
    u, v = iota((128, 128), 0), iota((128, 128), 1)
    turn = jnp.where((v < half) & (u == v + half), -1.0, 0.0)
    turn = jnp.where((v >= half) & (v < width) & (u == v - half), 1.0, turn).astype(jnp.bfloat16)
    turned = dot(slot_ref[...].reshape(groups * rows, 128), turn).astype(jnp.bfloat16)
    turned_ref[...] = turned.reshape(groups, rows, 128)
    sum_ref[...] = jnp.zeros(sum_ref.shape, jnp.float32)
    lane, row_id = iota((MAXBF, 128), 1), iota((MAXBF, 128), 0)
    for g in range(groups):
        slots = slot_ref[g]
        wide = slots.astype(jnp.float32)
        tiles = []
        for r in range(2):
            tile = wide[r * MAXBF : (r + 1) * MAXBF]
            real = jnp.where(lane // MAXBF == r, pltpu.roll(tile, 32 + 16 * r, 1), 0.0)
            imag = jnp.where(lane // MAXBF == 2 + r, pltpu.roll(tile, 48 + 16 * r, 1), 0.0)
            tiles.append(real + imag)
        tiles = jnp.concatenate(tiles, axis=0)[:, 0:64].astype(jnp.bfloat16)
        gains = dot(tiles, jnp.concatenate([slots, turned_ref[g]], axis=0))
        for r in range(2):
            part = gains[r * MAXBF : (r + 1) * MAXBF]
            part = jnp.where(row_id < count_ref[2 * g + r], part, 0.0)
            where = pl.ds(row_ref[2 * g + r], MAXBF)
            sum_ref[where] = sum_ref[where] + part
    out_ref[...] = sum_ref[0:bas_dev].T[0:width]


def vmem_spec():
    return pl.BlockSpec(memory_space=pltpu.VMEM)


def smem_spec():
    return pl.BlockSpec(memory_space=pltpu.SMEM)


def limit(mib):
    return pltpu.CompilerParams(vmem_limit_bytes=mib * MIB)


def in_hbm(array):
    return pltpu.with_memory_space_constraint(array, pltpu.HBM)


def stage(own, *fetched):
    shapes = [fetched[0].shape, own.shape, (2, 256, 256), (256, 256), (16, 128)]
    return pl.pallas_call(
        stage_kernel,
        in_specs=[vmem_spec()] + [pl.BlockSpec(memory_space=pltpu.HBM)] * len(fetched),
        out_specs=[vmem_spec()] * len(shapes),
        out_shape=[pltpu.VMEM(shape, jnp.bfloat16) for shape in shapes],
        scratch_shapes=[pltpu.VMEM(x.shape, x.dtype) for x in fetched[1:]]
        + [pltpu.VMEM((16, 128), jnp.float32), pltpu.SemaphoreType.DMA((len(fetched),))],
        compiler_params=limit(16),
        cost_estimate=pl.CostEstimate(flops=1 << 28, bytes_accessed=5 * MIB, transcendentals=0),
        name="stage",
    )(own, *[in_hbm(x) for x in fetched])


def fit(odd, near, far, window_rows, ints, order, mix, meta):
    aux_dev, bas_dev, window = ints.shape
    width = near.shape[1]
    blocks = bas_dev // ROWBLK
    shape = (4 * aux_dev, blocks * PACKED + 16, 128)
    return pl.pallas_call(
        fit_kernel,
        in_specs=[smem_spec()] + [vmem_spec()] * 7,
        out_specs=pl.BlockSpec(memory_space=pltpu.HBM),
        out_shape=pltpu.HBM(shape, jnp.bfloat16),
        scratch_shapes=[
            pltpu.VMEM((window, width), jnp.bfloat16),
            pltpu.VMEM(shape, jnp.bfloat16),
            pltpu.SemaphoreType.DMA((blocks // 2,)),
        ],
        compiler_params=limit(32),
        cost_estimate=pl.CostEstimate(
            flops=2 * aux_dev * bas_dev * width * (window + 256),
            bytes_accessed=6 * MIB,
            transcendentals=0,
        ),
        name="fit",
    )(odd, near, far, window_rows, ints, order, mix, meta)


def pair_sums(me, coef, got):
    groups = got.shape[0]
    rows = groups * (got.shape[1] // PACKED) * ROWBLK + MAXBF
    shape = (groups, 6 * MAXBF, 128)
    return pl.pallas_call(
        pair_kernel,
        in_specs=[smem_spec(), vmem_spec(), vmem_spec()],
        out_specs=[vmem_spec(), pl.BlockSpec(memory_space=pltpu.HBM)],
        out_shape=[
            jax.ShapeDtypeStruct((groups, 128), jnp.int32),
            pltpu.HBM(shape, jnp.bfloat16),
        ],
        scratch_shapes=[
            pltpu.VMEM((rows, 128), jnp.float32),
            pltpu.VMEM((rows, 128), jnp.float32),
            pltpu.VMEM((coef.shape[0] + MAXBF, 128), jnp.float32),
            pltpu.VMEM(shape, jnp.bfloat16),
            pltpu.VMEM((groups, 128), jnp.float32),
            pltpu.VMEM((groups, 128), jnp.float32),
            pltpu.VMEM((groups, 128), jnp.float32),
            pltpu.SMEM((groups, 128), jnp.int32),
            pltpu.SemaphoreType.DMA,
            pltpu.SemaphoreType.DMA((groups // BATCH,)),
        ]
        + [pltpu.VMEM((256, 256), jnp.bfloat16), pltpu.VMEM((128, 256), jnp.bfloat16)] * (2 * BATCH),
        compiler_params=limit(40),
        name="pair_sums",
    )(me, coef, got)


def make_slots(scale, targets, ranks, places, parts, got):
    def body(*refs):
        slot_kernel(scale, *refs)

    return pl.pallas_call(
        body,
        in_specs=[smem_spec()] * 3 + [vmem_spec()] * 2,
        out_specs=vmem_spec(),
        out_shape=jax.ShapeDtypeStruct((got.shape[0], 2 * MAXBF, 128), jnp.bfloat16),
        scratch_shapes=[pltpu.VMEM((528, 128), jnp.float32)],
        compiler_params=limit(16),
        name="make_slots",
    )(targets, ranks, places, parts, got)


def add_gains(rows, counts, slots, width, bas_dev):
    return pl.pallas_call(
        gain_kernel,
        in_specs=[smem_spec()] * 2 + [vmem_spec()],
        out_specs=vmem_spec(),
        out_shape=jax.ShapeDtypeStruct((width, bas_dev), jnp.float32),
        scratch_shapes=[
            pltpu.VMEM((bas_dev + MAXBF, 128), jnp.float32),
            pltpu.VMEM(slots.shape, jnp.bfloat16),
        ],
        compiler_params=limit(16),
        name="add_gains",
    )(rows, counts, slots)


def pick(hit, values):
    return jnp.sum(jnp.where(hit, values, 0), axis=-1)


def per_device(integrals, coeffs, metric, atom_sizes, pair_device, pair_atom):
    aux_dev, bas_dev, window = integrals.shape
    occ = coeffs.shape[2]
    groups = lax.axis_size("atom")
    aux_count = lax.axis_size("aux")
    occ_part = occ // aux_count
    ref_count = pair_atom.shape[0]
    halo = (window - bas_dev) // 2
    scale = 1.0 / math.sqrt(2 * occ * aux_dev * aux_count * MAXBF)
    me = lax.axis_index("atom")

    own = coeffs.reshape(bas_dev, 2 * occ)
    odd = lax.axis_index("atom") % 2
    near = lax.dynamic_slice_in_dim(own, (1 - odd) * halo, halo, 0)
    near = lax.ppermute(near, "atom", [(i, i ^ 1) for i in range(groups)])
    far = lax.dynamic_slice_in_dim(own, odd * halo, halo, 0)
    inner = range(1, groups - 1)
    far = lax.ppermute(far, "atom", [(i, i + 1 if i % 2 else i - 1) for i in inner])

    ints, window_rows, order, mix, meta = stage(
        own, integrals, metric, atom_sizes, pair_device.T, pair_atom[None]
    )
    odd = jnp.full((1,), odd, jnp.int32)
    packed = fit(odd, near, far, window_rows, ints, order, mix, meta)
    got = lax.all_to_all(packed, "atom", split_axis=0, concat_axis=0, tiled=True)
    coef_part = lax.dynamic_slice_in_dim(
        coeffs, lax.axis_index("aux") * occ_part, occ_part, 2
    ).reshape(bas_dev, 2 * occ_part)
    me = jnp.full((1,), lax.axis_index("atom"), jnp.int32)

    targets = pair_device[:, 0]
    order = jnp.arange(ref_count, dtype=jnp.int32)
    earlier = (targets[:, None] == targets[None, :]) & (order[None, :] < order[:, None])
    ranks = jnp.sum(earlier.astype(jnp.int32), axis=1)
    asked = targets * 2 + ranks
    place = (order % 2) * 256 + (order // 2) * MAXBF
    asked_hit = asked[None, :] == jnp.arange(2 * groups, dtype=jnp.int32)[:, None]
    places = 512 + pick(asked_hit, place[None, :] - 512)

    table, sent = pair_sums(me, coef_part, got)
    owned = lax.all_to_all(sent, "atom", split_axis=0, concat_axis=0, tiled=True)
    own_sums = jnp.sum(owned[:, : 4 * MAXBF].astype(jnp.float32), axis=0).astype(jnp.bfloat16)
    shared = jnp.broadcast_to(own_sums[None], (aux_count,) + own_sums.shape)
    parts = lax.all_to_all(shared, "aux", split_axis=0, concat_axis=0, tiled=True)
    slots = make_slots(scale, targets, ranks, places, parts, owned)
    slots = lax.all_to_all(slots, "atom", split_axis=0, concat_axis=0, tiled=True)
    rows, counts = table[:, 32:34].reshape(-1), table[:, 34:36].reshape(-1)
    result = add_gains(rows, counts, slots, 2 * occ_part, bas_dev)
    return result.reshape(2, occ_part, bas_dev).transpose(2, 0, 1)


def solution(mesh):
    placed = (
        P("aux", "atom", None),
        P("atom", None, None),
        P("aux", None),
        P("atom", None),
        P("atom", None),
        P("atom"),
    )
    return jax.shard_map(
        per_device, mesh=mesh, in_specs=placed, out_specs=P("atom", None, "aux"), check_vma=False
    )
```

```python
import math

import jax
import jax.numpy as jnp
from jax import lax
from jax.experimental import pallas as pl
from jax.experimental.pallas import tpu as pltpu
from jax.sharding import PartitionSpec as P

MAXBF = 16
ROWBLK = 32
PACKED = ROWBLK + ROWBLK // 2
BATCH = 16
MIB = 1 << 20


def iota(shape, dim):
    return lax.broadcasted_iota(jnp.int32, shape, dim)


def dot(a, b):
    return jnp.dot(a, b, preferred_element_type=jnp.float32)


def dot_nt(a, b):
    return lax.dot_general(a, b, (((1,), (1,)), ((), ())), preferred_element_type=jnp.float32)


def dot_tn(a, b):
    return lax.dot_general(a, b, (((0,), (0,)), ((), ())), preferred_element_type=jnp.float32)


def ordered(part_ref, order_ref, window_ref, at):
    rows = part_ref.shape[0]
    half = part_ref.shape[1] // 2
    for t in range(3):
        real = part_ref[:, t * 128 : (t + 1) * 128]
        imag = part_ref[:, half + t * 128 : half + (t + 1) * 128]
        value = dot(jnp.concatenate([real, imag], axis=1), order_ref[t // 2])
        place = pl.ds(at if isinstance(at, int) else pl.multiple_of(at, 128), rows)
        window_ref[place, t * 256 : (t + 1) * 256] = value.astype(jnp.bfloat16)


def stage_kernel(
    own_ref, ints_hbm, metric_hbm, size_hbm, dev_hbm, atom_hbm,
    ints_ref, window_ref, order_ref, mix_ref, meta_ref,
    metric_ref, size_ref, dev_ref, atom_ref, rows_ref, sem_ref,
):
    sources = (ints_hbm, metric_hbm, size_hbm, dev_hbm, atom_hbm)
    targets = (ints_ref, metric_ref, size_ref, dev_ref, atom_ref)
    fetches = [
        pltpu.make_async_copy(a, b, sem_ref.at[i]) for i, (a, b) in enumerate(zip(sources, targets))
    ]
    for fetch in fetches:
        fetch.start()
    u, v = iota((256, 256), 0), iota((256, 256), 1)
    main_order = u == ((v % 128) // 64) * 128 + (v // 128) * 64 + v % 64
    side_order = u == ((v % 64) // 32) * 128 + (v // 64) * 32 + v % 32
    order_ref[0] = jnp.where(main_order, 1.0, 0.0).astype(jnp.bfloat16)
    order_ref[1] = jnp.where(side_order, 1.0, 0.0).astype(jnp.bfloat16)
    ordered(own_ref, order_ref, window_ref, 0)
    for fetch in fetches[1:]:
        fetch.wait()
    member = iota((256, 8), 0) // ROWBLK == iota((256, 8), 1)
    member = jnp.where(member, 1.0, 0.0).astype(jnp.bfloat16)
    mix = dot_nt(dot_nt(member, metric_ref[...]).astype(jnp.bfloat16), member)
    mix_ref[...] = jnp.where(u % ROWBLK == v % ROWBLK, mix, 0.0).astype(jnp.bfloat16)
    rows_ref[...] = jnp.zeros(rows_ref.shape, jnp.float32)
    for row, value_ref in enumerate((size_ref, dev_ref, atom_ref)):
        rows_ref[row : row + 1, 0 : value_ref.shape[1]] = value_ref[...].astype(jnp.float32)
    meta_ref[...] = rows_ref[...].astype(jnp.bfloat16)
    fetches[0].wait()


def fit_kernel(
    odd_ref, near_ref, far_ref, own_ref, ints_ref, order_ref, mix_ref, meta_ref, out_ref,
    window_ref, packed_ref, out_sem,
):
    aux_dev, bas_dev, span = ints_ref.shape
    blocks = bas_dev // ROWBLK
    halo = near_ref.shape[0]
    far_at = odd_ref[0] * (halo + bas_dev)
    ordered(near_ref, order_ref, window_ref, halo + bas_dev - far_at)
    window_ref[halo : halo + bas_dev] = own_ref[...]
    ordered(far_ref, order_ref, window_ref, far_at)
    mix = mix_ref[...]
    left = iota((ROWBLK // 2, 128), 1) < 64
    copies = []
    for u in range(blocks):
        if u % 4 == 0:
            ints = ints_ref[:, u * ROWBLK : (u + 4) * ROWBLK].reshape(-1, span)
            wide = dot(ints, window_ref[...]).astype(jnp.bfloat16)
            wide = wide.reshape(aux_dev, 4 * ROWBLK, -1)
        at = (u % 4) * ROWBLK
        half = wide[:, at : at + ROWBLK].reshape(aux_dev * ROWBLK, -1)
        fitted = dot(mix, half)
        main = slice(u * PACKED, u * PACKED + ROWBLK)
        side = slice(u * PACKED + ROWBLK, (u + 1) * PACKED)
        for p in range(aux_dev):
            rows = fitted[p * ROWBLK : (p + 1) * ROWBLK]
            for k in range(4):
                tile = rows[:, k * 128 : (k + 1) * 128]
                packed_ref[p * 4 + k, main] = tile.astype(jnp.bfloat16)
            for k in range(2):
                shared = rows[:, 512 + k * 128 : 640 + k * 128]
                top, bottom = shared[: ROWBLK // 2], shared[ROWBLK // 2 :]
                even = jnp.where(left, top, pltpu.roll(bottom, 64, 1))
                odd = jnp.where(left, pltpu.roll(top, 64, 1), bottom)
                packed_ref[p * 4 + 2 * k, side] = even.astype(jnp.bfloat16)
                packed_ref[p * 4 + 2 * k + 1, side] = odd.astype(jnp.bfloat16)
        if u == blocks - 1:
            for d in range(4 * aux_dev):
                packed_ref[d, blocks * PACKED : blocks * PACKED + 16] = meta_ref[...]
        if u % 2 == 1:
            first = (u - 1) * PACKED
            span_rows = pl.ds(first, 2 * PACKED + (16 if u == blocks - 1 else 0))
            copies.append(
                pltpu.make_async_copy(
                    packed_ref.at[:, span_rows], out_ref.at[:, span_rows], out_sem.at[u // 2]
                )
            )
            copies[-1].start()
    for copy in copies:
        copy.wait()


def end_table(me, got_ref, size_ref, dev_ref, atom_ref):
    groups, at = got_ref.shape[0], got_ref.shape[1] - 16
    for d in range(groups):
        rows = got_ref[d, at : at + 16].astype(jnp.float32)
        for i, dest in enumerate((size_ref, dev_ref, atom_ref)):
            dest[d : d + 1] = rows[i : i + 1]
    before = jnp.where(iota((128, 128), 0) < iota((128, 128), 1), 1.0, 0.0).astype(jnp.bfloat16)
    sizes = size_ref[...]
    packed = dot(sizes.astype(jnp.bfloat16), before) * 32.0 + sizes
    devices = dev_ref[...].astype(jnp.int32)
    atoms = atom_ref[...].astype(jnp.int32)
    found = jnp.zeros(packed.shape, jnp.float32)
    for d in range(groups):
        row = jnp.broadcast_to(packed[d : d + 1], packed.shape)
        found = jnp.where(devices == d, jnp.take_along_axis(row, atoms, axis=1), found)
    found = found.astype(jnp.int32)
    starts, counts = found // 32, found % 32
    lane = iota(found.shape, 1)
    here = (devices == me) & (lane < 32)
    rank = dot(jnp.where(here, 1.0, 0.0).astype(jnp.bfloat16), before)
    table = jnp.where(lane < 32, devices * 256 + starts, 0)
    for i, value in enumerate((starts, counts)):
        value = value.astype(jnp.float32)
        for r in range(2):
            one = jnp.sum(jnp.where(here & (rank == r), value, 0.0), axis=1, keepdims=True)
            table = jnp.where(lane == 32 + 2 * i + r, one.astype(jnp.int32), table)
    return table


def pair_kernel(
    me_ref, coef_ref, got_ref, table_ref, out_ref, real_ref, imag_ref, rows_ref, sums_ref,
    size_ref, dev_ref, atom_ref, row_ref, table_sem, sem_ref, *sides,
):
    table_ref[...] = end_table(me_ref[0], got_ref, size_ref, dev_ref, atom_ref)
    fetch = pltpu.make_async_copy(table_ref, row_ref, table_sem)
    fetch.start()
    groups, blocks = got_ref.shape[0], got_ref.shape[1] // PACKED
    lane = iota((ROWBLK // 2, 128), 1)
    left, valid = lane < 64, lane < 96

    def unpack(b, carry):
        for i in range(blocks):
            base = pl.multiple_of(b * (blocks * ROWBLK) + i * ROWBLK, ROWBLK)
            shared = got_ref[b, i * PACKED + ROWBLK : (i + 1) * PACKED].astype(jnp.float32)
            for h in range(2):
                at = i * PACKED + h * 16
                main = got_ref[b, at : at + 16].astype(jnp.float32)
                real = shared if h else pltpu.roll(shared, 64, 1)
                imag = pltpu.roll(shared, 96 if h else 32, 1)
                real = jnp.where(left, main, jnp.where(valid, real, 0.0))
                imag = jnp.where(left, pltpu.roll(main, 64, 1), jnp.where(valid, imag, 0.0))
                real_ref[pl.ds(base + h * 16, 16)] = real
                imag_ref[pl.ds(base + h * 16, 16)] = imag
        return carry

    lax.fori_loop(0, groups, unpack, 0, unroll=8)
    tail = groups * blocks * ROWBLK
    real_ref[tail : tail + MAXBF] = jnp.zeros((MAXBF, 128), jnp.float32)
    imag_ref[tail : tail + MAXBF] = jnp.zeros((MAXBF, 128), jnp.float32)
    bas_dev, width = coef_ref.shape
    rows_ref[...] = jnp.zeros(rows_ref.shape, jnp.float32)
    rows_ref[0:bas_dev, 0:width] = coef_ref[...].astype(jnp.float32)
    row_id = iota((MAXBF, 128), 0)
    lane_pair = lane // MAXBF
    batch = len(sides) // 4
    fetch.wait()

    def group(step, carry):
        for u in range(batch):
            g = step * batch + u
            for h in range(2):
                first_ref, second_ref = sides[u * 4 + h * 2], sides[u * 4 + h * 2 + 1]
                for j in range(16):
                    row = pl.ds(row_ref[g, h * 16 + j], 16)
                    place = (j // 2) * MAXBF
                    real, imag = real_ref[row], imag_ref[row]
                    if j % 2:
                        second_ref[place : place + 16, 0:128] = real.astype(jnp.bfloat16)
                        second_ref[place : place + 16, 128:256] = imag.astype(jnp.bfloat16)
                    else:
                        first_ref[place : place + 16, 0:128] = real.astype(jnp.bfloat16)
                        first_ref[place : place + 16, 128:256] = imag.astype(jnp.bfloat16)
                        place += 128
                        first_ref[place : place + 16, 0:128] = imag.astype(jnp.bfloat16)
                        first_ref[place : place + 16, 128:256] = (-real).astype(jnp.bfloat16)
                value = dot_nt(first_ref[...], second_ref[...])
                for c in range(2):
                    part = value[c * 128 : c * 128 + 16]
                    for j in range(1, 8):
                        here = value[c * 128 + j * 16 : c * 128 + j * 16 + 16]
                        part = jnp.where(lane_pair == j, here, part)
                    at = h * 32 + c * 16
                    sums_ref[g, at : at + 16] = part.astype(jnp.bfloat16)
                rows = rows_ref[pl.ds(row_ref[g, 32 + h], MAXBF)]
                rows = jnp.where(row_id < row_ref[g, 34 + h], rows, 0.0)
                sums_ref[g, 64 + h * 16 : 80 + h * 16] = rows.astype(jnp.bfloat16)
        send(step).start()
        return carry

    def send(step):
        done = pl.ds(step * batch, batch)
        return pltpu.make_async_copy(sums_ref.at[done], out_ref.at[done], sem_ref.at[step])

    lax.fori_loop(0, groups // batch, group, 0)
    for step in range(groups // batch):
        send(step).wait()


def slot_kernel(scale, target_ref, rank_ref, place_ref, parts_ref, got_ref, out_ref, tile_ref):
    total = parts_ref[0].astype(jnp.float32)
    for z in range(1, parts_ref.shape[0]):
        total = total + parts_ref[z].astype(jnp.float32)
    kernel = (total * scale).astype(jnp.bfloat16)
    u, v = iota((128, 128), 0), iota((128, 128), 1)
    same = u // MAXBF == v // MAXBF
    folds = [jnp.where(v == 96 + c * 16 + u % 16, 1.0, 0.0).astype(jnp.bfloat16) for c in range(2)]
    u, v = iota((32, 128), 0), iota((32, 128), 1)
    turned = jnp.where(v == 96 + u, jnp.where(u < MAXBF, 1.0, -1.0), 0.0).astype(jnp.bfloat16)

    def coef(e):
        at = pl.multiple_of(64 + rank_ref[e] * MAXBF, MAXBF)
        return got_ref[target_ref[e], pl.ds(at, MAXBF)]

    for h in range(2):
        block = kernel[h * 32 : (h + 1) * 32]
        first = jnp.zeros((128, 128), jnp.float32)
        for c in range(2):
            tile = block[c * MAXBF : (c + 1) * MAXBF].astype(jnp.float32)
            wide = jnp.where(same, jnp.concatenate([tile] * 8, axis=0), 0.0)
            first = first + dot(wide.astype(jnp.bfloat16), folds[c])
        first = first.astype(jnp.bfloat16)
        second = dot_tn(block, turned).astype(jnp.bfloat16)
        for j in range(8):
            pair, rows = h * 8 + j, slice(j * MAXBF, (j + 1) * MAXBF)
            at = pair * MAXBF
            tile_ref[at : at + MAXBF] = first[rows] + coef(2 * pair + 1)
            tile_ref[256 + at : 256 + at + MAXBF] = second[rows] + coef(2 * pair)
    tile_ref[512:528] = jnp.zeros((MAXBF, 128), jnp.bfloat16)
    for s in range(2 * out_ref.shape[0]):
        rows = tile_ref[pl.ds(pl.multiple_of(place_ref[s], MAXBF), MAXBF)]
        out_ref[s // 2, (s % 2) * MAXBF : (s % 2 + 1) * MAXBF] = rows


def gain_kernel(row_ref, count_ref, slot_ref, out_ref, sum_ref, turned_ref):
    groups, rows, _ = slot_ref.shape
    width, bas_dev = out_ref.shape
    half = width // 2
    u, v = iota((128, 128), 0), iota((128, 128), 1)
    turn = jnp.where((v < half) & (u == v + half), -1.0, 0.0)
    turn = jnp.where((v >= half) & (v < width) & (u == v - half), 1.0, turn).astype(jnp.bfloat16)
    turned = dot(slot_ref[...].reshape(groups * rows, 128), turn).astype(jnp.bfloat16)
    turned_ref[...] = turned.reshape(groups, rows, 128)
    sum_ref[...] = jnp.zeros(sum_ref.shape, jnp.float32)
    lane, row_id = iota((MAXBF, 128), 1), iota((MAXBF, 128), 0)
    for g in range(groups):
        slots = slot_ref[g]
        wide = slots.astype(jnp.float32)
        tiles = []
        for r in range(2):
            tile = wide[r * MAXBF : (r + 1) * MAXBF]
            real = jnp.where(lane // MAXBF == r, pltpu.roll(tile, 32 + 16 * r, 1), 0.0)
            imag = jnp.where(lane // MAXBF == 2 + r, pltpu.roll(tile, 48 + 16 * r, 1), 0.0)
            tiles.append(real + imag)
        tiles = jnp.concatenate(tiles, axis=0)[:, 0:64].astype(jnp.bfloat16)
        gains = dot(tiles, jnp.concatenate([slots, turned_ref[g]], axis=0))
        for r in range(2):
            part = gains[r * MAXBF : (r + 1) * MAXBF]
            part = jnp.where(row_id < count_ref[2 * g + r], part, 0.0)
            where = pl.ds(row_ref[2 * g + r], MAXBF)
            sum_ref[where] = sum_ref[where] + part
    out_ref[...] = sum_ref[0:bas_dev].T[0:width]


def vmem_spec():
    return pl.BlockSpec(memory_space=pltpu.VMEM)


def smem_spec():
    return pl.BlockSpec(memory_space=pltpu.SMEM)


def limit(mib):
    return pltpu.CompilerParams(vmem_limit_bytes=mib * MIB)


def in_hbm(array):
    return pltpu.with_memory_space_constraint(array, pltpu.HBM)


def stage(own, *fetched):
    shapes = [fetched[0].shape, own.shape, (2, 256, 256), (256, 256), (16, 128)]
    return pl.pallas_call(
        stage_kernel,
        in_specs=[vmem_spec()] + [pl.BlockSpec(memory_space=pltpu.HBM)] * len(fetched),
        out_specs=[vmem_spec()] * len(shapes),
        out_shape=[pltpu.VMEM(shape, jnp.bfloat16) for shape in shapes],
        scratch_shapes=[pltpu.VMEM(x.shape, x.dtype) for x in fetched[1:]]
        + [pltpu.VMEM((16, 128), jnp.float32), pltpu.SemaphoreType.DMA((len(fetched),))],
        compiler_params=limit(16),
        cost_estimate=pl.CostEstimate(flops=1 << 28, bytes_accessed=5 * MIB, transcendentals=0),
        name="stage",
    )(own, *[in_hbm(x) for x in fetched])


def fit(odd, near, far, window_rows, ints, order, mix, meta):
    aux_dev, bas_dev, window = ints.shape
    width = near.shape[1]
    blocks = bas_dev // ROWBLK
    shape = (4 * aux_dev, blocks * PACKED + 16, 128)
    return pl.pallas_call(
        fit_kernel,
        in_specs=[smem_spec()] + [vmem_spec()] * 7,
        out_specs=pl.BlockSpec(memory_space=pltpu.HBM),
        out_shape=pltpu.HBM(shape, jnp.bfloat16),
        scratch_shapes=[
            pltpu.VMEM((window, width), jnp.bfloat16),
            pltpu.VMEM(shape, jnp.bfloat16),
            pltpu.SemaphoreType.DMA((blocks // 2,)),
        ],
        compiler_params=limit(32),
        cost_estimate=pl.CostEstimate(
            flops=2 * aux_dev * bas_dev * width * (window + 256),
            bytes_accessed=6 * MIB,
            transcendentals=0,
        ),
        name="fit",
    )(odd, near, far, window_rows, ints, order, mix, meta)


def pair_sums(me, coef, got):
    groups = got.shape[0]
    rows = groups * (got.shape[1] // PACKED) * ROWBLK + MAXBF
    shape = (groups, 6 * MAXBF, 128)
    return pl.pallas_call(
        pair_kernel,
        in_specs=[smem_spec(), vmem_spec(), vmem_spec()],
        out_specs=[vmem_spec(), pl.BlockSpec(memory_space=pltpu.HBM)],
        out_shape=[
            jax.ShapeDtypeStruct((groups, 128), jnp.int32),
            pltpu.HBM(shape, jnp.bfloat16),
        ],
        scratch_shapes=[
            pltpu.VMEM((rows, 128), jnp.float32),
            pltpu.VMEM((rows, 128), jnp.float32),
            pltpu.VMEM((coef.shape[0] + MAXBF, 128), jnp.float32),
            pltpu.VMEM(shape, jnp.bfloat16),
            pltpu.VMEM((groups, 128), jnp.float32),
            pltpu.VMEM((groups, 128), jnp.float32),
            pltpu.VMEM((groups, 128), jnp.float32),
            pltpu.SMEM((groups, 128), jnp.int32),
            pltpu.SemaphoreType.DMA,
            pltpu.SemaphoreType.DMA((groups // BATCH,)),
        ]
        + [pltpu.VMEM((256, 256), jnp.bfloat16), pltpu.VMEM((128, 256), jnp.bfloat16)] * (2 * BATCH),
        compiler_params=limit(40),
        name="pair_sums",
    )(me, coef, got)


def make_slots(scale, targets, ranks, places, parts, got):
    def body(*refs):
        slot_kernel(scale, *refs)

    return pl.pallas_call(
        body,
        in_specs=[smem_spec()] * 3 + [vmem_spec()] * 2,
        out_specs=vmem_spec(),
        out_shape=jax.ShapeDtypeStruct((got.shape[0], 2 * MAXBF, 128), jnp.bfloat16),
        scratch_shapes=[pltpu.VMEM((528, 128), jnp.bfloat16)],
        compiler_params=limit(16),
        name="make_slots",
    )(targets, ranks, places, parts, got)


def add_gains(rows, counts, slots, width, bas_dev):
    return pl.pallas_call(
        gain_kernel,
        in_specs=[smem_spec()] * 2 + [vmem_spec()],
        out_specs=vmem_spec(),
        out_shape=jax.ShapeDtypeStruct((width, bas_dev), jnp.float32),
        scratch_shapes=[
            pltpu.VMEM((bas_dev + MAXBF, 128), jnp.float32),
            pltpu.VMEM(slots.shape, jnp.bfloat16),
        ],
        compiler_params=limit(16),
        name="add_gains",
    )(rows, counts, slots)


def pick(hit, values):
    return jnp.sum(jnp.where(hit, values, 0), axis=-1)


def per_device(integrals, coeffs, metric, atom_sizes, pair_device, pair_atom):
    aux_dev, bas_dev, window = integrals.shape
    occ = coeffs.shape[2]
    groups = lax.axis_size("atom")
    aux_count = lax.axis_size("aux")
    occ_part = occ // aux_count
    ref_count = pair_atom.shape[0]
    halo = (window - bas_dev) // 2
    scale = 1.0 / math.sqrt(2 * occ * aux_dev * aux_count * MAXBF)
    me = lax.axis_index("atom")

    own = coeffs.reshape(bas_dev, 2 * occ)
    odd = lax.axis_index("atom") % 2
    inner = range(1, groups - 1)
    far = lax.dynamic_slice_in_dim(own, odd * halo, halo, 0)
    far = lax.ppermute(far, "atom", [(i, i + 1 if i % 2 else i - 1) for i in inner])
    near = lax.dynamic_slice_in_dim(own, (1 - odd) * halo, halo, 0)
    near = lax.ppermute(near, "atom", [(i, i ^ 1) for i in range(groups)])

    ints, window_rows, order, mix, meta = stage(
        own, integrals, metric, atom_sizes, pair_device.T, pair_atom[None]
    )
    odd = jnp.full((1,), odd, jnp.int32)
    packed = fit(odd, near, far, window_rows, ints, order, mix, meta)
    got = lax.all_to_all(packed, "atom", split_axis=0, concat_axis=0, tiled=True)
    coef_part = lax.dynamic_slice_in_dim(
        coeffs, lax.axis_index("aux") * occ_part, occ_part, 2
    ).reshape(bas_dev, 2 * occ_part)
    me = jnp.full((1,), lax.axis_index("atom"), jnp.int32)

    targets = pair_device[:, 0]
    order = jnp.arange(ref_count, dtype=jnp.int32)
    earlier = (targets[:, None] == targets[None, :]) & (order[None, :] < order[:, None])
    ranks = jnp.sum(earlier.astype(jnp.int32), axis=1)
    asked = targets * 2 + ranks
    place = (order % 2) * 256 + (order // 2) * MAXBF
    asked_hit = asked[None, :] == jnp.arange(2 * groups, dtype=jnp.int32)[:, None]
    places = 512 + pick(asked_hit, place[None, :] - 512)

    table, sent = pair_sums(me, coef_part, got)
    owned = lax.all_to_all(sent, "atom", split_axis=0, concat_axis=0, tiled=True)
    own_sums = jnp.sum(owned[:, : 4 * MAXBF].astype(jnp.float32), axis=0).astype(jnp.bfloat16)
    shared = jnp.broadcast_to(own_sums[None], (aux_count,) + own_sums.shape)
    parts = lax.all_to_all(shared, "aux", split_axis=0, concat_axis=0, tiled=True)
    slots = make_slots(scale, targets, ranks, places, parts, owned)
    slots = lax.all_to_all(slots, "atom", split_axis=0, concat_axis=0, tiled=True)
    rows, counts = table[:, 32:34].reshape(-1), table[:, 34:36].reshape(-1)
    result = add_gains(rows, counts, slots, 2 * occ_part, bas_dev)
    return result.reshape(2, occ_part, bas_dev).transpose(2, 0, 1)


def solution(mesh):
    placed = (
        P("aux", "atom", None),
        P("atom", None, None),
        P("aux", None),
        P("atom", None),
        P("atom", None),
        P("atom"),
    )
    return jax.shard_map(
        per_device, mesh=mesh, in_specs=placed, out_specs=P("atom", None, "aux"), check_vma=False
    )
```

```python
import math

import jax
import jax.numpy as jnp
from jax import lax
from jax.experimental import pallas as pl
from jax.experimental.pallas import tpu as pltpu
from jax.sharding import PartitionSpec as P

MAXBF = 16
ROWBLK = 32
WORDS = ROWBLK * 3 // 4
BATCH = 16
MIB = 1 << 20


def iota(shape, dim):
    return lax.broadcasted_iota(jnp.int32, shape, dim)


def dot(a, b):
    return jnp.dot(a, b, preferred_element_type=jnp.float32)


def dot_nt(a, b):
    return lax.dot_general(a, b, (((1,), (1,)), ((), ())), preferred_element_type=jnp.float32)


def dot_tn(a, b):
    return lax.dot_general(a, b, (((0,), (0,)), ((), ())), preferred_element_type=jnp.float32)


def ordered(part_ref, order_ref, window_ref, at):
    rows = part_ref.shape[0]
    half = part_ref.shape[1] // 2
    for t in range(3):
        real = part_ref[:, t * 128 : (t + 1) * 128]
        imag = part_ref[:, half + t * 128 : half + (t + 1) * 128]
        value = dot(jnp.concatenate([real, imag], axis=1), order_ref[t // 2])
        place = pl.ds(at if isinstance(at, int) else pl.multiple_of(at, 128), rows)
        window_ref[place, t * 256 : (t + 1) * 256] = value.astype(jnp.bfloat16)


def stage_kernel(
    own_ref, ints_hbm, metric_hbm, size_hbm, dev_hbm, atom_hbm,
    ints_ref, window_ref, order_ref, mix_ref, meta_ref,
    metric_ref, size_ref, dev_ref, atom_ref, sem_ref,
):
    sources = (ints_hbm, metric_hbm, size_hbm, dev_hbm, atom_hbm)
    targets = (ints_ref, metric_ref, size_ref, dev_ref, atom_ref)
    fetches = [
        pltpu.make_async_copy(a, b, sem_ref.at[i]) for i, (a, b) in enumerate(zip(sources, targets))
    ]
    for fetch in fetches:
        fetch.start()
    u, v = iota((256, 256), 0), iota((256, 256), 1)
    main_order = u == ((v % 128) // 64) * 128 + (v // 128) * 64 + v % 64
    side_order = u == ((v % 64) // 32) * 128 + (v // 64) * 32 + v % 32
    order_ref[0] = jnp.where(main_order, 1.0, 0.0).astype(jnp.bfloat16)
    order_ref[1] = jnp.where(side_order, 1.0, 0.0).astype(jnp.bfloat16)
    ordered(own_ref, order_ref, window_ref, 0)
    for fetch in fetches[1:]:
        fetch.wait()
    member = iota((256, 8), 0) // ROWBLK == iota((256, 8), 1)
    member = jnp.where(member, 1.0, 0.0).astype(jnp.bfloat16)
    mix = dot_nt(dot_nt(member, metric_ref[...]).astype(jnp.bfloat16), member)
    mix_ref[...] = jnp.where(u % ROWBLK == v % ROWBLK, mix, 0.0).astype(jnp.bfloat16)
    meta_ref[...] = jnp.zeros(meta_ref.shape, jnp.int32)
    for row, value_ref in enumerate((size_ref, dev_ref, atom_ref)):
        meta_ref[row + 2 : row + 3, 0 : value_ref.shape[1]] = value_ref[...]
    fetches[0].wait()


def join(high, low):
    return (high << 16) + low


def split(words):
    high = (words + 32768) >> 16
    low = (words << 16) >> 16
    return high.astype(jnp.float32), low.astype(jnp.float32)


def fit_kernel(
    odd_ref, near_ref, far_ref, own_ref, ints_ref, order_ref, mix_ref, meta_ref, out_ref,
    window_ref, packed_ref, power_ref, out_sem,
):
    aux_dev, bas_dev, span = ints_ref.shape
    blocks = bas_dev // ROWBLK
    halo = near_ref.shape[0]
    far_at = odd_ref[0] * (halo + bas_dev)
    ordered(near_ref, order_ref, window_ref, halo + bas_dev - far_at)
    window_ref[halo : halo + bas_dev] = own_ref[...]
    ordered(far_ref, order_ref, window_ref, far_at)
    mix = mix_ref[...]
    left = iota((ROWBLK // 2, 128), 1) < 64
    power_ref[...] = jnp.zeros(power_ref.shape, jnp.float32)
    spot = iota((aux_dev * ROWBLK, 128), 1) - iota((aux_dev * ROWBLK, 128), 0) % ROWBLK
    copies = []

    def whole(values):
        return jnp.round(values).astype(jnp.int32)

    for u in range(blocks):
        if u % 4 == 0:
            ints = ints_ref[:, u * ROWBLK : (u + 4) * ROWBLK].reshape(-1, span)
            wide = dot(ints, window_ref[...]).astype(jnp.bfloat16)
            wide = wide.reshape(aux_dev, 4 * ROWBLK, -1)
        at = (u % 4) * ROWBLK
        half = wide[:, at : at + ROWBLK].reshape(aux_dev * ROWBLK, -1)
        fitted = dot(mix, half)
        largest = jnp.abs(fitted[:, 0:128])
        for t in range(1, 6):
            largest = jnp.maximum(largest, jnp.abs(fitted[:, t * 128 : (t + 1) * 128]))
        largest = jnp.maximum(jnp.max(largest, axis=1, keepdims=True), 1e-30)
        power = jnp.floor(jnp.log2(largest) + 1.5e-4) - 14.0
        fitted = fitted * jnp.exp2(-power)
        powers = jnp.where(spot == at, jnp.broadcast_to(power, spot.shape), 0.0)
        for p in range(aux_dev):
            row = 2 * p + u // 4
            mine = jnp.sum(powers[p * ROWBLK : (p + 1) * ROWBLK], axis=0, keepdims=True)
            power_ref[row : row + 1] = power_ref[row : row + 1] + mine
        for p in range(aux_dev):
            rows = fitted[p * ROWBLK : (p + 1) * ROWBLK]
            top, bottom = rows[: ROWBLK // 2], rows[ROWBLK // 2 :]
            main = join(whole(top[:, 0:512]), whole(bottom[:, 0:512]))
            first = u * WORDS
            for k in range(4):
                packed_ref[p * 4 + k, first : first + 16] = main[:, k * 128 : (k + 1) * 128]
            for k in range(2):
                lanes = slice(512 + k * 128, 640 + k * 128)
                even = jnp.where(left, top[:, lanes], pltpu.roll(bottom[:, lanes], 64, 1))
                odd = jnp.where(left, pltpu.roll(top[:, lanes], 64, 1), bottom[:, lanes])
                for d, side in ((2 * k, whole(even)), (2 * k + 1, whole(odd))):
                    packed_ref[p * 4 + d, first + 16 : first + 24] = join(side[0:8], side[8:16])
        if u == blocks - 1:
            row = iota((8, 128), 0)
            for p in range(aux_dev):
                tail = meta_ref[...]
                for i in range(2):
                    power = power_ref[2 * p + i : 2 * p + i + 1].astype(jnp.int32)
                    tail = jnp.where(row == i, jnp.broadcast_to(power, tail.shape), tail)
                for k in range(4):
                    packed_ref[p * 4 + k, blocks * WORDS : blocks * WORDS + 8] = tail
        if u % 2 == 1:
            span_rows = pl.ds((u - 1) * WORDS, 2 * WORDS + (8 if u == blocks - 1 else 0))
            copies.append(
                pltpu.make_async_copy(
                    packed_ref.at[:, span_rows], out_ref.at[:, span_rows], out_sem.at[u // 2]
                )
            )
            copies[-1].start()
    for copy in copies:
        copy.wait()


def end_table(me, got_ref, size_ref, dev_ref, atom_ref):
    groups, at = got_ref.shape[0], got_ref.shape[1] - 8
    for d in range(groups):
        rows = got_ref[d, at : at + 8].astype(jnp.float32)
        for i, dest in enumerate((size_ref, dev_ref, atom_ref)):
            dest[d : d + 1] = rows[i + 2 : i + 3]
    before = jnp.where(iota((128, 128), 0) < iota((128, 128), 1), 1.0, 0.0).astype(jnp.bfloat16)
    sizes = size_ref[...]
    packed = dot(sizes.astype(jnp.bfloat16), before) * 32.0 + sizes
    devices = dev_ref[...].astype(jnp.int32)
    atoms = atom_ref[...].astype(jnp.int32)
    found = jnp.zeros(packed.shape, jnp.float32)
    for d in range(groups):
        row = jnp.broadcast_to(packed[d : d + 1], packed.shape)
        found = jnp.where(devices == d, jnp.take_along_axis(row, atoms, axis=1), found)
    found = found.astype(jnp.int32)
    starts, counts = found // 32, found % 32
    lane = iota(found.shape, 1)
    here = (devices == me) & (lane < 32)
    rank = dot(jnp.where(here, 1.0, 0.0).astype(jnp.bfloat16), before)
    table = jnp.where(lane < 32, devices * 256 + starts, 0)
    for i, value in enumerate((starts, counts)):
        value = value.astype(jnp.float32)
        for r in range(2):
            one = jnp.sum(jnp.where(here & (rank == r), value, 0.0), axis=1, keepdims=True)
            table = jnp.where(lane == 32 + 2 * i + r, one.astype(jnp.int32), table)
    return table


def pair_kernel(
    me_ref, coef_ref, got_ref, table_ref, out_ref, real_ref, imag_ref, rows_ref, sums_ref,
    size_ref, dev_ref, atom_ref, row_ref, table_sem, sem_ref, *sides,
):
    table_ref[...] = end_table(me_ref[0], got_ref, size_ref, dev_ref, atom_ref)
    fetch = pltpu.make_async_copy(table_ref, row_ref, table_sem)
    fetch.start()
    groups, blocks = got_ref.shape[0], got_ref.shape[1] // WORDS
    lane = iota((ROWBLK // 2, 128), 1)
    left, valid = lane < 64, lane < 96

    row = iota((16, 256), 0)
    spread = jnp.where(row == iota((16, 256), 1) // 128, 1.0, 0.0).astype(jnp.bfloat16)
    row = iota((8, 128), 0)

    def unpack(b, carry):
        powers = got_ref[b, blocks * WORDS : blocks * WORDS + 8]
        powers = jnp.exp2(jnp.where(row < 2, powers, 0).astype(jnp.float32))
        powers = jnp.concatenate([powers, jnp.zeros((8, 128), jnp.float32)], axis=0)
        scales = dot_tn(powers.astype(jnp.bfloat16), spread)
        for i in range(blocks):
            base = pl.multiple_of(b * (blocks * ROWBLK) + i * ROWBLK, ROWBLK)
            mains = split(got_ref[b, i * WORDS : i * WORDS + 16])
            shared = split(got_ref[b, i * WORDS + 16 : (i + 1) * WORDS])
            shared = jnp.concatenate(shared, axis=0)
            for h in range(2):
                main = mains[h]
                at = (i % 4) * ROWBLK + h * 16
                scale = scales[at : at + 16, (i // 4) * 128 : (i // 4 + 1) * 128]
                real = shared if h else pltpu.roll(shared, 64, 1)
                imag = pltpu.roll(shared, 96 if h else 32, 1)
                real = jnp.where(left, main, jnp.where(valid, real, 0.0))
                imag = jnp.where(left, pltpu.roll(main, 64, 1), jnp.where(valid, imag, 0.0))
                real_ref[pl.ds(base + h * 16, 16)] = real * scale
                imag_ref[pl.ds(base + h * 16, 16)] = imag * scale
        return carry

    lax.fori_loop(0, groups, unpack, 0, unroll=8)
    tail = groups * blocks * ROWBLK
    real_ref[tail : tail + MAXBF] = jnp.zeros((MAXBF, 128), jnp.float32)
    imag_ref[tail : tail + MAXBF] = jnp.zeros((MAXBF, 128), jnp.float32)
    bas_dev, width = coef_ref.shape
    rows_ref[...] = jnp.zeros(rows_ref.shape, jnp.float32)
    rows_ref[0:bas_dev, 0:width] = coef_ref[...].astype(jnp.float32)
    row_id = iota((MAXBF, 128), 0)
    lane_pair = lane // MAXBF
    batch = len(sides) // 4
    fetch.wait()

    def group(step, carry):
        for u in range(batch):
            g = step * batch + u
            for h in range(2):
                first_ref, second_ref = sides[u * 4 + h * 2], sides[u * 4 + h * 2 + 1]
                for j in range(16):
                    row = pl.ds(row_ref[g, h * 16 + j], 16)
                    place = (j // 2) * MAXBF
                    real, imag = real_ref[row], imag_ref[row]
                    if j % 2:
                        second_ref[place : place + 16, 0:128] = real.astype(jnp.bfloat16)
                        second_ref[place : place + 16, 128:256] = imag.astype(jnp.bfloat16)
                    else:
                        first_ref[place : place + 16, 0:128] = real.astype(jnp.bfloat16)
                        first_ref[place : place + 16, 128:256] = imag.astype(jnp.bfloat16)
                        place += 128
                        first_ref[place : place + 16, 0:128] = imag.astype(jnp.bfloat16)
                        first_ref[place : place + 16, 128:256] = (-real).astype(jnp.bfloat16)
                value = dot_nt(first_ref[...], second_ref[...])
                for c in range(2):
                    part = value[c * 128 : c * 128 + 16]
                    for j in range(1, 8):
                        here = value[c * 128 + j * 16 : c * 128 + j * 16 + 16]
                        part = jnp.where(lane_pair == j, here, part)
                    at = h * 32 + c * 16
                    sums_ref[g, at : at + 16] = part.astype(jnp.bfloat16)
                rows = rows_ref[pl.ds(row_ref[g, 32 + h], MAXBF)]
                rows = jnp.where(row_id < row_ref[g, 34 + h], rows, 0.0)
                sums_ref[g, 64 + h * 16 : 80 + h * 16] = rows.astype(jnp.bfloat16)
        send(step).start()
        return carry

    def send(step):
        done = pl.ds(step * batch, batch)
        return pltpu.make_async_copy(sums_ref.at[done], out_ref.at[done], sem_ref.at[step])

    lax.fori_loop(0, groups // batch, group, 0)
    for step in range(groups // batch):
        send(step).wait()


def slot_kernel(scale, target_ref, rank_ref, place_ref, parts_ref, got_ref, out_ref, tile_ref):
    total = parts_ref[0].astype(jnp.float32)
    for z in range(1, parts_ref.shape[0]):
        total = total + parts_ref[z].astype(jnp.float32)
    kernel = (total * scale).astype(jnp.bfloat16)
    u, v = iota((128, 128), 0), iota((128, 128), 1)
    same = u // MAXBF == v // MAXBF
    folds = [jnp.where(v == 96 + c * 16 + u % 16, 1.0, 0.0).astype(jnp.bfloat16) for c in range(2)]
    u, v = iota((32, 128), 0), iota((32, 128), 1)
    turned = jnp.where(v == 96 + u, jnp.where(u < MAXBF, 1.0, -1.0), 0.0).astype(jnp.bfloat16)

    def coef(e):
        at = pl.multiple_of(64 + rank_ref[e] * MAXBF, MAXBF)
        return got_ref[target_ref[e], pl.ds(at, MAXBF)]

    for h in range(2):
        block = kernel[h * 32 : (h + 1) * 32]
        first = jnp.zeros((128, 128), jnp.float32)
        for c in range(2):
            tile = block[c * MAXBF : (c + 1) * MAXBF].astype(jnp.float32)
            wide = jnp.where(same, jnp.concatenate([tile] * 8, axis=0), 0.0)
            first = first + dot(wide.astype(jnp.bfloat16), folds[c])
        first = first.astype(jnp.bfloat16)
        second = dot_tn(block, turned).astype(jnp.bfloat16)
        for j in range(8):
            pair, rows = h * 8 + j, slice(j * MAXBF, (j + 1) * MAXBF)
            at = pair * MAXBF
            tile_ref[at : at + MAXBF] = first[rows] + coef(2 * pair + 1)
            tile_ref[256 + at : 256 + at + MAXBF] = second[rows] + coef(2 * pair)
    tile_ref[512:528] = jnp.zeros((MAXBF, 128), jnp.bfloat16)
    for s in range(2 * out_ref.shape[0]):
        rows = tile_ref[pl.ds(pl.multiple_of(place_ref[s], MAXBF), MAXBF)]
        out_ref[s // 2, (s % 2) * MAXBF : (s % 2 + 1) * MAXBF] = rows


def gain_kernel(row_ref, count_ref, slot_ref, out_ref, sum_ref, turned_ref):
    groups, rows, _ = slot_ref.shape
    width, bas_dev = out_ref.shape
    half = width // 2
    u, v = iota((128, 128), 0), iota((128, 128), 1)
    turn = jnp.where((v < half) & (u == v + half), -1.0, 0.0)
    turn = jnp.where((v >= half) & (v < width) & (u == v - half), 1.0, turn).astype(jnp.bfloat16)
    turned = dot(slot_ref[...].reshape(groups * rows, 128), turn).astype(jnp.bfloat16)
    turned_ref[...] = turned.reshape(groups, rows, 128)
    sum_ref[...] = jnp.zeros(sum_ref.shape, jnp.float32)
    lane, row_id = iota((MAXBF, 128), 1), iota((MAXBF, 128), 0)
    for g in range(groups):
        slots = slot_ref[g]
        wide = slots.astype(jnp.float32)
        tiles = []
        for r in range(2):
            tile = wide[r * MAXBF : (r + 1) * MAXBF]
            real = jnp.where(lane // MAXBF == r, pltpu.roll(tile, 32 + 16 * r, 1), 0.0)
            imag = jnp.where(lane // MAXBF == 2 + r, pltpu.roll(tile, 48 + 16 * r, 1), 0.0)
            tiles.append(real + imag)
        tiles = jnp.concatenate(tiles, axis=0)[:, 0:64].astype(jnp.bfloat16)
        gains = dot(tiles, jnp.concatenate([slots, turned_ref[g]], axis=0))
        for r in range(2):
            part = gains[r * MAXBF : (r + 1) * MAXBF]
            part = jnp.where(row_id < count_ref[2 * g + r], part, 0.0)
            where = pl.ds(row_ref[2 * g + r], MAXBF)
            sum_ref[where] = sum_ref[where] + part
    out_ref[...] = sum_ref[0:bas_dev].T[0:width]


def vmem_spec():
    return pl.BlockSpec(memory_space=pltpu.VMEM)


def smem_spec():
    return pl.BlockSpec(memory_space=pltpu.SMEM)


def limit(mib):
    return pltpu.CompilerParams(vmem_limit_bytes=mib * MIB)


def in_hbm(array):
    return pltpu.with_memory_space_constraint(array, pltpu.HBM)


def stage(own, *fetched):
    shapes = [fetched[0].shape, own.shape, (2, 256, 256), (256, 256)]
    return pl.pallas_call(
        stage_kernel,
        in_specs=[vmem_spec()] + [pl.BlockSpec(memory_space=pltpu.HBM)] * len(fetched),
        out_specs=[vmem_spec()] * 5,
        out_shape=[pltpu.VMEM(shape, jnp.bfloat16) for shape in shapes]
        + [pltpu.VMEM((8, 128), jnp.int32)],
        scratch_shapes=[pltpu.VMEM(x.shape, x.dtype) for x in fetched[1:]]
        + [pltpu.SemaphoreType.DMA((len(fetched),))],
        compiler_params=limit(16),
        cost_estimate=pl.CostEstimate(flops=1 << 28, bytes_accessed=5 * MIB, transcendentals=0),
        name="stage",
    )(own, *[in_hbm(x) for x in fetched])


def fit(odd, near, far, window_rows, ints, order, mix, meta):
    aux_dev, bas_dev, window = ints.shape
    width = near.shape[1]
    blocks = bas_dev // ROWBLK
    shape = (4 * aux_dev, blocks * WORDS + 8, 128)
    return pl.pallas_call(
        fit_kernel,
        in_specs=[smem_spec()] + [vmem_spec()] * 7,
        out_specs=pl.BlockSpec(memory_space=pltpu.HBM),
        out_shape=pltpu.HBM(shape, jnp.int32),
        scratch_shapes=[
            pltpu.VMEM((window, width), jnp.bfloat16),
            pltpu.VMEM(shape, jnp.int32),
            pltpu.VMEM((2 * aux_dev, 128), jnp.float32),
            pltpu.SemaphoreType.DMA((blocks // 2,)),
        ],
        compiler_params=limit(32),
        cost_estimate=pl.CostEstimate(
            flops=2 * aux_dev * bas_dev * width * (window + 256),
            bytes_accessed=6 * MIB,
            transcendentals=0,
        ),
        name="fit",
    )(odd, near, far, window_rows, ints, order, mix, meta)


def pair_sums(me, coef, got):
    groups = got.shape[0]
    rows = groups * (got.shape[1] // WORDS) * ROWBLK + MAXBF
    shape = (groups, 6 * MAXBF, 128)
    return pl.pallas_call(
        pair_kernel,
        in_specs=[smem_spec(), vmem_spec(), vmem_spec()],
        out_specs=[vmem_spec(), pl.BlockSpec(memory_space=pltpu.HBM)],
        out_shape=[
            jax.ShapeDtypeStruct((groups, 128), jnp.int32),
            pltpu.HBM(shape, jnp.bfloat16),
        ],
        scratch_shapes=[
            pltpu.VMEM((rows, 128), jnp.float32),
            pltpu.VMEM((rows, 128), jnp.float32),
            pltpu.VMEM((coef.shape[0] + MAXBF, 128), jnp.float32),
            pltpu.VMEM(shape, jnp.bfloat16),
            pltpu.VMEM((groups, 128), jnp.float32),
            pltpu.VMEM((groups, 128), jnp.float32),
            pltpu.VMEM((groups, 128), jnp.float32),
            pltpu.SMEM((groups, 128), jnp.int32),
            pltpu.SemaphoreType.DMA,
            pltpu.SemaphoreType.DMA((groups // BATCH,)),
        ]
        + [pltpu.VMEM((256, 256), jnp.bfloat16), pltpu.VMEM((128, 256), jnp.bfloat16)] * (2 * BATCH),
        compiler_params=limit(40),
        name="pair_sums",
    )(me, coef, got)


def make_slots(scale, targets, ranks, places, parts, got):
    def body(*refs):
        slot_kernel(scale, *refs)

    return pl.pallas_call(
        body,
        in_specs=[smem_spec()] * 3 + [vmem_spec()] * 2,
        out_specs=vmem_spec(),
        out_shape=jax.ShapeDtypeStruct((got.shape[0], 2 * MAXBF, 128), jnp.bfloat16),
        scratch_shapes=[pltpu.VMEM((528, 128), jnp.bfloat16)],
        compiler_params=limit(16),
        name="make_slots",
    )(targets, ranks, places, parts, got)


def add_gains(rows, counts, slots, width, bas_dev):
    return pl.pallas_call(
        gain_kernel,
        in_specs=[smem_spec()] * 2 + [vmem_spec()],
        out_specs=vmem_spec(),
        out_shape=jax.ShapeDtypeStruct((width, bas_dev), jnp.float32),
        scratch_shapes=[
            pltpu.VMEM((bas_dev + MAXBF, 128), jnp.float32),
            pltpu.VMEM(slots.shape, jnp.bfloat16),
        ],
        compiler_params=limit(16),
        name="add_gains",
    )(rows, counts, slots)


def pick(hit, values):
    return jnp.sum(jnp.where(hit, values, 0), axis=-1)


def per_device(integrals, coeffs, metric, atom_sizes, pair_device, pair_atom):
    aux_dev, bas_dev, window = integrals.shape
    occ = coeffs.shape[2]
    groups = lax.axis_size("atom")
    aux_count = lax.axis_size("aux")
    occ_part = occ // aux_count
    ref_count = pair_atom.shape[0]
    halo = (window - bas_dev) // 2
    scale = 1.0 / math.sqrt(2 * occ * aux_dev * aux_count * MAXBF)
    me = lax.axis_index("atom")

    own = coeffs.reshape(bas_dev, 2 * occ)
    odd = lax.axis_index("atom") % 2
    inner = range(1, groups - 1)
    far = lax.dynamic_slice_in_dim(own, odd * halo, halo, 0)
    far = lax.ppermute(far, "atom", [(i, i + 1 if i % 2 else i - 1) for i in inner])
    near = lax.dynamic_slice_in_dim(own, (1 - odd) * halo, halo, 0)
    near = lax.ppermute(near, "atom", [(i, i ^ 1) for i in range(groups)])

    ints, window_rows, order, mix, meta = stage(
        own, integrals, metric, atom_sizes, pair_device.T, pair_atom[None]
    )
    odd = jnp.full((1,), odd, jnp.int32)
    packed = fit(odd, near, far, window_rows, ints, order, mix, meta)
    got = lax.all_to_all(packed, "atom", split_axis=0, concat_axis=0, tiled=True)
    coef_part = lax.dynamic_slice_in_dim(
        coeffs, lax.axis_index("aux") * occ_part, occ_part, 2
    ).reshape(bas_dev, 2 * occ_part)
    me = jnp.full((1,), lax.axis_index("atom"), jnp.int32)

    targets = pair_device[:, 0]
    order = jnp.arange(ref_count, dtype=jnp.int32)
    earlier = (targets[:, None] == targets[None, :]) & (order[None, :] < order[:, None])
    ranks = jnp.sum(earlier.astype(jnp.int32), axis=1)
    asked = targets * 2 + ranks
    place = (order % 2) * 256 + (order // 2) * MAXBF
    asked_hit = asked[None, :] == jnp.arange(2 * groups, dtype=jnp.int32)[:, None]
    places = 512 + pick(asked_hit, place[None, :] - 512)

    table, sent = pair_sums(me, coef_part, got)
    owned = lax.all_to_all(sent, "atom", split_axis=0, concat_axis=0, tiled=True)
    own_sums = jnp.sum(owned[:, : 4 * MAXBF].astype(jnp.float32), axis=0).astype(jnp.bfloat16)
    shared = jnp.broadcast_to(own_sums[None], (aux_count,) + own_sums.shape)
    parts = lax.all_to_all(shared, "aux", split_axis=0, concat_axis=0, tiled=True)
    slots = make_slots(scale, targets, ranks, places, parts, owned)
    slots = lax.all_to_all(slots, "atom", split_axis=0, concat_axis=0, tiled=True)
    rows, counts = table[:, 32:34].reshape(-1), table[:, 34:36].reshape(-1)
    result = add_gains(rows, counts, slots, 2 * occ_part, bas_dev)
    return result.reshape(2, occ_part, bas_dev).transpose(2, 0, 1)


def solution(mesh):
    placed = (
        P("aux", "atom", None),
        P("atom", None, None),
        P("aux", None),
        P("atom", None),
        P("atom", None),
        P("atom"),
    )
    return jax.shard_map(
        per_device, mesh=mesh, in_specs=placed, out_specs=P("atom", None, "aux"), check_vma=False
    )
```

```python
import math

import jax
import jax.numpy as jnp
from jax import lax
from jax.experimental import pallas as pl
from jax.experimental.pallas import tpu as pltpu
from jax.sharding import PartitionSpec as P

MAXBF = 16
ROWBLK = 32
PACKED = ROWBLK + ROWBLK // 2
BATCH = 16
MIB = 1 << 20


def iota(shape, dim):
    return lax.broadcasted_iota(jnp.int32, shape, dim)


def dot(a, b):
    return jnp.dot(a, b, preferred_element_type=jnp.float32)


def dot_nt(a, b):
    return lax.dot_general(a, b, (((1,), (1,)), ((), ())), preferred_element_type=jnp.float32)


def dot_tn(a, b):
    return lax.dot_general(a, b, (((0,), (0,)), ((), ())), preferred_element_type=jnp.float32)


def ordered(part_ref, order_ref, window_ref, at):
    rows = part_ref.shape[0]
    half = part_ref.shape[1] // 2
    for t in range(3):
        real = part_ref[:, t * 128 : (t + 1) * 128]
        imag = part_ref[:, half + t * 128 : half + (t + 1) * 128]
        value = dot(jnp.concatenate([real, imag], axis=1), order_ref[t // 2])
        place = pl.ds(at if isinstance(at, int) else pl.multiple_of(at, 128), rows)
        window_ref[place, t * 256 : (t + 1) * 256] = value.astype(jnp.bfloat16)


def stage_kernel(
    own_ref, ints_hbm, metric_hbm, size_hbm, dev_hbm, atom_hbm,
    ints_ref, window_ref, order_ref, mix_ref, meta_ref,
    metric_ref, size_ref, dev_ref, atom_ref, rows_ref, sem_ref,
):
    sources = (ints_hbm, metric_hbm, size_hbm, dev_hbm, atom_hbm)
    targets = (ints_ref, metric_ref, size_ref, dev_ref, atom_ref)
    fetches = [
        pltpu.make_async_copy(a, b, sem_ref.at[i]) for i, (a, b) in enumerate(zip(sources, targets))
    ]
    for fetch in fetches:
        fetch.start()
    u, v = iota((256, 256), 0), iota((256, 256), 1)
    main_order = u == ((v % 128) // 64) * 128 + (v // 128) * 64 + v % 64
    side_order = u == ((v % 64) // 32) * 128 + (v // 64) * 32 + v % 32
    order_ref[0] = jnp.where(main_order, 1.0, 0.0).astype(jnp.bfloat16)
    order_ref[1] = jnp.where(side_order, 1.0, 0.0).astype(jnp.bfloat16)
    ordered(own_ref, order_ref, window_ref, 0)
    for fetch in fetches[1:]:
        fetch.wait()
    member = iota((256, 8), 0) // ROWBLK == iota((256, 8), 1)
    member = jnp.where(member, 1.0, 0.0).astype(jnp.bfloat16)
    mix = dot_nt(dot_nt(member, metric_ref[...]).astype(jnp.bfloat16), member)
    mix_ref[...] = jnp.where(u % ROWBLK == v % ROWBLK, mix, 0.0).astype(jnp.bfloat16)
    rows_ref[...] = jnp.zeros(rows_ref.shape, jnp.float32)
    for row, value_ref in enumerate((size_ref, dev_ref, atom_ref)):
        rows_ref[row : row + 1, 0 : value_ref.shape[1]] = value_ref[...].astype(jnp.float32)
    meta_ref[...] = rows_ref[...].astype(jnp.bfloat16)
    fetches[0].wait()


def fit_kernel(
    odd_ref, near_ref, far_ref, own_ref, ints_ref, order_ref, mix_ref, meta_ref, out_ref,
    window_ref, packed_ref, out_sem,
):
    aux_dev, bas_dev, span = ints_ref.shape
    blocks = bas_dev // ROWBLK
    halo = near_ref.shape[0]
    far_at = odd_ref[0] * (halo + bas_dev)
    ordered(near_ref, order_ref, window_ref, halo + bas_dev - far_at)
    window_ref[halo : halo + bas_dev] = own_ref[...]
    ordered(far_ref, order_ref, window_ref, far_at)
    mix = mix_ref[...]
    left = iota((ROWBLK // 2, 128), 1) < 64
    copies = []
    for u in range(blocks):
        if u % 4 == 0:
            ints = ints_ref[:, u * ROWBLK : (u + 4) * ROWBLK].reshape(-1, span)
            wide = dot(ints, window_ref[...]).astype(jnp.bfloat16)
            wide = wide.reshape(aux_dev, 4 * ROWBLK, -1)
        at = (u % 4) * ROWBLK
        half = wide[:, at : at + ROWBLK].reshape(aux_dev * ROWBLK, -1)
        fitted = dot(mix, half)
        main = slice(u * PACKED, u * PACKED + ROWBLK)
        side = slice(u * PACKED + ROWBLK, (u + 1) * PACKED)
        for p in range(aux_dev):
            rows = fitted[p * ROWBLK : (p + 1) * ROWBLK]
            for k in range(4):
                tile = rows[:, k * 128 : (k + 1) * 128]
                packed_ref[p * 4 + k, main] = tile.astype(jnp.bfloat16)
            for k in range(2):
                shared = rows[:, 512 + k * 128 : 640 + k * 128]
                top, bottom = shared[: ROWBLK // 2], shared[ROWBLK // 2 :]
                even = jnp.where(left, top, pltpu.roll(bottom, 64, 1))
                odd = jnp.where(left, pltpu.roll(top, 64, 1), bottom)
                packed_ref[p * 4 + 2 * k, side] = even.astype(jnp.bfloat16)
                packed_ref[p * 4 + 2 * k + 1, side] = odd.astype(jnp.bfloat16)
        if u == blocks - 1:
            for d in range(4 * aux_dev):
                packed_ref[d, blocks * PACKED : blocks * PACKED + 16] = meta_ref[...]
        if u % 2 == 1:
            first = (u - 1) * PACKED
            span_rows = pl.ds(first, 2 * PACKED + (16 if u == blocks - 1 else 0))
            copies.append(
                pltpu.make_async_copy(
                    packed_ref.at[:, span_rows], out_ref.at[:, span_rows], out_sem.at[u // 2]
                )
            )
            copies[-1].start()
    for copy in copies:
        copy.wait()


def end_table(me, got_ref, size_ref, dev_ref, atom_ref):
    groups, at = got_ref.shape[0], got_ref.shape[1] - 16
    for d in range(groups):
        rows = got_ref[d, at : at + 16].astype(jnp.float32)
        for i, dest in enumerate((size_ref, dev_ref, atom_ref)):
            dest[d : d + 1] = rows[i : i + 1]
    before = jnp.where(iota((128, 128), 0) < iota((128, 128), 1), 1.0, 0.0).astype(jnp.bfloat16)
    sizes = size_ref[...]
    packed = dot(sizes.astype(jnp.bfloat16), before) * 32.0 + sizes
    devices = dev_ref[...].astype(jnp.int32)
    atoms = atom_ref[...].astype(jnp.int32)
    found = jnp.zeros(packed.shape, jnp.float32)
    for d in range(groups):
        row = jnp.broadcast_to(packed[d : d + 1], packed.shape)
        found = jnp.where(devices == d, jnp.take_along_axis(row, atoms, axis=1), found)
    found = found.astype(jnp.int32)
    starts, counts = found // 32, found % 32
    lane = iota(found.shape, 1)
    here = (devices == me) & (lane < 32)
    rank = dot(jnp.where(here, 1.0, 0.0).astype(jnp.bfloat16), before)
    table = jnp.where(lane < 32, devices * 256 + starts, 0)
    for i, value in enumerate((starts, counts)):
        value = value.astype(jnp.float32)
        for r in range(2):
            one = jnp.sum(jnp.where(here & (rank == r), value, 0.0), axis=1, keepdims=True)
            table = jnp.where(lane == 32 + 2 * i + r, one.astype(jnp.int32), table)
    return table


def pair_kernel(
    me_ref, coef_ref, got_ref, table_ref, out_ref, real_ref, imag_ref, rows_ref,
    size_ref, dev_ref, atom_ref, row_ref, table_sem, *sides,
):
    table_ref[...] = end_table(me_ref[0], got_ref, size_ref, dev_ref, atom_ref)
    fetch = pltpu.make_async_copy(table_ref, row_ref, table_sem)
    fetch.start()
    groups, blocks = got_ref.shape[0], got_ref.shape[1] // PACKED
    lane = iota((ROWBLK // 2, 128), 1)
    left, valid = lane < 64, lane < 96

    def unpack(b, carry):
        for i in range(blocks):
            base = pl.multiple_of(b * (blocks * ROWBLK) + i * ROWBLK, ROWBLK)
            shared = got_ref[b, i * PACKED + ROWBLK : (i + 1) * PACKED].astype(jnp.float32)
            for h in range(2):
                at = i * PACKED + h * 16
                main = got_ref[b, at : at + 16].astype(jnp.float32)
                real = shared if h else pltpu.roll(shared, 64, 1)
                imag = pltpu.roll(shared, 96 if h else 32, 1)
                real = jnp.where(left, main, jnp.where(valid, real, 0.0))
                imag = jnp.where(left, pltpu.roll(main, 64, 1), jnp.where(valid, imag, 0.0))
                real_ref[pl.ds(base + h * 16, 16)] = real
                imag_ref[pl.ds(base + h * 16, 16)] = imag
        return carry

    lax.fori_loop(0, groups, unpack, 0, unroll=8)
    tail = groups * blocks * ROWBLK
    real_ref[tail : tail + MAXBF] = jnp.zeros((MAXBF, 128), jnp.float32)
    imag_ref[tail : tail + MAXBF] = jnp.zeros((MAXBF, 128), jnp.float32)
    bas_dev, width = coef_ref.shape
    rows_ref[...] = jnp.zeros(rows_ref.shape, jnp.float32)
    rows_ref[0:bas_dev, 0:width] = coef_ref[...].astype(jnp.float32)
    row_id = iota((MAXBF, 128), 0)
    lane_pair = lane // MAXBF
    batch = len(sides) // 4
    fetch.wait()

    def group(step, carry):
        for u in range(batch):
            g = step * batch + u
            for h in range(2):
                first_ref, second_ref = sides[u * 4 + h * 2], sides[u * 4 + h * 2 + 1]
                for j in range(16):
                    row = pl.ds(row_ref[g, h * 16 + j], 16)
                    place = (j // 2) * MAXBF
                    real, imag = real_ref[row], imag_ref[row]
                    if j % 2:
                        second_ref[place : place + 16, 0:128] = real.astype(jnp.bfloat16)
                        second_ref[place : place + 16, 128:256] = imag.astype(jnp.bfloat16)
                    else:
                        first_ref[place : place + 16, 0:128] = real.astype(jnp.bfloat16)
                        first_ref[place : place + 16, 128:256] = imag.astype(jnp.bfloat16)
                        place += 128
                        first_ref[place : place + 16, 0:128] = imag.astype(jnp.bfloat16)
                        first_ref[place : place + 16, 128:256] = (-real).astype(jnp.bfloat16)
                value = dot_nt(first_ref[...], second_ref[...])
                for c in range(2):
                    part = value[c * 128 : c * 128 + 16]
                    for j in range(1, 8):
                        here = value[c * 128 + j * 16 : c * 128 + j * 16 + 16]
                        part = jnp.where(lane_pair == j, here, part)
                    at = h * 32 + c * 16
                    out_ref[g, at : at + 16] = part.astype(jnp.bfloat16)
                rows = rows_ref[pl.ds(row_ref[g, 32 + h], MAXBF)]
                rows = jnp.where(row_id < row_ref[g, 34 + h], rows, 0.0)
                out_ref[g, 64 + h * 16 : 80 + h * 16] = rows.astype(jnp.bfloat16)
        return carry

    lax.fori_loop(0, groups // batch, group, 0)


def slot_kernel(scale, target_ref, rank_ref, place_ref, parts_ref, got_ref, out_ref, tile_ref):
    total = parts_ref[0].astype(jnp.float32)
    for z in range(1, parts_ref.shape[0]):
        total = total + parts_ref[z].astype(jnp.float32)
    kernel = (total * scale).astype(jnp.bfloat16)
    u, v = iota((128, 128), 0), iota((128, 128), 1)
    same = u // MAXBF == v // MAXBF
    folds = [jnp.where(v == 96 + c * 16 + u % 16, 1.0, 0.0).astype(jnp.bfloat16) for c in range(2)]
    u, v = iota((32, 128), 0), iota((32, 128), 1)
    turned = jnp.where(v == 96 + u, jnp.where(u < MAXBF, 1.0, -1.0), 0.0).astype(jnp.bfloat16)

    def coef(e):
        at = pl.multiple_of(64 + rank_ref[e] * MAXBF, MAXBF)
        return got_ref[target_ref[e], pl.ds(at, MAXBF)]

    for h in range(2):
        block = kernel[h * 32 : (h + 1) * 32]
        first = jnp.zeros((128, 128), jnp.float32)
        for c in range(2):
            tile = block[c * MAXBF : (c + 1) * MAXBF].astype(jnp.float32)
            wide = jnp.where(same, jnp.concatenate([tile] * 8, axis=0), 0.0)
            first = first + dot(wide.astype(jnp.bfloat16), folds[c])
        first = first.astype(jnp.bfloat16)
        second = dot_tn(block, turned).astype(jnp.bfloat16)
        for j in range(8):
            pair, rows = h * 8 + j, slice(j * MAXBF, (j + 1) * MAXBF)
            at = pair * MAXBF
            tile_ref[at : at + MAXBF] = first[rows] + coef(2 * pair + 1)
            tile_ref[256 + at : 256 + at + MAXBF] = second[rows] + coef(2 * pair)
    tile_ref[512:528] = jnp.zeros((MAXBF, 128), jnp.bfloat16)
    for s in range(2 * out_ref.shape[0]):
        rows = tile_ref[pl.ds(pl.multiple_of(place_ref[s], MAXBF), MAXBF)]
        out_ref[s // 2, (s % 2) * MAXBF : (s % 2 + 1) * MAXBF] = rows


def gain_kernel(table_ref, slot_ref, out_ref, sum_ref, turned_ref):
    groups, rows, _ = slot_ref.shape
    width, bas_dev = out_ref.shape
    half = width // 2
    u, v = iota((128, 128), 0), iota((128, 128), 1)
    turn = jnp.where((v < half) & (u == v + half), -1.0, 0.0)
    turn = jnp.where((v >= half) & (v < width) & (u == v - half), 1.0, turn).astype(jnp.bfloat16)
    turned = dot(slot_ref[...].reshape(groups * rows, 128), turn).astype(jnp.bfloat16)
    turned_ref[...] = turned.reshape(groups, rows, 128)
    sum_ref[...] = jnp.zeros(sum_ref.shape, jnp.float32)
    lane, row_id = iota((MAXBF, 128), 1), iota((MAXBF, 128), 0)
    for g in range(groups):
        slots = slot_ref[g]
        wide = slots.astype(jnp.float32)
        tiles = []
        for r in range(2):
            tile = wide[r * MAXBF : (r + 1) * MAXBF]
            real = jnp.where(lane // MAXBF == r, pltpu.roll(tile, 32 + 16 * r, 1), 0.0)
            imag = jnp.where(lane // MAXBF == 2 + r, pltpu.roll(tile, 48 + 16 * r, 1), 0.0)
            tiles.append(real + imag)
        tiles = jnp.concatenate(tiles, axis=0)[:, 0:64].astype(jnp.bfloat16)
        gains = dot(tiles, jnp.concatenate([slots, turned_ref[g]], axis=0))
        for r in range(2):
            part = gains[r * MAXBF : (r + 1) * MAXBF]
            part = jnp.where(row_id < table_ref[g, 34 + r], part, 0.0)
            where = pl.ds(table_ref[g, 32 + r], MAXBF)
            sum_ref[where] = sum_ref[where] + part
    out_ref[...] = sum_ref[0:bas_dev].T[0:width]


def vmem_spec():
    return pl.BlockSpec(memory_space=pltpu.VMEM)


def smem_spec():
    return pl.BlockSpec(memory_space=pltpu.SMEM)


def limit(mib):
    return pltpu.CompilerParams(vmem_limit_bytes=mib * MIB)


def in_hbm(array):
    return pltpu.with_memory_space_constraint(array, pltpu.HBM)


def stage(own, *fetched):
    shapes = [fetched[0].shape, own.shape, (2, 256, 256), (256, 256), (16, 128)]
    return pl.pallas_call(
        stage_kernel,
        in_specs=[vmem_spec()] + [pl.BlockSpec(memory_space=pltpu.HBM)] * len(fetched),
        out_specs=[vmem_spec()] * len(shapes),
        out_shape=[pltpu.VMEM(shape, jnp.bfloat16) for shape in shapes],
        scratch_shapes=[pltpu.VMEM(x.shape, x.dtype) for x in fetched[1:]]
        + [pltpu.VMEM((16, 128), jnp.float32), pltpu.SemaphoreType.DMA((len(fetched),))],
        compiler_params=limit(16),
        cost_estimate=pl.CostEstimate(flops=1 << 28, bytes_accessed=5 * MIB, transcendentals=0),
        name="stage",
    )(own, *[in_hbm(x) for x in fetched])


def fit(odd, near, far, window_rows, ints, order, mix, meta):
    aux_dev, bas_dev, window = ints.shape
    width = near.shape[1]
    blocks = bas_dev // ROWBLK
    shape = (4 * aux_dev, blocks * PACKED + 16, 128)
    return pl.pallas_call(
        fit_kernel,
        in_specs=[smem_spec()] + [vmem_spec()] * 7,
        out_specs=pl.BlockSpec(memory_space=pltpu.HBM),
        out_shape=pltpu.HBM(shape, jnp.bfloat16),
        scratch_shapes=[
            pltpu.VMEM((window, width), jnp.bfloat16),
            pltpu.VMEM(shape, jnp.bfloat16),
            pltpu.SemaphoreType.DMA((blocks // 2,)),
        ],
        compiler_params=limit(32),
        cost_estimate=pl.CostEstimate(
            flops=2 * aux_dev * bas_dev * width * (window + 256),
            bytes_accessed=6 * MIB,
            transcendentals=0,
        ),
        name="fit",
    )(odd, near, far, window_rows, ints, order, mix, meta)


def pair_sums(me, coef, got):
    groups = got.shape[0]
    rows = groups * (got.shape[1] // PACKED) * ROWBLK + MAXBF
    shape = (groups, 6 * MAXBF, 128)
    return pl.pallas_call(
        pair_kernel,
        in_specs=[smem_spec(), vmem_spec(), vmem_spec()],
        out_specs=[vmem_spec()] * 2,
        out_shape=[
            jax.ShapeDtypeStruct((groups, 128), jnp.int32),
            jax.ShapeDtypeStruct(shape, jnp.bfloat16),
        ],
        scratch_shapes=[
            pltpu.VMEM((rows, 128), jnp.float32),
            pltpu.VMEM((rows, 128), jnp.float32),
            pltpu.VMEM((coef.shape[0] + MAXBF, 128), jnp.float32),
            pltpu.VMEM((groups, 128), jnp.float32),
            pltpu.VMEM((groups, 128), jnp.float32),
            pltpu.VMEM((groups, 128), jnp.float32),
            pltpu.SMEM((groups, 128), jnp.int32),
            pltpu.SemaphoreType.DMA,
        ]
        + [pltpu.VMEM((256, 256), jnp.bfloat16), pltpu.VMEM((128, 256), jnp.bfloat16)] * (2 * BATCH),
        compiler_params=limit(40),
        name="pair_sums",
    )(me, coef, got)


def make_slots(scale, targets, ranks, places, parts, got):
    def body(*refs):
        slot_kernel(scale, *refs)

    return pl.pallas_call(
        body,
        in_specs=[smem_spec()] * 3 + [vmem_spec()] * 2,
        out_specs=vmem_spec(),
        out_shape=jax.ShapeDtypeStruct((got.shape[0], 2 * MAXBF, 128), jnp.bfloat16),
        scratch_shapes=[pltpu.VMEM((528, 128), jnp.bfloat16)],
        compiler_params=limit(16),
        name="make_slots",
    )(targets, ranks, places, parts, got)


def add_gains(table, slots, width, bas_dev):
    return pl.pallas_call(
        gain_kernel,
        in_specs=[smem_spec(), vmem_spec()],
        out_specs=vmem_spec(),
        out_shape=jax.ShapeDtypeStruct((width, bas_dev), jnp.float32),
        scratch_shapes=[
            pltpu.VMEM((bas_dev + MAXBF, 128), jnp.float32),
            pltpu.VMEM(slots.shape, jnp.bfloat16),
        ],
        compiler_params=limit(16),
        name="add_gains",
    )(table, slots)


def pick(hit, values):
    return jnp.sum(jnp.where(hit, values, 0), axis=-1)


def per_device(integrals, coeffs, metric, atom_sizes, pair_device, pair_atom):
    aux_dev, bas_dev, window = integrals.shape
    occ = coeffs.shape[2]
    groups = lax.axis_size("atom")
    aux_count = lax.axis_size("aux")
    occ_part = occ // aux_count
    ref_count = pair_atom.shape[0]
    halo = (window - bas_dev) // 2
    scale = 1.0 / math.sqrt(2 * occ * aux_dev * aux_count * MAXBF)
    me = lax.axis_index("atom")

    own = coeffs.reshape(bas_dev, 2 * occ)
    odd = lax.axis_index("atom") % 2
    inner = range(1, groups - 1)
    far = lax.dynamic_slice_in_dim(own, odd * halo, halo, 0)
    far = lax.ppermute(far, "atom", [(i, i + 1 if i % 2 else i - 1) for i in inner])
    near = lax.dynamic_slice_in_dim(own, (1 - odd) * halo, halo, 0)
    near = lax.ppermute(near, "atom", [(i, i ^ 1) for i in range(groups)])

    ints, window_rows, order, mix, meta = stage(
        own, integrals, metric, atom_sizes, pair_device.T, pair_atom[None]
    )
    odd = jnp.full((1,), odd, jnp.int32)
    packed = fit(odd, near, far, window_rows, ints, order, mix, meta)
    got = lax.all_to_all(packed, "atom", split_axis=0, concat_axis=0, tiled=True)
    coef_part = lax.dynamic_slice_in_dim(
        coeffs, lax.axis_index("aux") * occ_part, occ_part, 2
    ).reshape(bas_dev, 2 * occ_part)
    me = jnp.full((1,), lax.axis_index("atom"), jnp.int32)

    targets = pair_device[:, 0]
    order = jnp.arange(ref_count, dtype=jnp.int32)
    earlier = (targets[:, None] == targets[None, :]) & (order[None, :] < order[:, None])
    ranks = jnp.sum(earlier.astype(jnp.int32), axis=1)
    asked = targets * 2 + ranks
    place = (order % 2) * 256 + (order // 2) * MAXBF
    asked_hit = asked[None, :] == jnp.arange(2 * groups, dtype=jnp.int32)[:, None]
    places = 512 + pick(asked_hit, place[None, :] - 512)

    me, coef_part, got, targets, ranks, places = lax.optimization_barrier(
        (me, coef_part, got, targets, ranks, places)
    )
    table, sent = pair_sums(me, coef_part, got)
    owned = lax.all_to_all(sent, "atom", split_axis=0, concat_axis=0, tiled=True)
    own_sums = jnp.sum(owned[:, : 4 * MAXBF].astype(jnp.float32), axis=0).astype(jnp.bfloat16)
    shared = jnp.broadcast_to(own_sums[None], (aux_count,) + own_sums.shape)
    parts = lax.all_to_all(shared, "aux", split_axis=0, concat_axis=0, tiled=True)
    slots = make_slots(scale, targets, ranks, places, parts, owned)
    slots = lax.all_to_all(slots, "atom", split_axis=0, concat_axis=0, tiled=True)
    result = add_gains(table, slots, 2 * occ_part, bas_dev)
    return result.reshape(2, occ_part, bas_dev).transpose(2, 0, 1)


def solution(mesh):
    placed = (
        P("aux", "atom", None),
        P("atom", None, None),
        P("aux", None),
        P("atom", None),
        P("atom", None),
        P("atom"),
    )
    return jax.shard_map(
        per_device, mesh=mesh, in_specs=placed, out_specs=P("atom", None, "aux"), check_vma=False
    )
```

```python
import math

import jax
import jax.numpy as jnp
from jax import lax
from jax.experimental import pallas as pl
from jax.experimental.pallas import tpu as pltpu
from jax.sharding import PartitionSpec as P

MAXBF = 16
ROWBLK = 32
PACKED = ROWBLK + ROWBLK // 2
BATCH = 16
MIB = 1 << 20


def iota(shape, dim):
    return lax.broadcasted_iota(jnp.int32, shape, dim)


def dot(a, b):
    return jnp.dot(a, b, preferred_element_type=jnp.float32)


def dot_nt(a, b):
    return lax.dot_general(a, b, (((1,), (1,)), ((), ())), preferred_element_type=jnp.float32)


def dot_tn(a, b):
    return lax.dot_general(a, b, (((0,), (0,)), ((), ())), preferred_element_type=jnp.float32)


def ordered(part_ref, order_ref, window_ref, at):
    rows = part_ref.shape[0]
    half = part_ref.shape[1] // 2
    for t in range(3):
        real = part_ref[:, t * 128 : (t + 1) * 128]
        imag = part_ref[:, half + t * 128 : half + (t + 1) * 128]
        value = dot(jnp.concatenate([real, imag], axis=1), order_ref[t // 2])
        place = pl.ds(at if isinstance(at, int) else pl.multiple_of(at, 128), rows)
        window_ref[place, t * 256 : (t + 1) * 256] = value.astype(jnp.bfloat16)


def stage_kernel(
    part_ref, own_ref, ints_hbm, metric_hbm, size_hbm, dev_hbm, atom_hbm,
    ints_ref, window_ref, order_ref, mix_ref, meta_ref, coef_ref,
    metric_ref, size_ref, dev_ref, atom_ref, rows_ref, sem_ref,
):
    sources = (ints_hbm, metric_hbm, size_hbm, dev_hbm, atom_hbm)
    targets = (ints_ref, metric_ref, size_ref, dev_ref, atom_ref)
    fetches = [
        pltpu.make_async_copy(a, b, sem_ref.at[i]) for i, (a, b) in enumerate(zip(sources, targets))
    ]
    for fetch in fetches:
        fetch.start()
    u, v = iota((256, 256), 0), iota((256, 256), 1)
    main_order = u == ((v % 128) // 64) * 128 + (v // 128) * 64 + v % 64
    side_order = u == ((v % 64) // 32) * 128 + (v // 64) * 32 + v % 32
    order_ref[0] = jnp.where(main_order, 1.0, 0.0).astype(jnp.bfloat16)
    order_ref[1] = jnp.where(side_order, 1.0, 0.0).astype(jnp.bfloat16)
    ordered(own_ref, order_ref, window_ref, 0)
    width = own_ref.shape[1]
    part = width // 16
    row, lane = iota((width, 128), 0), iota((width, 128), 1)
    source = part_ref[0] * part + jnp.where(lane < part, lane, lane + width // 2 - part)
    chosen = jnp.where((row == source) & (lane < 2 * part), 1.0, 0.0).astype(jnp.bfloat16)
    coef_ref[...] = dot(own_ref[...], chosen).astype(jnp.bfloat16)
    for fetch in fetches[1:]:
        fetch.wait()
    member = iota((256, 8), 0) // ROWBLK == iota((256, 8), 1)
    member = jnp.where(member, 1.0, 0.0).astype(jnp.bfloat16)
    mix = dot_nt(dot_nt(member, metric_ref[...]).astype(jnp.bfloat16), member)
    mix_ref[...] = jnp.where(u % ROWBLK == v % ROWBLK, mix, 0.0).astype(jnp.bfloat16)
    rows_ref[...] = jnp.zeros(rows_ref.shape, jnp.float32)
    for row, value_ref in enumerate((size_ref, dev_ref, atom_ref)):
        rows_ref[row : row + 1, 0 : value_ref.shape[1]] = value_ref[...].astype(jnp.float32)
    meta_ref[...] = rows_ref[...].astype(jnp.bfloat16)
    fetches[0].wait()


def fit_kernel(
    odd_ref, near_ref, far_ref, own_ref, ints_ref, order_ref, mix_ref, meta_ref, out_ref,
    window_ref,
):
    aux_dev, bas_dev, span = ints_ref.shape
    blocks = bas_dev // ROWBLK
    halo = near_ref.shape[0]
    far_at = odd_ref[0] * (halo + bas_dev)
    ordered(near_ref, order_ref, window_ref, halo + bas_dev - far_at)
    window_ref[halo : halo + bas_dev] = own_ref[...]
    ordered(far_ref, order_ref, window_ref, far_at)
    mix = mix_ref[...]
    left = iota((ROWBLK // 2, 128), 1) < 64
    for u in range(blocks):
        if u % 4 == 0:
            ints = ints_ref[:, u * ROWBLK : (u + 4) * ROWBLK].reshape(-1, span)
            wide = dot(ints, window_ref[...]).astype(jnp.bfloat16)
            wide = wide.reshape(aux_dev, 4 * ROWBLK, -1)
        at = (u % 4) * ROWBLK
        half = wide[:, at : at + ROWBLK].reshape(aux_dev * ROWBLK, -1)
        fitted = dot(mix, half)
        main = slice(u * PACKED, u * PACKED + ROWBLK)
        side = slice(u * PACKED + ROWBLK, (u + 1) * PACKED)
        for p in range(aux_dev):
            rows = fitted[p * ROWBLK : (p + 1) * ROWBLK]
            for k in range(4):
                tile = rows[:, k * 128 : (k + 1) * 128]
                out_ref[p * 4 + k, main] = tile.astype(jnp.bfloat16)
            for k in range(2):
                shared = rows[:, 512 + k * 128 : 640 + k * 128]
                top, bottom = shared[: ROWBLK // 2], shared[ROWBLK // 2 :]
                even = jnp.where(left, top, pltpu.roll(bottom, 64, 1))
                odd = jnp.where(left, pltpu.roll(top, 64, 1), bottom)
                out_ref[p * 4 + 2 * k, side] = even.astype(jnp.bfloat16)
                out_ref[p * 4 + 2 * k + 1, side] = odd.astype(jnp.bfloat16)
        if u == blocks - 1:
            for d in range(4 * aux_dev):
                out_ref[d, blocks * PACKED : blocks * PACKED + 16] = meta_ref[...]


def end_table(me, got_ref, size_ref, dev_ref, atom_ref):
    groups, at = got_ref.shape[0], got_ref.shape[1] - 16
    for d in range(groups):
        rows = got_ref[d, at : at + 16].astype(jnp.float32)
        for i, dest in enumerate((size_ref, dev_ref, atom_ref)):
            dest[d : d + 1] = rows[i : i + 1]
    before = jnp.where(iota((128, 128), 0) < iota((128, 128), 1), 1.0, 0.0).astype(jnp.bfloat16)
    sizes = size_ref[...]
    packed = dot(sizes.astype(jnp.bfloat16), before) * 32.0 + sizes
    devices = dev_ref[...].astype(jnp.int32)
    atoms = atom_ref[...].astype(jnp.int32)
    found = jnp.zeros(packed.shape, jnp.float32)
    for d in range(groups):
        row = jnp.broadcast_to(packed[d : d + 1], packed.shape)
        found = jnp.where(devices == d, jnp.take_along_axis(row, atoms, axis=1), found)
    found = found.astype(jnp.int32)
    starts, counts = found // 32, found % 32
    lane = iota(found.shape, 1)
    here = (devices == me) & (lane < 32)
    rank = dot(jnp.where(here, 1.0, 0.0).astype(jnp.bfloat16), before)
    table = jnp.where(lane < 32, devices * 256 + starts, 0)
    for i, value in enumerate((starts, counts)):
        value = value.astype(jnp.float32)
        for r in range(2):
            one = jnp.sum(jnp.where(here & (rank == r), value, 0.0), axis=1, keepdims=True)
            table = jnp.where(lane == 32 + 2 * i + r, one.astype(jnp.int32), table)
    return table


def pair_kernel(
    me_ref, coef_ref, got_ref, table_ref, out_ref, real_ref, imag_ref, rows_ref,
    size_ref, dev_ref, atom_ref, row_ref, table_sem, *sides,
):
    table_ref[...] = end_table(me_ref[0], got_ref, size_ref, dev_ref, atom_ref)
    fetch = pltpu.make_async_copy(table_ref, row_ref, table_sem)
    fetch.start()
    groups, blocks = got_ref.shape[0], got_ref.shape[1] // PACKED
    lane = iota((ROWBLK // 2, 128), 1)
    left, valid = lane < 64, lane < 96

    def unpack(b, carry):
        for i in range(blocks):
            base = pl.multiple_of(b * (blocks * ROWBLK) + i * ROWBLK, ROWBLK)
            shared = got_ref[b, i * PACKED + ROWBLK : (i + 1) * PACKED].astype(jnp.float32)
            for h in range(2):
                at = i * PACKED + h * 16
                main = got_ref[b, at : at + 16].astype(jnp.float32)
                real = shared if h else pltpu.roll(shared, 64, 1)
                imag = pltpu.roll(shared, 96 if h else 32, 1)
                real = jnp.where(left, main, jnp.where(valid, real, 0.0))
                imag = jnp.where(left, pltpu.roll(main, 64, 1), jnp.where(valid, imag, 0.0))
                real_ref[pl.ds(base + h * 16, 16)] = real
                imag_ref[pl.ds(base + h * 16, 16)] = imag
        return carry

    lax.fori_loop(0, groups, unpack, 0, unroll=8)
    tail = groups * blocks * ROWBLK
    real_ref[tail : tail + MAXBF] = jnp.zeros((MAXBF, 128), jnp.float32)
    imag_ref[tail : tail + MAXBF] = jnp.zeros((MAXBF, 128), jnp.float32)
    bas_dev = coef_ref.shape[0]
    rows_ref[...] = jnp.zeros(rows_ref.shape, jnp.float32)
    rows_ref[0:bas_dev] = coef_ref[...].astype(jnp.float32)
    row_id = iota((MAXBF, 128), 0)
    lane_pair = lane // MAXBF
    batch = len(sides) // 4
    fetch.wait()

    def group(step, carry):
        for u in range(batch):
            g = step * batch + u
            for h in range(2):
                first_ref, second_ref = sides[u * 4 + h * 2], sides[u * 4 + h * 2 + 1]
                for j in range(16):
                    row = pl.ds(row_ref[g, h * 16 + j], 16)
                    place = (j // 2) * MAXBF
                    real, imag = real_ref[row], imag_ref[row]
                    if j % 2:
                        second_ref[place : place + 16, 0:128] = real.astype(jnp.bfloat16)
                        second_ref[place : place + 16, 128:256] = imag.astype(jnp.bfloat16)
                    else:
                        first_ref[place : place + 16, 0:128] = real.astype(jnp.bfloat16)
                        first_ref[place : place + 16, 128:256] = imag.astype(jnp.bfloat16)
                        place += 128
                        first_ref[place : place + 16, 0:128] = imag.astype(jnp.bfloat16)
                        first_ref[place : place + 16, 128:256] = (-real).astype(jnp.bfloat16)
                value = dot_nt(first_ref[...], second_ref[...])
                for c in range(2):
                    part = value[c * 128 : c * 128 + 16]
                    for j in range(1, 8):
                        here = value[c * 128 + j * 16 : c * 128 + j * 16 + 16]
                        part = jnp.where(lane_pair == j, here, part)
                    at = h * 32 + c * 16
                    out_ref[g, at : at + 16] = part.astype(jnp.bfloat16)
                rows = rows_ref[pl.ds(row_ref[g, 32 + h], MAXBF)]
                rows = jnp.where(row_id < row_ref[g, 34 + h], rows, 0.0)
                out_ref[g, 64 + h * 16 : 80 + h * 16] = rows.astype(jnp.bfloat16)
        return carry

    lax.fori_loop(0, groups // batch, group, 0)


def slot_kernel(scale, asked_ref, place_ref, parts_ref, got_ref, out_ref, tile_ref):
    total = parts_ref[0].astype(jnp.float32)
    for z in range(1, parts_ref.shape[0]):
        total = total + parts_ref[z].astype(jnp.float32)
    kernel = (total * scale).astype(jnp.bfloat16)
    u, v = iota((128, 128), 0), iota((128, 128), 1)
    same = u // MAXBF == v // MAXBF
    folds = [jnp.where(v == 96 + c * 16 + u % 16, 1.0, 0.0).astype(jnp.bfloat16) for c in range(2)]
    u, v = iota((32, 128), 0), iota((32, 128), 1)
    turned = jnp.where(v == 96 + u, jnp.where(u < MAXBF, 1.0, -1.0), 0.0).astype(jnp.bfloat16)

    def coef(e):
        at = pl.multiple_of(64 + (asked_ref[e] % 2) * MAXBF, MAXBF)
        return got_ref[asked_ref[e] // 2, pl.ds(at, MAXBF)]

    for h in range(2):
        block = kernel[h * 32 : (h + 1) * 32]
        first = jnp.zeros((128, 128), jnp.float32)
        for c in range(2):
            tile = block[c * MAXBF : (c + 1) * MAXBF].astype(jnp.float32)
            wide = jnp.where(same, jnp.concatenate([tile] * 8, axis=0), 0.0)
            first = first + dot(wide.astype(jnp.bfloat16), folds[c])
        first = first.astype(jnp.bfloat16)
        second = dot_tn(block, turned).astype(jnp.bfloat16)
        for j in range(8):
            pair, rows = h * 8 + j, slice(j * MAXBF, (j + 1) * MAXBF)
            at = pair * MAXBF
            tile_ref[at : at + MAXBF] = first[rows] + coef(2 * pair + 1)
            tile_ref[256 + at : 256 + at + MAXBF] = second[rows] + coef(2 * pair)
    tile_ref[512:528] = jnp.zeros((MAXBF, 128), jnp.bfloat16)
    for s in range(2 * out_ref.shape[0]):
        rows = tile_ref[pl.ds(pl.multiple_of(place_ref[s], MAXBF), MAXBF)]
        out_ref[s // 2, (s % 2) * MAXBF : (s % 2 + 1) * MAXBF] = rows


def gain_kernel(table_ref, slot_ref, out_ref, sum_ref, turned_ref):
    groups, rows, _ = slot_ref.shape
    width, bas_dev = out_ref.shape
    half = width // 2
    u, v = iota((128, 128), 0), iota((128, 128), 1)
    turn = jnp.where((v < half) & (u == v + half), -1.0, 0.0)
    turn = jnp.where((v >= half) & (v < width) & (u == v - half), 1.0, turn).astype(jnp.bfloat16)
    turned = dot(slot_ref[...].reshape(groups * rows, 128), turn).astype(jnp.bfloat16)
    turned_ref[...] = turned.reshape(groups, rows, 128)
    sum_ref[...] = jnp.zeros(sum_ref.shape, jnp.float32)
    lane, row_id = iota((MAXBF, 128), 1), iota((MAXBF, 128), 0)
    for g in range(groups):
        slots = slot_ref[g]
        wide = slots.astype(jnp.float32)
        tiles = []
        for r in range(2):
            tile = wide[r * MAXBF : (r + 1) * MAXBF]
            real = jnp.where(lane // MAXBF == r, pltpu.roll(tile, 32 + 16 * r, 1), 0.0)
            imag = jnp.where(lane // MAXBF == 2 + r, pltpu.roll(tile, 48 + 16 * r, 1), 0.0)
            tiles.append(real + imag)
        tiles = jnp.concatenate(tiles, axis=0)[:, 0:64].astype(jnp.bfloat16)
        gains = dot(tiles, jnp.concatenate([slots, turned_ref[g]], axis=0))
        for r in range(2):
            part = gains[r * MAXBF : (r + 1) * MAXBF]
            part = jnp.where(row_id < table_ref[g, 34 + r], part, 0.0)
            where = pl.ds(table_ref[g, 32 + r], MAXBF)
            sum_ref[where] = sum_ref[where] + part
    out_ref[...] = sum_ref[0:bas_dev].T[0:width]


def vmem_spec():
    return pl.BlockSpec(memory_space=pltpu.VMEM)


def smem_spec():
    return pl.BlockSpec(memory_space=pltpu.SMEM)


def limit(mib):
    return pltpu.CompilerParams(vmem_limit_bytes=mib * MIB)


def in_hbm(array):
    return pltpu.with_memory_space_constraint(array, pltpu.HBM)


def stage(part, own, *fetched):
    shapes = [fetched[0].shape, own.shape, (2, 256, 256), (256, 256), (16, 128)]
    shapes.append((own.shape[0], 128))
    return pl.pallas_call(
        stage_kernel,
        in_specs=[smem_spec(), vmem_spec()]
        + [pl.BlockSpec(memory_space=pltpu.HBM)] * len(fetched),
        out_specs=[vmem_spec()] * len(shapes),
        out_shape=[pltpu.VMEM(shape, jnp.bfloat16) for shape in shapes],
        scratch_shapes=[pltpu.VMEM(x.shape, x.dtype) for x in fetched[1:]]
        + [pltpu.VMEM((16, 128), jnp.float32), pltpu.SemaphoreType.DMA((len(fetched),))],
        compiler_params=limit(16),
        cost_estimate=pl.CostEstimate(flops=1 << 28, bytes_accessed=5 * MIB, transcendentals=0),
        name="stage",
    )(part, own, *[in_hbm(x) for x in fetched])


def fit(odd, near, far, window_rows, ints, order, mix, meta):
    aux_dev, bas_dev, window = ints.shape
    width = near.shape[1]
    blocks = bas_dev // ROWBLK
    shape = (4 * aux_dev, blocks * PACKED + 16, 128)
    return pl.pallas_call(
        fit_kernel,
        in_specs=[smem_spec()] + [vmem_spec()] * 7,
        out_specs=vmem_spec(),
        out_shape=jax.ShapeDtypeStruct(shape, jnp.bfloat16),
        scratch_shapes=[pltpu.VMEM((window, width), jnp.bfloat16)],
        compiler_params=limit(32),
        cost_estimate=pl.CostEstimate(
            flops=2 * aux_dev * bas_dev * width * (window + 256),
            bytes_accessed=6 * MIB,
            transcendentals=0,
        ),
        name="fit",
    )(odd, near, far, window_rows, ints, order, mix, meta)


def pair_sums(me, coef, got):
    groups = got.shape[0]
    rows = groups * (got.shape[1] // PACKED) * ROWBLK + MAXBF
    shape = (groups, 6 * MAXBF, 128)
    return pl.pallas_call(
        pair_kernel,
        in_specs=[smem_spec(), vmem_spec(), vmem_spec()],
        out_specs=[vmem_spec()] * 2,
        out_shape=[
            jax.ShapeDtypeStruct((groups, 128), jnp.int32),
            jax.ShapeDtypeStruct(shape, jnp.bfloat16),
        ],
        scratch_shapes=[
            pltpu.VMEM((rows, 128), jnp.float32),
            pltpu.VMEM((rows, 128), jnp.float32),
            pltpu.VMEM((coef.shape[0] + MAXBF, 128), jnp.float32),
            pltpu.VMEM((groups, 128), jnp.float32),
            pltpu.VMEM((groups, 128), jnp.float32),
            pltpu.VMEM((groups, 128), jnp.float32),
            pltpu.SMEM((groups, 128), jnp.int32),
            pltpu.SemaphoreType.DMA,
        ]
        + [pltpu.VMEM((256, 256), jnp.bfloat16), pltpu.VMEM((128, 256), jnp.bfloat16)] * (2 * BATCH),
        compiler_params=limit(40),
        name="pair_sums",
    )(me, coef, got)


def make_slots(scale, asked, places, parts, got):
    def body(*refs):
        slot_kernel(scale, *refs)

    return pl.pallas_call(
        body,
        in_specs=[smem_spec()] * 2 + [vmem_spec()] * 2,
        out_specs=vmem_spec(),
        out_shape=jax.ShapeDtypeStruct((got.shape[0], 2 * MAXBF, 128), jnp.bfloat16),
        scratch_shapes=[pltpu.VMEM((528, 128), jnp.bfloat16)],
        compiler_params=limit(16),
        name="make_slots",
    )(asked, places, parts, got)


def add_gains(table, slots, width, bas_dev):
    return pl.pallas_call(
        gain_kernel,
        in_specs=[smem_spec(), vmem_spec()],
        out_specs=vmem_spec(),
        out_shape=jax.ShapeDtypeStruct((width, bas_dev), jnp.float32),
        scratch_shapes=[
            pltpu.VMEM((bas_dev + MAXBF, 128), jnp.float32),
            pltpu.VMEM(slots.shape, jnp.bfloat16),
        ],
        compiler_params=limit(16),
        name="add_gains",
    )(table, slots)


def pick(hit, values):
    return jnp.sum(jnp.where(hit, values, 0), axis=-1)


def per_device(integrals, coeffs, metric, atom_sizes, pair_device, pair_atom):
    aux_dev, bas_dev, window = integrals.shape
    occ = coeffs.shape[2]
    groups = lax.axis_size("atom")
    aux_count = lax.axis_size("aux")
    occ_part = occ // aux_count
    ref_count = pair_atom.shape[0]
    halo = (window - bas_dev) // 2
    scale = 1.0 / math.sqrt(2 * occ * aux_dev * aux_count * MAXBF)
    me = lax.axis_index("atom")

    own = coeffs.reshape(bas_dev, 2 * occ)
    odd = lax.axis_index("atom") % 2
    inner = range(1, groups - 1)
    far = lax.dynamic_slice_in_dim(own, odd * halo, halo, 0)
    far = lax.ppermute(far, "atom", [(i, i + 1 if i % 2 else i - 1) for i in inner])
    near = lax.dynamic_slice_in_dim(own, (1 - odd) * halo, halo, 0)
    near = lax.ppermute(near, "atom", [(i, i ^ 1) for i in range(groups)])

    part = jnp.full((1,), lax.axis_index("aux"), jnp.int32)
    ints, window_rows, columns, mix, meta, coef_part = stage(
        part, own, integrals, metric, atom_sizes, pair_device.T, pair_atom[None]
    )
    me = jnp.full((1,), lax.axis_index("atom"), jnp.int32)

    targets = pair_device[:, 0]
    order = jnp.arange(ref_count, dtype=jnp.int32)
    earlier = (targets[:, None] == targets[None, :]) & (order[None, :] < order[:, None])
    ranks = jnp.sum(earlier.astype(jnp.int32), axis=1)
    asked = targets * 2 + ranks
    place = (order % 2) * 256 + (order // 2) * MAXBF
    asked_hit = asked[None, :] == jnp.arange(2 * groups, dtype=jnp.int32)[:, None]
    places = 512 + pick(asked_hit, place[None, :] - 512)

    near, far, me, coef_part, asked, places = lax.optimization_barrier(
        (near, far, me, coef_part, asked, places)
    )
    odd = jnp.full((1,), odd, jnp.int32)
    packed = fit(odd, near, far, window_rows, ints, columns, mix, meta)
    got = lax.all_to_all(packed, "atom", split_axis=0, concat_axis=0, tiled=True)
    table, sent = pair_sums(me, coef_part, got)
    owned = lax.all_to_all(sent, "atom", split_axis=0, concat_axis=0, tiled=True)
    own_sums = jnp.sum(owned[:, : 4 * MAXBF].astype(jnp.float32), axis=0).astype(jnp.bfloat16)
    shared = jnp.broadcast_to(own_sums[None], (aux_count,) + own_sums.shape)
    parts = lax.all_to_all(shared, "aux", split_axis=0, concat_axis=0, tiled=True)
    slots = make_slots(scale, asked, places, parts, owned)
    slots = lax.all_to_all(slots, "atom", split_axis=0, concat_axis=0, tiled=True)
    result = add_gains(table, slots, 2 * occ_part, bas_dev)
    return result.reshape(2, occ_part, bas_dev).transpose(2, 0, 1)


def solution(mesh):
    placed = (
        P("aux", "atom", None),
        P("atom", None, None),
        P("aux", None),
        P("atom", None),
        P("atom", None),
        P("atom"),
    )
    return jax.shard_map(
        per_device, mesh=mesh, in_specs=placed, out_specs=P("atom", None, "aux"), check_vma=False
    )
```

```python
import math

import jax
import jax.numpy as jnp
from jax import lax
from jax.experimental import pallas as pl
from jax.experimental.pallas import tpu as pltpu
from jax.sharding import PartitionSpec as P

MAXBF = 16
ROWBLK = 32
PACKED = ROWBLK + ROWBLK // 2
BATCH = 16
MIB = 1 << 20


def iota(shape, dim):
    return lax.broadcasted_iota(jnp.int32, shape, dim)


def dot(a, b):
    return jnp.dot(a, b, preferred_element_type=jnp.float32)


def dot_nt(a, b):
    return lax.dot_general(a, b, (((1,), (1,)), ((), ())), preferred_element_type=jnp.float32)


def dot_tn(a, b):
    return lax.dot_general(a, b, (((0,), (0,)), ((), ())), preferred_element_type=jnp.float32)


def ordered(part_ref, order_ref, window_ref, at):
    rows = part_ref.shape[0]
    half = part_ref.shape[1] // 2
    for t in range(3):
        real = part_ref[:, t * 128 : (t + 1) * 128]
        imag = part_ref[:, half + t * 128 : half + (t + 1) * 128]
        value = dot(jnp.concatenate([real, imag], axis=1), order_ref[t // 2])
        place = pl.ds(at if isinstance(at, int) else pl.multiple_of(at, 128), rows)
        window_ref[place, t * 256 : (t + 1) * 256] = value.astype(jnp.bfloat16)


def stage_kernel(
    part_ref, own_ref, ints_hbm, metric_hbm, size_hbm, dev_hbm, atom_hbm,
    ints_ref, window_ref, order_ref, mix_ref, meta_ref, coef_ref,
    metric_ref, size_ref, dev_ref, atom_ref, rows_ref, sem_ref,
):
    sources = (ints_hbm, metric_hbm, size_hbm, dev_hbm, atom_hbm)
    targets = (ints_ref, metric_ref, size_ref, dev_ref, atom_ref)
    fetches = [
        pltpu.make_async_copy(a, b, sem_ref.at[i]) for i, (a, b) in enumerate(zip(sources, targets))
    ]
    for fetch in fetches:
        fetch.start()
    u, v = iota((256, 256), 0), iota((256, 256), 1)
    main_order = u == ((v % 128) // 64) * 128 + (v // 128) * 64 + v % 64
    side_order = u == ((v % 64) // 32) * 128 + (v // 64) * 32 + v % 32
    order_ref[0] = jnp.where(main_order, 1.0, 0.0).astype(jnp.bfloat16)
    order_ref[1] = jnp.where(side_order, 1.0, 0.0).astype(jnp.bfloat16)
    ordered(own_ref, order_ref, window_ref, 0)
    width = own_ref.shape[1]
    part = width // 16
    row, lane = iota((width, 128), 0), iota((width, 128), 1)
    source = part_ref[0] * part + jnp.where(lane < part, lane, lane + width // 2 - part)
    chosen = jnp.where((row == source) & (lane < 2 * part), 1.0, 0.0).astype(jnp.bfloat16)
    coef_ref[...] = dot(own_ref[...], chosen).astype(jnp.bfloat16)
    for fetch in fetches[1:]:
        fetch.wait()
    member = iota((256, 8), 0) // ROWBLK == iota((256, 8), 1)
    member = jnp.where(member, 1.0, 0.0).astype(jnp.bfloat16)
    mix = dot_nt(dot_nt(member, metric_ref[...]).astype(jnp.bfloat16), member)
    mix_ref[...] = jnp.where(u % ROWBLK == v % ROWBLK, mix, 0.0).astype(jnp.bfloat16)
    rows_ref[...] = jnp.zeros(rows_ref.shape, jnp.float32)
    for row, value_ref in enumerate((size_ref, dev_ref, atom_ref)):
        rows_ref[row : row + 1, 0 : value_ref.shape[1]] = value_ref[...].astype(jnp.float32)
    meta_ref[...] = rows_ref[...].astype(jnp.bfloat16)
    fetches[0].wait()


def fit_kernel(
    odd_ref, near_ref, far_ref, own_ref, ints_ref, order_ref, mix_ref, meta_ref, out_ref,
    window_ref,
):
    aux_dev, bas_dev, span = ints_ref.shape
    blocks = bas_dev // ROWBLK
    halo = near_ref.shape[0]
    far_at = odd_ref[0] * (halo + bas_dev)
    ordered(near_ref, order_ref, window_ref, halo + bas_dev - far_at)
    window_ref[halo : halo + bas_dev] = own_ref[...]
    ordered(far_ref, order_ref, window_ref, far_at)
    mix = mix_ref[...]
    left = iota((ROWBLK // 2, 128), 1) < 64
    for u in range(blocks):
        if u % 4 == 0:
            ints = ints_ref[:, u * ROWBLK : (u + 4) * ROWBLK].reshape(-1, span)
            wide = dot(ints, window_ref[...]).astype(jnp.bfloat16)
            wide = wide.reshape(aux_dev, 4 * ROWBLK, -1)
        at = (u % 4) * ROWBLK
        half = wide[:, at : at + ROWBLK].reshape(aux_dev * ROWBLK, -1)
        fitted = dot(mix, half)
        main = slice(u * PACKED, u * PACKED + ROWBLK)
        side = slice(u * PACKED + ROWBLK, (u + 1) * PACKED)
        for p in range(aux_dev):
            rows = fitted[p * ROWBLK : (p + 1) * ROWBLK]
            for k in range(4):
                tile = rows[:, k * 128 : (k + 1) * 128]
                out_ref[p * 4 + k, main] = tile.astype(jnp.bfloat16)
            for k in range(2):
                shared = rows[:, 512 + k * 128 : 640 + k * 128]
                top, bottom = shared[: ROWBLK // 2], shared[ROWBLK // 2 :]
                even = jnp.where(left, top, pltpu.roll(bottom, 64, 1))
                odd = jnp.where(left, pltpu.roll(top, 64, 1), bottom)
                out_ref[p * 4 + 2 * k, side] = even.astype(jnp.bfloat16)
                out_ref[p * 4 + 2 * k + 1, side] = odd.astype(jnp.bfloat16)
        if u == blocks - 1:
            for d in range(4 * aux_dev):
                out_ref[d, blocks * PACKED : blocks * PACKED + 8] = meta_ref[...]


def end_table(me, got_ref, size_ref, dev_ref, atom_ref):
    groups, at = got_ref.shape[0], got_ref.shape[1] - 8
    for d in range(groups):
        rows = got_ref[d, at : at + 8].astype(jnp.float32)
        for i, dest in enumerate((size_ref, dev_ref, atom_ref)):
            dest[d : d + 1] = rows[i : i + 1]
    before = jnp.where(iota((128, 128), 0) < iota((128, 128), 1), 1.0, 0.0).astype(jnp.bfloat16)
    sizes = size_ref[...]
    packed = dot(sizes.astype(jnp.bfloat16), before) * 32.0 + sizes
    devices = dev_ref[...].astype(jnp.int32)
    atoms = atom_ref[...].astype(jnp.int32)
    found = jnp.zeros(packed.shape, jnp.float32)
    for d in range(groups):
        row = jnp.broadcast_to(packed[d : d + 1], packed.shape)
        found = jnp.where(devices == d, jnp.take_along_axis(row, atoms, axis=1), found)
    found = found.astype(jnp.int32)
    starts, counts = found // 32, found % 32
    lane = iota(found.shape, 1)
    here = (devices == me) & (lane < 32)
    rank = dot(jnp.where(here, 1.0, 0.0).astype(jnp.bfloat16), before)
    table = jnp.where(lane < 32, devices * 256 + starts, 0)
    for i, value in enumerate((starts, counts)):
        value = value.astype(jnp.float32)
        for r in range(2):
            one = jnp.sum(jnp.where(here & (rank == r), value, 0.0), axis=1, keepdims=True)
            table = jnp.where(lane == 32 + 2 * i + r, one.astype(jnp.int32), table)
    return table


def pair_kernel(
    me_ref, coef_ref, got_ref, slot_ref, out_ref, real_ref, imag_ref, rows_ref, table_ref,
    size_ref, dev_ref, atom_ref, row_ref, table_sem, *sides,
):
    table = end_table(me_ref[0], got_ref, size_ref, dev_ref, atom_ref)
    table_ref[...] = table
    slot_ref[...] = jnp.zeros(slot_ref.shape, jnp.int32)
    slot_ref[:, 0 : table.shape[0]] = table.astype(jnp.float32).T[32:40].astype(jnp.int32)
    fetch = pltpu.make_async_copy(table_ref, row_ref, table_sem)
    fetch.start()
    groups, blocks = got_ref.shape[0], got_ref.shape[1] // PACKED
    lane = iota((ROWBLK // 2, 128), 1)
    left, valid = lane < 64, lane < 96

    def unpack(b, carry):
        for i in range(blocks):
            base = pl.multiple_of(b * (blocks * ROWBLK) + i * ROWBLK, ROWBLK)
            shared = got_ref[b, i * PACKED + ROWBLK : (i + 1) * PACKED].astype(jnp.float32)
            for h in range(2):
                at = i * PACKED + h * 16
                main = got_ref[b, at : at + 16].astype(jnp.float32)
                real = shared if h else pltpu.roll(shared, 64, 1)
                imag = pltpu.roll(shared, 96 if h else 32, 1)
                real = jnp.where(left, main, jnp.where(valid, real, 0.0))
                imag = jnp.where(left, pltpu.roll(main, 64, 1), jnp.where(valid, imag, 0.0))
                real_ref[pl.ds(base + h * 16, 16)] = real
                imag_ref[pl.ds(base + h * 16, 16)] = imag
        return carry

    lax.fori_loop(0, groups, unpack, 0, unroll=8)
    tail = groups * blocks * ROWBLK
    real_ref[tail : tail + MAXBF] = jnp.zeros((MAXBF, 128), jnp.float32)
    imag_ref[tail : tail + MAXBF] = jnp.zeros((MAXBF, 128), jnp.float32)
    bas_dev = coef_ref.shape[0]
    rows_ref[...] = jnp.zeros(rows_ref.shape, jnp.float32)
    rows_ref[0:bas_dev] = coef_ref[...].astype(jnp.float32)
    row_id = iota((MAXBF, 128), 0)
    lane_pair = lane // MAXBF
    batch = len(sides) // 4
    fetch.wait()

    def group(step, carry):
        for u in range(batch):
            g = step * batch + u
            for h in range(2):
                first_ref, second_ref = sides[u * 4 + h * 2], sides[u * 4 + h * 2 + 1]
                for j in range(16):
                    row = pl.ds(row_ref[g, h * 16 + j], 16)
                    place = (j // 2) * MAXBF
                    real, imag = real_ref[row], imag_ref[row]
                    if j % 2:
                        second_ref[place : place + 16, 0:128] = real.astype(jnp.bfloat16)
                        second_ref[place : place + 16, 128:256] = imag.astype(jnp.bfloat16)
                    else:
                        first_ref[place : place + 16, 0:128] = real.astype(jnp.bfloat16)
                        first_ref[place : place + 16, 128:256] = imag.astype(jnp.bfloat16)
                        place += 128
                        first_ref[place : place + 16, 0:128] = imag.astype(jnp.bfloat16)
                        first_ref[place : place + 16, 128:256] = (-real).astype(jnp.bfloat16)
                value = dot_nt(first_ref[...], second_ref[...])
                for c in range(2):
                    part = value[c * 128 : c * 128 + 16]
                    for j in range(1, 8):
                        here = value[c * 128 + j * 16 : c * 128 + j * 16 + 16]
                        part = jnp.where(lane_pair == j, here, part)
                    at = h * 32 + c * 16
                    out_ref[g, at : at + 16] = part.astype(jnp.bfloat16)
                rows = rows_ref[pl.ds(row_ref[g, 32 + h], MAXBF)]
                rows = jnp.where(row_id < row_ref[g, 34 + h], rows, 0.0)
                out_ref[g, 64 + h * 16 : 80 + h * 16] = rows.astype(jnp.bfloat16)
        return carry

    lax.fori_loop(0, groups // batch, group, 0)


def slot_kernel(scale, asked_ref, place_ref, parts_ref, got_ref, out_ref, tile_ref):
    total = parts_ref[0].astype(jnp.float32)
    for z in range(1, parts_ref.shape[0]):
        total = total + parts_ref[z].astype(jnp.float32)
    kernel = (total * scale).astype(jnp.bfloat16)
    u, v = iota((128, 128), 0), iota((128, 128), 1)
    same = u // MAXBF == v // MAXBF
    folds = [jnp.where(v == 96 + c * 16 + u % 16, 1.0, 0.0).astype(jnp.bfloat16) for c in range(2)]
    u, v = iota((32, 128), 0), iota((32, 128), 1)
    turned = jnp.where(v == 96 + u, jnp.where(u < MAXBF, 1.0, -1.0), 0.0).astype(jnp.bfloat16)

    def coef(e):
        at = pl.multiple_of(64 + (asked_ref[e] % 2) * MAXBF, MAXBF)
        return got_ref[asked_ref[e] // 2, pl.ds(at, MAXBF)]

    for h in range(2):
        block = kernel[h * 32 : (h + 1) * 32]
        first = jnp.zeros((128, 128), jnp.float32)
        for c in range(2):
            tile = block[c * MAXBF : (c + 1) * MAXBF].astype(jnp.float32)
            wide = jnp.where(same, jnp.concatenate([tile] * 8, axis=0), 0.0)
            first = first + dot(wide.astype(jnp.bfloat16), folds[c])
        first = first.astype(jnp.bfloat16)
        second = dot_tn(block, turned).astype(jnp.bfloat16)
        for j in range(8):
            pair, rows = h * 8 + j, slice(j * MAXBF, (j + 1) * MAXBF)
            at = pair * MAXBF
            tile_ref[at : at + MAXBF] = first[rows] + coef(2 * pair + 1)
            tile_ref[256 + at : 256 + at + MAXBF] = second[rows] + coef(2 * pair)
    tile_ref[512:528] = jnp.zeros((MAXBF, 128), jnp.bfloat16)
    for s in range(2 * out_ref.shape[0]):
        rows = tile_ref[pl.ds(pl.multiple_of(place_ref[s], MAXBF), MAXBF)]
        out_ref[s // 2, (s % 2) * MAXBF : (s % 2 + 1) * MAXBF] = rows


def gain_kernel(table_ref, slot_ref, out_ref, sum_ref, turned_ref):
    groups, rows, _ = slot_ref.shape
    width, bas_dev = out_ref.shape
    half = width // 2
    u, v = iota((128, 128), 0), iota((128, 128), 1)
    turn = jnp.where((v < half) & (u == v + half), -1.0, 0.0)
    turn = jnp.where((v >= half) & (v < width) & (u == v - half), 1.0, turn).astype(jnp.bfloat16)
    turned = dot(slot_ref[...].reshape(groups * rows, 128), turn).astype(jnp.bfloat16)
    turned_ref[...] = turned.reshape(groups, rows, 128)
    sum_ref[...] = jnp.zeros(sum_ref.shape, jnp.float32)
    lane, row_id = iota((MAXBF, 128), 1), iota((MAXBF, 128), 0)
    for g in range(groups):
        slots = slot_ref[g]
        wide = slots.astype(jnp.float32)
        tiles = []
        for r in range(2):
            tile = wide[r * MAXBF : (r + 1) * MAXBF]
            real = jnp.where(lane // MAXBF == r, pltpu.roll(tile, 32 + 16 * r, 1), 0.0)
            imag = jnp.where(lane // MAXBF == 2 + r, pltpu.roll(tile, 48 + 16 * r, 1), 0.0)
            tiles.append(real + imag)
        tiles = jnp.concatenate(tiles, axis=0)[:, 0:64].astype(jnp.bfloat16)
        gains = dot(tiles, jnp.concatenate([slots, turned_ref[g]], axis=0))
        for r in range(2):
            part = gains[r * MAXBF : (r + 1) * MAXBF]
            part = jnp.where(row_id < table_ref[2 + r, g], part, 0.0)
            where = pl.ds(table_ref[r, g], MAXBF)
            sum_ref[where] = sum_ref[where] + part
    out_ref[...] = sum_ref[0:bas_dev].T[0:width]


def vmem_spec():
    return pl.BlockSpec(memory_space=pltpu.VMEM)


def smem_spec():
    return pl.BlockSpec(memory_space=pltpu.SMEM)


def limit(mib):
    return pltpu.CompilerParams(vmem_limit_bytes=mib * MIB)


def in_hbm(array):
    return pltpu.with_memory_space_constraint(array, pltpu.HBM)


def stage(part, own, *fetched):
    shapes = [fetched[0].shape, own.shape, (2, 256, 256), (256, 256), (8, 128)]
    shapes.append((own.shape[0], 128))
    return pl.pallas_call(
        stage_kernel,
        in_specs=[smem_spec(), vmem_spec()]
        + [pl.BlockSpec(memory_space=pltpu.HBM)] * len(fetched),
        out_specs=[vmem_spec()] * len(shapes),
        out_shape=[pltpu.VMEM(shape, jnp.bfloat16) for shape in shapes],
        scratch_shapes=[pltpu.VMEM(x.shape, x.dtype) for x in fetched[1:]]
        + [pltpu.VMEM((8, 128), jnp.float32), pltpu.SemaphoreType.DMA((len(fetched),))],
        compiler_params=limit(16),
        cost_estimate=pl.CostEstimate(flops=1 << 28, bytes_accessed=5 * MIB, transcendentals=0),
        name="stage",
    )(part, own, *[in_hbm(x) for x in fetched])


def fit(odd, near, far, window_rows, ints, order, mix, meta):
    aux_dev, bas_dev, window = ints.shape
    width = near.shape[1]
    blocks = bas_dev // ROWBLK
    shape = (4 * aux_dev, blocks * PACKED + 8, 128)
    return pl.pallas_call(
        fit_kernel,
        in_specs=[smem_spec()] + [vmem_spec()] * 7,
        out_specs=vmem_spec(),
        out_shape=jax.ShapeDtypeStruct(shape, jnp.bfloat16),
        scratch_shapes=[pltpu.VMEM((window, width), jnp.bfloat16)],
        compiler_params=limit(32),
        cost_estimate=pl.CostEstimate(
            flops=2 * aux_dev * bas_dev * width * (window + 256),
            bytes_accessed=6 * MIB,
            transcendentals=0,
        ),
        name="fit",
    )(odd, near, far, window_rows, ints, order, mix, meta)


def pair_sums(me, coef, got):
    groups = got.shape[0]
    rows = groups * (got.shape[1] // PACKED) * ROWBLK + MAXBF
    shape = (groups, 6 * MAXBF, 128)
    return pl.pallas_call(
        pair_kernel,
        in_specs=[smem_spec(), vmem_spec(), vmem_spec()],
        out_specs=[vmem_spec()] * 2,
        out_shape=[
            jax.ShapeDtypeStruct((8, 128), jnp.int32),
            jax.ShapeDtypeStruct(shape, jnp.bfloat16),
        ],
        scratch_shapes=[
            pltpu.VMEM((rows, 128), jnp.float32),
            pltpu.VMEM((rows, 128), jnp.float32),
            pltpu.VMEM((coef.shape[0] + MAXBF, 128), jnp.float32),
            pltpu.VMEM((groups, 128), jnp.int32),
            pltpu.VMEM((groups, 128), jnp.float32),
            pltpu.VMEM((groups, 128), jnp.float32),
            pltpu.VMEM((groups, 128), jnp.float32),
            pltpu.SMEM((groups, 128), jnp.int32),
            pltpu.SemaphoreType.DMA,
        ]
        + [pltpu.VMEM((256, 256), jnp.bfloat16), pltpu.VMEM((128, 256), jnp.bfloat16)] * (2 * BATCH),
        compiler_params=limit(40),
        name="pair_sums",
    )(me, coef, got)


def make_slots(scale, asked, places, parts, got):
    def body(*refs):
        slot_kernel(scale, *refs)

    return pl.pallas_call(
        body,
        in_specs=[smem_spec()] * 2 + [vmem_spec()] * 2,
        out_specs=vmem_spec(),
        out_shape=jax.ShapeDtypeStruct((got.shape[0], 2 * MAXBF, 128), jnp.bfloat16),
        scratch_shapes=[pltpu.VMEM((528, 128), jnp.bfloat16)],
        compiler_params=limit(16),
        name="make_slots",
    )(asked, places, parts, got)


def add_gains(table, slots, width, bas_dev):
    return pl.pallas_call(
        gain_kernel,
        in_specs=[smem_spec(), vmem_spec()],
        out_specs=vmem_spec(),
        out_shape=jax.ShapeDtypeStruct((width, bas_dev), jnp.float32),
        scratch_shapes=[
            pltpu.VMEM((bas_dev + MAXBF, 128), jnp.float32),
            pltpu.VMEM(slots.shape, jnp.bfloat16),
        ],
        compiler_params=limit(16),
        name="add_gains",
    )(table, slots)


def pick(hit, values):
    return jnp.sum(jnp.where(hit, values, 0), axis=-1)


def per_device(integrals, coeffs, metric, atom_sizes, pair_device, pair_atom):
    aux_dev, bas_dev, window = integrals.shape
    occ = coeffs.shape[2]
    groups = lax.axis_size("atom")
    aux_count = lax.axis_size("aux")
    occ_part = occ // aux_count
    ref_count = pair_atom.shape[0]
    halo = (window - bas_dev) // 2
    scale = 1.0 / math.sqrt(2 * occ * aux_dev * aux_count * MAXBF)
    me = lax.axis_index("atom")

    own = coeffs.reshape(bas_dev, 2 * occ)
    odd = lax.axis_index("atom") % 2
    inner = range(1, groups - 1)
    far = lax.dynamic_slice_in_dim(own, odd * halo, halo, 0)
    far = lax.ppermute(far, "atom", [(i, i + 1 if i % 2 else i - 1) for i in inner])
    near = lax.dynamic_slice_in_dim(own, (1 - odd) * halo, halo, 0)
    near = lax.ppermute(near, "atom", [(i, i ^ 1) for i in range(groups)])

    part = jnp.full((1,), lax.axis_index("aux"), jnp.int32)
    ints, window_rows, columns, mix, meta, coef_part = stage(
        part, own, integrals, metric, atom_sizes, pair_device.T, pair_atom[None]
    )
    me = jnp.full((1,), lax.axis_index("atom"), jnp.int32)

    targets = pair_device[:, 0]
    order = jnp.arange(ref_count, dtype=jnp.int32)
    earlier = (targets[:, None] == targets[None, :]) & (order[None, :] < order[:, None])
    ranks = jnp.sum(earlier.astype(jnp.int32), axis=1)
    asked = targets * 2 + ranks
    place = (order % 2) * 256 + (order // 2) * MAXBF
    asked_hit = asked[None, :] == jnp.arange(2 * groups, dtype=jnp.int32)[:, None]
    places = 512 + pick(asked_hit, place[None, :] - 512)

    near, far, me, coef_part, asked, places = lax.optimization_barrier(
        (near, far, me, coef_part, asked, places)
    )
    odd = jnp.full((1,), odd, jnp.int32)
    packed = fit(odd, near, far, window_rows, ints, columns, mix, meta)
    got = lax.all_to_all(packed, "atom", split_axis=0, concat_axis=0, tiled=True)
    table, sent = pair_sums(me, coef_part, got)
    owned = lax.all_to_all(sent, "atom", split_axis=0, concat_axis=0, tiled=True)
    own_sums = jnp.sum(owned[:, : 4 * MAXBF].astype(jnp.float32), axis=0).astype(jnp.bfloat16)
    shared = jnp.broadcast_to(own_sums[None], (aux_count,) + own_sums.shape)
    parts = lax.all_to_all(shared, "aux", split_axis=0, concat_axis=0, tiled=True)
    slots = make_slots(scale, asked, places, parts, owned)
    slots = lax.all_to_all(slots, "atom", split_axis=0, concat_axis=0, tiled=True)
    result = add_gains(table, slots, 2 * occ_part, bas_dev)
    return result.reshape(2, occ_part, bas_dev).transpose(2, 0, 1)


def solution(mesh):
    placed = (
        P("aux", "atom", None),
        P("atom", None, None),
        P("aux", None),
        P("atom", None),
        P("atom", None),
        P("atom"),
    )
    return jax.shard_map(
        per_device, mesh=mesh, in_specs=placed, out_specs=P("atom", None, "aux"), check_vma=False
    )
```

```python
import math

import jax
import jax.numpy as jnp
from jax import lax
from jax.experimental import pallas as pl
from jax.experimental.pallas import tpu as pltpu
from jax.sharding import PartitionSpec as P

MAXBF = 16
ROWBLK = 32
PACKED = ROWBLK + ROWBLK // 2
BATCH = 16
MIB = 1 << 20


def iota(shape, dim):
    return lax.broadcasted_iota(jnp.int32, shape, dim)


def dot(a, b):
    return jnp.dot(a, b, preferred_element_type=jnp.float32)


def dot_nt(a, b):
    return lax.dot_general(a, b, (((1,), (1,)), ((), ())), preferred_element_type=jnp.float32)


def dot_tn(a, b):
    return lax.dot_general(a, b, (((0,), (0,)), ((), ())), preferred_element_type=jnp.float32)


def ordered(part_ref, order_ref, window_ref, at):
    rows = part_ref.shape[0]
    half = part_ref.shape[1] // 2
    for t in range(3):
        real = part_ref[:, t * 128 : (t + 1) * 128]
        imag = part_ref[:, half + t * 128 : half + (t + 1) * 128]
        value = dot(jnp.concatenate([real, imag], axis=1), order_ref[t // 2])
        place = pl.ds(at if isinstance(at, int) else pl.multiple_of(at, 128), rows)
        window_ref[place, t * 256 : (t + 1) * 256] = value.astype(jnp.bfloat16)


def stage_kernel(
    part_ref, own_ref, ints_hbm, metric_hbm, size_hbm, dev_hbm, atom_hbm,
    ints_ref, window_ref, order_ref, mix_ref, meta_ref, coef_ref,
    metric_ref, size_ref, dev_ref, atom_ref, rows_ref, sem_ref,
):
    sources = (ints_hbm, metric_hbm, size_hbm, dev_hbm, atom_hbm)
    targets = (ints_ref, metric_ref, size_ref, dev_ref, atom_ref)
    fetches = [
        pltpu.make_async_copy(a, b, sem_ref.at[i]) for i, (a, b) in enumerate(zip(sources, targets))
    ]
    for fetch in fetches:
        fetch.start()
    u, v = iota((256, 256), 0), iota((256, 256), 1)
    main_order = u == ((v % 128) // 64) * 128 + (v // 128) * 64 + v % 64
    side_order = u == ((v % 64) // 32) * 128 + (v // 64) * 32 + v % 32
    order_ref[0] = jnp.where(main_order, 1.0, 0.0).astype(jnp.bfloat16)
    order_ref[1] = jnp.where(side_order, 1.0, 0.0).astype(jnp.bfloat16)
    ordered(own_ref, order_ref, window_ref, 0)
    width = own_ref.shape[1]
    part = width // 16
    row, lane = iota((width, 128), 0), iota((width, 128), 1)
    source = part_ref[0] * part + jnp.where(lane < part, lane, lane + width // 2 - part)
    chosen = jnp.where((row == source) & (lane < 2 * part), 1.0, 0.0).astype(jnp.bfloat16)
    coef_ref[...] = dot(own_ref[...], chosen).astype(jnp.bfloat16)
    for fetch in fetches[1:]:
        fetch.wait()
    member = iota((256, 8), 0) // ROWBLK == iota((256, 8), 1)
    member = jnp.where(member, 1.0, 0.0).astype(jnp.bfloat16)
    mix = dot_nt(dot_nt(member, metric_ref[...]).astype(jnp.bfloat16), member)
    mix_ref[...] = jnp.where(u % ROWBLK == v % ROWBLK, mix, 0.0).astype(jnp.bfloat16)
    rows_ref[...] = jnp.zeros(rows_ref.shape, jnp.float32)
    for row, value_ref in enumerate((size_ref, dev_ref, atom_ref)):
        rows_ref[row : row + 1, 0 : value_ref.shape[1]] = value_ref[...].astype(jnp.float32)
    meta_ref[...] = rows_ref[...].astype(jnp.bfloat16)
    fetches[0].wait()


def fit_kernel(
    odd_ref, near_ref, far_ref, own_ref, ints_ref, order_ref, mix_ref, meta_ref, out_ref,
    window_ref,
):
    aux_dev, bas_dev, span = ints_ref.shape
    blocks = bas_dev // ROWBLK
    halo = near_ref.shape[0]
    far_at = odd_ref[0] * (halo + bas_dev)
    ordered(near_ref, order_ref, window_ref, halo + bas_dev - far_at)
    window_ref[halo : halo + bas_dev] = own_ref[...]
    ordered(far_ref, order_ref, window_ref, far_at)
    mix = mix_ref[...]
    left = iota((ROWBLK // 2, 128), 1) < 64
    for u in range(blocks):
        if u % 4 == 0:
            ints = ints_ref[:, u * ROWBLK : (u + 4) * ROWBLK].reshape(-1, span)
            wide = dot(ints, window_ref[...]).astype(jnp.bfloat16)
            wide = wide.reshape(aux_dev, 4 * ROWBLK, -1)
        at = (u % 4) * ROWBLK
        half = wide[:, at : at + ROWBLK].reshape(aux_dev * ROWBLK, -1)
        fitted = dot(mix, half)
        main = slice(u * PACKED, u * PACKED + ROWBLK)
        side = slice(u * PACKED + ROWBLK, (u + 1) * PACKED)
        for p in range(aux_dev):
            rows = fitted[p * ROWBLK : (p + 1) * ROWBLK]
            for k in range(4):
                tile = rows[:, k * 128 : (k + 1) * 128]
                out_ref[p * 4 + k, main] = tile.astype(jnp.bfloat16)
            for k in range(2):
                shared = rows[:, 512 + k * 128 : 640 + k * 128]
                top, bottom = shared[: ROWBLK // 2], shared[ROWBLK // 2 :]
                even = jnp.where(left, top, pltpu.roll(bottom, 64, 1))
                odd = jnp.where(left, pltpu.roll(top, 64, 1), bottom)
                out_ref[p * 4 + 2 * k, side] = even.astype(jnp.bfloat16)
                out_ref[p * 4 + 2 * k + 1, side] = odd.astype(jnp.bfloat16)
        if u == blocks - 1:
            for d in range(4 * aux_dev):
                out_ref[d, blocks * PACKED : blocks * PACKED + 8] = meta_ref[...]


def end_table(me, got_ref, size_ref, dev_ref, atom_ref):
    groups, at = got_ref.shape[0], got_ref.shape[1] - 8
    for d in range(groups):
        rows = got_ref[d, at : at + 8].astype(jnp.float32)
        for i, dest in enumerate((size_ref, dev_ref, atom_ref)):
            dest[d : d + 1] = rows[i : i + 1]
    before = jnp.where(iota((128, 128), 0) < iota((128, 128), 1), 1.0, 0.0).astype(jnp.bfloat16)
    sizes = size_ref[...]
    packed = dot(sizes.astype(jnp.bfloat16), before) * 32.0 + sizes
    devices = dev_ref[...].astype(jnp.int32)
    atoms = atom_ref[...].astype(jnp.int32)
    found = jnp.zeros(packed.shape, jnp.float32)
    for d in range(groups):
        row = jnp.broadcast_to(packed[d : d + 1], packed.shape)
        found = jnp.where(devices == d, jnp.take_along_axis(row, atoms, axis=1), found)
    found = found.astype(jnp.int32)
    starts, counts = found // 32, found % 32
    lane = iota(found.shape, 1)
    here = (devices == me) & (lane < 32)
    rank = dot(jnp.where(here, 1.0, 0.0).astype(jnp.bfloat16), before)
    table = jnp.where(lane < 32, devices * 256 + starts, 0)
    for i, value in enumerate((starts, counts)):
        value = value.astype(jnp.float32)
        for r in range(2):
            one = jnp.sum(jnp.where(here & (rank == r), value, 0.0), axis=1, keepdims=True)
            table = jnp.where(lane == 32 + 2 * i + r, one.astype(jnp.int32), table)
    return table


def pair_kernel(
    me_ref, coef_ref, got_ref, slot_ref, out_ref, real_ref, imag_ref, rows_ref, table_ref,
    size_ref, dev_ref, atom_ref, row_ref, table_sem, *sides,
):
    table = end_table(me_ref[0], got_ref, size_ref, dev_ref, atom_ref)
    table_ref[...] = table
    fetch = pltpu.make_async_copy(table_ref, row_ref, table_sem)
    fetch.start()
    groups, blocks = got_ref.shape[0], got_ref.shape[1] // PACKED
    lane = iota((ROWBLK // 2, 128), 1)
    left, valid = lane < 64, lane < 96

    def unpack(b, carry):
        for i in range(blocks):
            base = pl.multiple_of(b * (blocks * ROWBLK) + i * ROWBLK, ROWBLK)
            shared = got_ref[b, i * PACKED + ROWBLK : (i + 1) * PACKED].astype(jnp.float32)
            for h in range(2):
                at = i * PACKED + h * 16
                main = got_ref[b, at : at + 16].astype(jnp.float32)
                real = shared if h else pltpu.roll(shared, 64, 1)
                imag = pltpu.roll(shared, 96 if h else 32, 1)
                real = jnp.where(left, main, jnp.where(valid, real, 0.0))
                imag = jnp.where(left, pltpu.roll(main, 64, 1), jnp.where(valid, imag, 0.0))
                real_ref[pl.ds(base + h * 16, 16)] = real
                imag_ref[pl.ds(base + h * 16, 16)] = imag
        return carry

    lax.fori_loop(0, groups, unpack, 0, unroll=8)
    tail = groups * blocks * ROWBLK
    real_ref[tail : tail + MAXBF] = jnp.zeros((MAXBF, 128), jnp.float32)
    imag_ref[tail : tail + MAXBF] = jnp.zeros((MAXBF, 128), jnp.float32)
    bas_dev = coef_ref.shape[0]
    rows_ref[...] = jnp.zeros(rows_ref.shape, jnp.float32)
    rows_ref[0:bas_dev] = coef_ref[...].astype(jnp.float32)
    row_id = iota((MAXBF, 128), 0)
    lane_pair = lane // MAXBF
    batch = len(sides) // 4
    slot_ref[...] = jnp.zeros(slot_ref.shape, jnp.int32)
    slot_ref[:, 0:groups] = table.astype(jnp.float32).T[32:40].astype(jnp.int32)
    fetch.wait()

    def group(step, carry):
        for u in range(batch):
            g = step * batch + u
            for h in range(2):
                first_ref, second_ref = sides[u * 4 + h * 2], sides[u * 4 + h * 2 + 1]
                for j in range(16):
                    row = pl.ds(row_ref[g, h * 16 + j], 16)
                    place = (j // 2) * MAXBF
                    real, imag = real_ref[row], imag_ref[row]
                    if j % 2:
                        second_ref[place : place + 16, 0:128] = real.astype(jnp.bfloat16)
                        second_ref[place : place + 16, 128:256] = imag.astype(jnp.bfloat16)
                    else:
                        first_ref[place : place + 16, 0:128] = real.astype(jnp.bfloat16)
                        first_ref[place : place + 16, 128:256] = imag.astype(jnp.bfloat16)
                        place += 128
                        first_ref[place : place + 16, 0:128] = imag.astype(jnp.bfloat16)
                        first_ref[place : place + 16, 128:256] = (-real).astype(jnp.bfloat16)
                value = dot_nt(first_ref[...], second_ref[...])
                for c in range(2):
                    part = value[c * 128 : c * 128 + 16]
                    for j in range(1, 8):
                        here = value[c * 128 + j * 16 : c * 128 + j * 16 + 16]
                        part = jnp.where(lane_pair == j, here, part)
                    at = h * 32 + c * 16
                    out_ref[g, at : at + 16] = part.astype(jnp.bfloat16)
            rows = []
            for r in range(2):
                value = rows_ref[pl.ds(row_ref[g, 32 + r], MAXBF)]
                rows.append(jnp.where(row_id < row_ref[g, 34 + r], value, 0.0))
            rest = pltpu.roll(rows[1], 96, 1)
            out_ref[g, 64:80] = jnp.where(valid, rows[0], rest).astype(jnp.bfloat16)
            rest = jnp.where(left[0:8], rest[0:8], pltpu.roll(rest[8:16], 64, 1))
            out_ref[g, 80:88] = rest.astype(jnp.bfloat16)
        return carry

    lax.fori_loop(0, groups // batch, group, 0)


def slot_kernel(scale, asked_ref, place_ref, parts_ref, got_ref, out_ref, tile_ref):
    total = parts_ref[0].astype(jnp.float32)
    for z in range(1, parts_ref.shape[0]):
        total = total + parts_ref[z].astype(jnp.float32)
    kernel = (total * scale).astype(jnp.bfloat16)
    u, v = iota((128, 128), 0), iota((128, 128), 1)
    same = u // MAXBF == v // MAXBF
    folds = [jnp.where(v == 96 + c * 16 + u % 16, 1.0, 0.0).astype(jnp.bfloat16) for c in range(2)]
    u, v = iota((32, 128), 0), iota((32, 128), 1)
    turned = jnp.where(v == 96 + u, jnp.where(u < MAXBF, 1.0, -1.0), 0.0).astype(jnp.bfloat16)

    lane = iota((MAXBF, 128), 1)

    def coef(e):
        source = asked_ref[e] // 2
        rows = got_ref[source, 64:80].astype(jnp.float32)
        rest = got_ref[source, 80:88].astype(jnp.float32)
        rest = jnp.concatenate([rest, pltpu.roll(rest, 64, 1)], axis=0)
        second = jnp.where(lane < 64, rest, jnp.where(lane < 96, 0.0, rows))
        second = pltpu.roll(second, 32, 1)
        first = jnp.where(lane < 96, rows, 0.0)
        return jnp.where(asked_ref[e] % 2 == 1, second, first)

    for h in range(2):
        block = kernel[h * 32 : (h + 1) * 32]
        first = jnp.zeros((128, 128), jnp.float32)
        for c in range(2):
            tile = block[c * MAXBF : (c + 1) * MAXBF].astype(jnp.float32)
            wide = jnp.where(same, jnp.concatenate([tile] * 8, axis=0), 0.0)
            first = first + dot(wide.astype(jnp.bfloat16), folds[c])
        second = dot_tn(block, turned)
        for j in range(8):
            pair, rows = h * 8 + j, slice(j * MAXBF, (j + 1) * MAXBF)
            at = pair * MAXBF
            tile = first[rows] + coef(2 * pair + 1)
            tile_ref[at : at + MAXBF] = tile.astype(jnp.bfloat16)
            tile = second[rows] + coef(2 * pair)
            tile_ref[256 + at : 256 + at + MAXBF] = tile.astype(jnp.bfloat16)
    tile_ref[512:528] = jnp.zeros((MAXBF, 128), jnp.bfloat16)
    for s in range(2 * out_ref.shape[0]):
        rows = tile_ref[pl.ds(pl.multiple_of(place_ref[s], MAXBF), MAXBF)]
        out_ref[s // 2, (s % 2) * MAXBF : (s % 2 + 1) * MAXBF] = rows


def gain_kernel(table_ref, slot_ref, out_ref, sum_ref, turned_ref):
    groups, rows, _ = slot_ref.shape
    width, bas_dev = out_ref.shape
    half = width // 2
    u, v = iota((128, 128), 0), iota((128, 128), 1)
    turn = jnp.where((v < half) & (u == v + half), -1.0, 0.0)
    turn = jnp.where((v >= half) & (v < width) & (u == v - half), 1.0, turn).astype(jnp.bfloat16)
    turned = dot(slot_ref[...].reshape(groups * rows, 128), turn).astype(jnp.bfloat16)
    turned_ref[...] = turned.reshape(groups, rows, 128)
    sum_ref[...] = jnp.zeros(sum_ref.shape, jnp.float32)
    lane, row_id = iota((MAXBF, 128), 1), iota((MAXBF, 128), 0)
    for g in range(groups):
        slots = slot_ref[g]
        wide = slots.astype(jnp.float32)
        tiles = []
        for r in range(2):
            tile = wide[r * MAXBF : (r + 1) * MAXBF]
            real = jnp.where(lane // MAXBF == r, pltpu.roll(tile, 32 + 16 * r, 1), 0.0)
            imag = jnp.where(lane // MAXBF == 2 + r, pltpu.roll(tile, 48 + 16 * r, 1), 0.0)
            tiles.append(real + imag)
        tiles = jnp.concatenate(tiles, axis=0)[:, 0:64].astype(jnp.bfloat16)
        gains = dot(tiles, jnp.concatenate([slots, turned_ref[g]], axis=0))
        for r in range(2):
            part = gains[r * MAXBF : (r + 1) * MAXBF]
            part = jnp.where(row_id < table_ref[2 + r, g], part, 0.0)
            where = pl.ds(table_ref[r, g], MAXBF)
            sum_ref[where] = sum_ref[where] + part
    out_ref[...] = sum_ref[0:bas_dev].T[0:width]


def vmem_spec():
    return pl.BlockSpec(memory_space=pltpu.VMEM)


def smem_spec():
    return pl.BlockSpec(memory_space=pltpu.SMEM)


def limit(mib):
    return pltpu.CompilerParams(vmem_limit_bytes=mib * MIB)


def in_hbm(array):
    return pltpu.with_memory_space_constraint(array, pltpu.HBM)


def stage(part, own, *fetched):
    shapes = [fetched[0].shape, own.shape, (2, 256, 256), (256, 256), (8, 128)]
    shapes.append((own.shape[0], 128))
    return pl.pallas_call(
        stage_kernel,
        in_specs=[smem_spec(), vmem_spec()]
        + [pl.BlockSpec(memory_space=pltpu.HBM)] * len(fetched),
        out_specs=[vmem_spec()] * len(shapes),
        out_shape=[pltpu.VMEM(shape, jnp.bfloat16) for shape in shapes],
        scratch_shapes=[pltpu.VMEM(x.shape, x.dtype) for x in fetched[1:]]
        + [pltpu.VMEM((8, 128), jnp.float32), pltpu.SemaphoreType.DMA((len(fetched),))],
        compiler_params=limit(16),
        cost_estimate=pl.CostEstimate(flops=1 << 28, bytes_accessed=5 * MIB, transcendentals=0),
        name="stage",
    )(part, own, *[in_hbm(x) for x in fetched])


def fit(odd, near, far, window_rows, ints, order, mix, meta):
    aux_dev, bas_dev, window = ints.shape
    width = near.shape[1]
    blocks = bas_dev // ROWBLK
    shape = (4 * aux_dev, blocks * PACKED + 8, 128)
    return pl.pallas_call(
        fit_kernel,
        in_specs=[smem_spec()] + [vmem_spec()] * 7,
        out_specs=vmem_spec(),
        out_shape=jax.ShapeDtypeStruct(shape, jnp.bfloat16),
        scratch_shapes=[pltpu.VMEM((window, width), jnp.bfloat16)],
        compiler_params=limit(32),
        cost_estimate=pl.CostEstimate(
            flops=2 * aux_dev * bas_dev * width * (window + 256),
            bytes_accessed=6 * MIB,
            transcendentals=0,
        ),
        name="fit",
    )(odd, near, far, window_rows, ints, order, mix, meta)


def pair_sums(me, coef, got):
    groups = got.shape[0]
    rows = groups * (got.shape[1] // PACKED) * ROWBLK + MAXBF
    shape = (groups, 88, 128)
    return pl.pallas_call(
        pair_kernel,
        in_specs=[smem_spec(), vmem_spec(), vmem_spec()],
        out_specs=[vmem_spec()] * 2,
        out_shape=[
            jax.ShapeDtypeStruct((8, 128), jnp.int32),
            jax.ShapeDtypeStruct(shape, jnp.bfloat16),
        ],
        scratch_shapes=[
            pltpu.VMEM((rows, 128), jnp.float32),
            pltpu.VMEM((rows, 128), jnp.float32),
            pltpu.VMEM((coef.shape[0] + MAXBF, 128), jnp.float32),
            pltpu.VMEM((groups, 128), jnp.int32),
            pltpu.VMEM((groups, 128), jnp.float32),
            pltpu.VMEM((groups, 128), jnp.float32),
            pltpu.VMEM((groups, 128), jnp.float32),
            pltpu.SMEM((groups, 128), jnp.int32),
            pltpu.SemaphoreType.DMA,
        ]
        + [pltpu.VMEM((256, 256), jnp.bfloat16), pltpu.VMEM((128, 256), jnp.bfloat16)] * (2 * BATCH),
        compiler_params=limit(40),
        name="pair_sums",
    )(me, coef, got)


def make_slots(scale, asked, places, parts, got):
    def body(*refs):
        slot_kernel(scale, *refs)

    return pl.pallas_call(
        body,
        in_specs=[smem_spec()] * 2 + [vmem_spec()] * 2,
        out_specs=vmem_spec(),
        out_shape=jax.ShapeDtypeStruct((got.shape[0], 2 * MAXBF, 128), jnp.bfloat16),
        scratch_shapes=[pltpu.VMEM((528, 128), jnp.bfloat16)],
        compiler_params=limit(16),
        name="make_slots",
    )(asked, places, parts, got)


def add_gains(table, slots, width, bas_dev):
    return pl.pallas_call(
        gain_kernel,
        in_specs=[smem_spec(), vmem_spec()],
        out_specs=vmem_spec(),
        out_shape=jax.ShapeDtypeStruct((width, bas_dev), jnp.float32),
        scratch_shapes=[
            pltpu.VMEM((bas_dev + MAXBF, 128), jnp.float32),
            pltpu.VMEM(slots.shape, jnp.bfloat16),
        ],
        compiler_params=limit(16),
        name="add_gains",
    )(table, slots)


def pick(hit, values):
    return jnp.sum(jnp.where(hit, values, 0), axis=-1)


def per_device(integrals, coeffs, metric, atom_sizes, pair_device, pair_atom):
    aux_dev, bas_dev, window = integrals.shape
    occ = coeffs.shape[2]
    groups = lax.axis_size("atom")
    aux_count = lax.axis_size("aux")
    occ_part = occ // aux_count
    ref_count = pair_atom.shape[0]
    halo = (window - bas_dev) // 2
    scale = 1.0 / math.sqrt(2 * occ * aux_dev * aux_count * MAXBF)
    me = lax.axis_index("atom")

    own = coeffs.reshape(bas_dev, 2 * occ)
    odd = lax.axis_index("atom") % 2
    inner = range(1, groups - 1)
    far = lax.dynamic_slice_in_dim(own, odd * halo, halo, 0)
    far = lax.ppermute(far, "atom", [(i, i + 1 if i % 2 else i - 1) for i in inner])
    near = lax.dynamic_slice_in_dim(own, (1 - odd) * halo, halo, 0)
    near = lax.ppermute(near, "atom", [(i, i ^ 1) for i in range(groups)])

    part = jnp.full((1,), lax.axis_index("aux"), jnp.int32)
    ints, window_rows, columns, mix, meta, coef_part = stage(
        part, own, integrals, metric, atom_sizes, pair_device.T, pair_atom[None]
    )
    me = jnp.full((1,), lax.axis_index("atom"), jnp.int32)

    targets = pair_device[:, 0]
    order = jnp.arange(ref_count, dtype=jnp.int32)
    earlier = (targets[:, None] == targets[None, :]) & (order[None, :] < order[:, None])
    ranks = jnp.sum(earlier.astype(jnp.int32), axis=1)
    asked = targets * 2 + ranks
    place = (order % 2) * 256 + (order // 2) * MAXBF
    asked_hit = asked[None, :] == jnp.arange(2 * groups, dtype=jnp.int32)[:, None]
    places = 512 + pick(asked_hit, place[None, :] - 512)

    near, far, me, coef_part, asked, places = lax.optimization_barrier(
        (near, far, me, coef_part, asked, places)
    )
    odd = jnp.full((1,), odd, jnp.int32)
    packed = fit(odd, near, far, window_rows, ints, columns, mix, meta)
    got = lax.all_to_all(packed, "atom", split_axis=0, concat_axis=0, tiled=True)
    table, sent = pair_sums(me, coef_part, got)
    owned = lax.all_to_all(sent, "atom", split_axis=0, concat_axis=0, tiled=True)
    own_sums = jnp.sum(owned[:, : 4 * MAXBF].astype(jnp.float32), axis=0).astype(jnp.bfloat16)
    shared = jnp.broadcast_to(own_sums[None], (aux_count,) + own_sums.shape)
    parts = lax.all_to_all(shared, "aux", split_axis=0, concat_axis=0, tiled=True)
    slots = make_slots(scale, asked, places, parts, owned)
    slots = lax.all_to_all(slots, "atom", split_axis=0, concat_axis=0, tiled=True)
    result = add_gains(table, slots, 2 * occ_part, bas_dev)
    return result.reshape(2, occ_part, bas_dev).transpose(2, 0, 1)


def solution(mesh):
    placed = (
        P("aux", "atom", None),
        P("atom", None, None),
        P("aux", None),
        P("atom", None),
        P("atom", None),
        P("atom"),
    )
    return jax.shard_map(
        per_device, mesh=mesh, in_specs=placed, out_specs=P("atom", None, "aux"), check_vma=False
    )
```

```python
import math

import jax
import jax.numpy as jnp
from jax import lax
from jax.experimental import pallas as pl
from jax.experimental.pallas import tpu as pltpu
from jax.sharding import PartitionSpec as P

MAXBF = 16
ROWBLK = 32
PACKED = ROWBLK + ROWBLK // 2
BATCH = 32
MIB = 1 << 20


def iota(shape, dim):
    return lax.broadcasted_iota(jnp.int32, shape, dim)


def dot(a, b):
    return jnp.dot(a, b, preferred_element_type=jnp.float32)


def dot_nt(a, b):
    return lax.dot_general(a, b, (((1,), (1,)), ((), ())), preferred_element_type=jnp.float32)


def dot_tn(a, b):
    return lax.dot_general(a, b, (((0,), (0,)), ((), ())), preferred_element_type=jnp.float32)


def ordered(part_ref, order_ref, window_ref, at):
    rows = part_ref.shape[0]
    half = part_ref.shape[1] // 2
    for t in range(3):
        real = part_ref[:, t * 128 : (t + 1) * 128]
        imag = part_ref[:, half + t * 128 : half + (t + 1) * 128]
        value = dot(jnp.concatenate([real, imag], axis=1), order_ref[t // 2])
        place = pl.ds(at if isinstance(at, int) else pl.multiple_of(at, 128), rows)
        window_ref[place, t * 256 : (t + 1) * 256] = value.astype(jnp.bfloat16)


def stage_kernel(
    part_ref, own_ref, ints_hbm, metric_hbm, size_hbm, dev_hbm, atom_hbm,
    half_ref, ints_ref, order_ref, mix_ref, meta_ref, coef_ref,
    window_ref, metric_ref, size_ref, dev_ref, atom_ref, rows_ref, sem_ref,
):
    sources = (ints_hbm, metric_hbm, size_hbm, dev_hbm, atom_hbm)
    targets = (ints_ref, metric_ref, size_ref, dev_ref, atom_ref)
    fetches = [
        pltpu.make_async_copy(a, b, sem_ref.at[i]) for i, (a, b) in enumerate(zip(sources, targets))
    ]
    for fetch in fetches:
        fetch.start()
    u, v = iota((256, 256), 0), iota((256, 256), 1)
    main_order = u == ((v % 128) // 64) * 128 + (v // 128) * 64 + v % 64
    side_order = u == ((v % 64) // 32) * 128 + (v // 64) * 32 + v % 32
    order_ref[0] = jnp.where(main_order, 1.0, 0.0).astype(jnp.bfloat16)
    order_ref[1] = jnp.where(side_order, 1.0, 0.0).astype(jnp.bfloat16)
    ordered(own_ref, order_ref, window_ref, 0)
    width = own_ref.shape[1]
    part = width // 16
    row, lane = iota((width, 128), 0), iota((width, 128), 1)
    source = part_ref[0] * part + jnp.where(lane < part, lane, lane + width // 2 - part)
    chosen = jnp.where((row == source) & (lane < 2 * part), 1.0, 0.0).astype(jnp.bfloat16)
    coef_ref[...] = dot(own_ref[...], chosen).astype(jnp.bfloat16)
    for fetch in fetches[1:]:
        fetch.wait()
    member = iota((256, 8), 0) // ROWBLK == iota((256, 8), 1)
    member = jnp.where(member, 1.0, 0.0).astype(jnp.bfloat16)
    mix = dot_nt(dot_nt(member, metric_ref[...]).astype(jnp.bfloat16), member)
    mix_ref[...] = jnp.where(u % ROWBLK == v % ROWBLK, mix, 0.0).astype(jnp.bfloat16)
    rows_ref[...] = jnp.zeros(rows_ref.shape, jnp.float32)
    for row, value_ref in enumerate((size_ref, dev_ref, atom_ref)):
        rows_ref[row : row + 1, 0 : value_ref.shape[1]] = value_ref[...].astype(jnp.float32)
    meta_ref[...] = rows_ref[...].astype(jnp.bfloat16)
    fetches[0].wait()
    aux_dev, bas_dev, span = ints_ref.shape
    halo = (span - bas_dev) // 2
    step = bas_dev // 2
    for u in range(2):
        rows = slice(u * step, (u + 1) * step)
        ints = ints_ref[:, rows, halo : halo + bas_dev].reshape(aux_dev * step, bas_dev)
        half_ref[:, rows] = dot(ints, window_ref[...]).reshape(aux_dev, step, -1)


def fit_kernel(
    odd_ref, near_ref, far_ref, half_ref, ints_ref, order_ref, mix_ref, meta_ref, out_ref,
    window_ref,
):
    aux_dev, bas_dev, span = ints_ref.shape
    blocks = bas_dev // ROWBLK
    halo = near_ref.shape[0]
    far_at = odd_ref[0] * halo
    ordered(near_ref, order_ref, window_ref, halo - far_at)
    ordered(far_ref, order_ref, window_ref, far_at)
    mix = mix_ref[...]
    left = iota((ROWBLK // 2, 128), 1) < 64
    for u in range(blocks):
        if u % 4 == 0:
            rows = slice(u * ROWBLK, (u + 4) * ROWBLK)
            low, high = ints_ref[:, rows, 0:halo], ints_ref[:, rows, span - halo : span]
            ints = jnp.concatenate([low, high], axis=2).reshape(-1, 2 * halo)
            wide = dot(ints, window_ref[...]) + half_ref[:, rows].reshape(ints.shape[0], -1)
            wide = wide.astype(jnp.bfloat16)
            wide = wide.reshape(aux_dev, 4 * ROWBLK, -1)
        at = (u % 4) * ROWBLK
        half = wide[:, at : at + ROWBLK].reshape(aux_dev * ROWBLK, -1)
        fitted = dot(mix, half)
        main = slice(u * PACKED, u * PACKED + ROWBLK)
        side = slice(u * PACKED + ROWBLK, (u + 1) * PACKED)
        for p in range(aux_dev):
            rows = fitted[p * ROWBLK : (p + 1) * ROWBLK]
            for k in range(4):
                tile = rows[:, k * 128 : (k + 1) * 128]
                out_ref[p * 4 + k, main] = tile.astype(jnp.bfloat16)
            for k in range(2):
                shared = rows[:, 512 + k * 128 : 640 + k * 128]
                top, bottom = shared[: ROWBLK // 2], shared[ROWBLK // 2 :]
                even = jnp.where(left, top, pltpu.roll(bottom, 64, 1))
                odd = jnp.where(left, pltpu.roll(top, 64, 1), bottom)
                out_ref[p * 4 + 2 * k, side] = even.astype(jnp.bfloat16)
                out_ref[p * 4 + 2 * k + 1, side] = odd.astype(jnp.bfloat16)
        if u == blocks - 1:
            for d in range(4 * aux_dev):
                out_ref[d, blocks * PACKED : blocks * PACKED + 8] = meta_ref[...]


def end_table(me, got_ref, size_ref, dev_ref, atom_ref):
    groups, at = got_ref.shape[0], got_ref.shape[1] - 8
    for d in range(groups):
        rows = got_ref[d, at : at + 8].astype(jnp.float32)
        for i, dest in enumerate((size_ref, dev_ref, atom_ref)):
            dest[d : d + 1] = rows[i : i + 1]
    before = jnp.where(iota((128, 128), 0) < iota((128, 128), 1), 1.0, 0.0).astype(jnp.bfloat16)
    sizes = size_ref[...]
    packed = dot(sizes.astype(jnp.bfloat16), before) * 32.0 + sizes
    devices = dev_ref[...].astype(jnp.int32)
    atoms = atom_ref[...].astype(jnp.int32)
    found = jnp.zeros(packed.shape, jnp.float32)
    for d in range(groups):
        row = jnp.broadcast_to(packed[d : d + 1], packed.shape)
        found = jnp.where(devices == d, jnp.take_along_axis(row, atoms, axis=1), found)
    found = found.astype(jnp.int32)
    starts, counts = found // 32, found % 32
    lane = iota(found.shape, 1)
    here = (devices == me) & (lane < 32)
    rank = dot(jnp.where(here, 1.0, 0.0).astype(jnp.bfloat16), before)
    table = jnp.where(lane < 32, devices * 256 + starts, 0)
    for i, value in enumerate((starts, counts)):
        value = value.astype(jnp.float32)
        for r in range(2):
            one = jnp.sum(jnp.where(here & (rank == r), value, 0.0), axis=1, keepdims=True)
            table = jnp.where(lane == 32 + 2 * i + r, one.astype(jnp.int32), table)
    return table


def pair_kernel(
    me_ref, coef_ref, got_ref, slot_ref, out_ref, real_ref, imag_ref, rows_ref, table_ref,
    size_ref, dev_ref, atom_ref, row_ref, table_sem, *sides,
):
    table = end_table(me_ref[0], got_ref, size_ref, dev_ref, atom_ref)
    table_ref[...] = table
    fetch = pltpu.make_async_copy(table_ref, row_ref, table_sem)
    fetch.start()
    groups, blocks = got_ref.shape[0], got_ref.shape[1] // PACKED
    lane = iota((ROWBLK // 2, 128), 1)
    left, valid = lane < 64, lane < 96

    def unpack(b, carry):
        for i in range(blocks):
            base = pl.multiple_of(b * (blocks * ROWBLK) + i * ROWBLK, ROWBLK)
            shared = got_ref[b, i * PACKED + ROWBLK : (i + 1) * PACKED].astype(jnp.float32)
            for h in range(2):
                at = i * PACKED + h * 16
                main = got_ref[b, at : at + 16].astype(jnp.float32)
                real = shared if h else pltpu.roll(shared, 64, 1)
                imag = pltpu.roll(shared, 96 if h else 32, 1)
                real = jnp.where(left, main, jnp.where(valid, real, 0.0))
                imag = jnp.where(left, pltpu.roll(main, 64, 1), jnp.where(valid, imag, 0.0))
                real_ref[pl.ds(base + h * 16, 16)] = real
                imag_ref[pl.ds(base + h * 16, 16)] = imag
        return carry

    lax.fori_loop(0, groups, unpack, 0, unroll=16)
    tail = groups * blocks * ROWBLK
    real_ref[tail : tail + MAXBF] = jnp.zeros((MAXBF, 128), jnp.float32)
    imag_ref[tail : tail + MAXBF] = jnp.zeros((MAXBF, 128), jnp.float32)
    bas_dev = coef_ref.shape[0]
    rows_ref[...] = jnp.zeros(rows_ref.shape, jnp.float32)
    rows_ref[0:bas_dev] = coef_ref[...].astype(jnp.float32)
    row_id = iota((MAXBF, 128), 0)
    lane_pair = lane // MAXBF
    batch = len(sides) // 4
    slot_ref[...] = jnp.zeros(slot_ref.shape, jnp.int32)
    slot_ref[:, 0:groups] = table.astype(jnp.float32).T[32:40].astype(jnp.int32)
    fetch.wait()

    def group(step, carry):
        for u in range(batch):
            g = step * batch + u
            for h in range(2):
                first_ref, second_ref = sides[u * 4 + h * 2], sides[u * 4 + h * 2 + 1]
                for j in range(16):
                    row = pl.ds(row_ref[g, h * 16 + j], 16)
                    place = (j // 2) * MAXBF
                    real, imag = real_ref[row], imag_ref[row]
                    if j % 2:
                        second_ref[place : place + 16, 0:128] = real.astype(jnp.bfloat16)
                        second_ref[place : place + 16, 128:256] = imag.astype(jnp.bfloat16)
                    else:
                        first_ref[place : place + 16, 0:128] = real.astype(jnp.bfloat16)
                        first_ref[place : place + 16, 128:256] = imag.astype(jnp.bfloat16)
                        place += 128
                        first_ref[place : place + 16, 0:128] = imag.astype(jnp.bfloat16)
                        first_ref[place : place + 16, 128:256] = (-real).astype(jnp.bfloat16)
                value = dot_nt(first_ref[...], second_ref[...])
                for c in range(2):
                    part = value[c * 128 : c * 128 + 16]
                    for j in range(1, 8):
                        here = value[c * 128 + j * 16 : c * 128 + j * 16 + 16]
                        part = jnp.where(lane_pair == j, here, part)
                    at = h * 32 + c * 16
                    out_ref[g, at : at + 16] = part.astype(jnp.bfloat16)
            rows = []
            for r in range(2):
                value = rows_ref[pl.ds(row_ref[g, 32 + r], MAXBF)]
                rows.append(jnp.where(row_id < row_ref[g, 34 + r], value, 0.0))
            rest = pltpu.roll(rows[1], 96, 1)
            out_ref[g, 64:80] = jnp.where(valid, rows[0], rest).astype(jnp.bfloat16)
            rest = jnp.where(left[0:8], rest[0:8], pltpu.roll(rest[8:16], 64, 1))
            out_ref[g, 80:88] = rest.astype(jnp.bfloat16)
        return carry

    lax.fori_loop(0, groups // batch, group, 0)


def slot_kernel(scale, asked_ref, place_ref, parts_ref, got_ref, out_ref, tile_ref):
    total = parts_ref[0].astype(jnp.float32)
    for z in range(1, parts_ref.shape[0]):
        total = total + parts_ref[z].astype(jnp.float32)
    kernel = (total * scale).astype(jnp.bfloat16)
    u, v = iota((128, 128), 0), iota((128, 128), 1)
    same = u // MAXBF == v // MAXBF
    folds = [jnp.where(v == 96 + c * 16 + u % 16, 1.0, 0.0).astype(jnp.bfloat16) for c in range(2)]
    u, v = iota((32, 128), 0), iota((32, 128), 1)
    turned = jnp.where(v == 96 + u, jnp.where(u < MAXBF, 1.0, -1.0), 0.0).astype(jnp.bfloat16)

    lane = iota((MAXBF, 128), 1)

    def coef(e):
        source = asked_ref[e] // 2
        rows = got_ref[source, 64:80].astype(jnp.float32)
        rest = got_ref[source, 80:88].astype(jnp.float32)
        rest = jnp.concatenate([rest, pltpu.roll(rest, 64, 1)], axis=0)
        second = jnp.where(lane < 64, rest, jnp.where(lane < 96, 0.0, rows))
        second = pltpu.roll(second, 32, 1)
        first = jnp.where(lane < 96, rows, 0.0)
        return jnp.where(asked_ref[e] % 2 == 1, second, first)

    for h in range(2):
        block = kernel[h * 32 : (h + 1) * 32]
        first = jnp.zeros((128, 128), jnp.float32)
        for c in range(2):
            tile = block[c * MAXBF : (c + 1) * MAXBF].astype(jnp.float32)
            wide = jnp.where(same, jnp.concatenate([tile] * 8, axis=0), 0.0)
            first = first + dot(wide.astype(jnp.bfloat16), folds[c])
        second = dot_tn(block, turned)
        for j in range(8):
            pair, rows = h * 8 + j, slice(j * MAXBF, (j + 1) * MAXBF)
            at = pair * MAXBF
            tile = first[rows] + coef(2 * pair + 1)
            tile_ref[at : at + MAXBF] = tile.astype(jnp.bfloat16)
            tile = second[rows] + coef(2 * pair)
            tile_ref[256 + at : 256 + at + MAXBF] = tile.astype(jnp.bfloat16)
    tile_ref[512:528] = jnp.zeros((MAXBF, 128), jnp.bfloat16)
    for s in range(2 * out_ref.shape[0]):
        rows = tile_ref[pl.ds(pl.multiple_of(place_ref[s], MAXBF), MAXBF)]
        out_ref[s // 2, (s % 2) * MAXBF : (s % 2 + 1) * MAXBF] = rows


def gain_kernel(table_ref, slot_ref, out_ref, sum_ref, turned_ref):
    groups, rows, _ = slot_ref.shape
    width, bas_dev = out_ref.shape
    half = width // 2
    u, v = iota((128, 128), 0), iota((128, 128), 1)
    turn = jnp.where((v < half) & (u == v + half), -1.0, 0.0)
    turn = jnp.where((v >= half) & (v < width) & (u == v - half), 1.0, turn).astype(jnp.bfloat16)
    turned = dot(slot_ref[...].reshape(groups * rows, 128), turn).astype(jnp.bfloat16)
    turned_ref[...] = turned.reshape(groups, rows, 128)
    sum_ref[...] = jnp.zeros(sum_ref.shape, jnp.float32)
    lane, row_id = iota((MAXBF, 128), 1), iota((MAXBF, 128), 0)
    for g in range(groups):
        slots = slot_ref[g]
        wide = slots.astype(jnp.float32)
        tiles = []
        for r in range(2):
            tile = wide[r * MAXBF : (r + 1) * MAXBF]
            real = jnp.where(lane // MAXBF == r, pltpu.roll(tile, 32 + 16 * r, 1), 0.0)
            imag = jnp.where(lane // MAXBF == 2 + r, pltpu.roll(tile, 48 + 16 * r, 1), 0.0)
            tiles.append(real + imag)
        tiles = jnp.concatenate(tiles, axis=0)[:, 0:64].astype(jnp.bfloat16)
        gains = dot(tiles, jnp.concatenate([slots, turned_ref[g]], axis=0))
        for r in range(2):
            part = gains[r * MAXBF : (r + 1) * MAXBF]
            part = jnp.where(row_id < table_ref[2 + r, g], part, 0.0)
            where = pl.ds(table_ref[r, g], MAXBF)
            sum_ref[where] = sum_ref[where] + part
    out_ref[...] = sum_ref[0:bas_dev].T[0:width]


def vmem_spec():
    return pl.BlockSpec(memory_space=pltpu.VMEM)


def smem_spec():
    return pl.BlockSpec(memory_space=pltpu.SMEM)


def limit(mib):
    return pltpu.CompilerParams(vmem_limit_bytes=mib * MIB)


def in_hbm(array):
    return pltpu.with_memory_space_constraint(array, pltpu.HBM)


def stage(part, own, *fetched):
    shapes = [fetched[0].shape, (2, 256, 256), (256, 256), (8, 128), (own.shape[0], 128)]
    half = fetched[0].shape[:2] + own.shape[1:]
    return pl.pallas_call(
        stage_kernel,
        in_specs=[smem_spec(), vmem_spec()]
        + [pl.BlockSpec(memory_space=pltpu.HBM)] * len(fetched),
        out_specs=[vmem_spec()] * (len(shapes) + 1),
        out_shape=[pltpu.VMEM(half, jnp.float32)]
        + [pltpu.VMEM(shape, jnp.bfloat16) for shape in shapes],
        scratch_shapes=[pltpu.VMEM(own.shape, jnp.bfloat16)]
        + [pltpu.VMEM(x.shape, x.dtype) for x in fetched[1:]]
        + [pltpu.VMEM((8, 128), jnp.float32), pltpu.SemaphoreType.DMA((len(fetched),))],
        compiler_params=limit(24),
        cost_estimate=pl.CostEstimate(flops=1 << 28, bytes_accessed=5 * MIB, transcendentals=0),
        name="stage",
    )(part, own, *[in_hbm(x) for x in fetched])


def fit(odd, near, far, half, ints, order, mix, meta):
    aux_dev, bas_dev, window = ints.shape
    width = near.shape[1]
    blocks = bas_dev // ROWBLK
    shape = (4 * aux_dev, blocks * PACKED + 8, 128)
    return pl.pallas_call(
        fit_kernel,
        in_specs=[smem_spec()] + [vmem_spec()] * 7,
        out_specs=vmem_spec(),
        out_shape=jax.ShapeDtypeStruct(shape, jnp.bfloat16),
        scratch_shapes=[pltpu.VMEM((window - bas_dev, width), jnp.bfloat16)],
        compiler_params=limit(32),
        cost_estimate=pl.CostEstimate(
            flops=2 * aux_dev * bas_dev * width * (window + 256),
            bytes_accessed=6 * MIB,
            transcendentals=0,
        ),
        name="fit",
    )(odd, near, far, half, ints, order, mix, meta)


def pair_sums(me, coef, got):
    groups = got.shape[0]
    rows = groups * (got.shape[1] // PACKED) * ROWBLK + MAXBF
    shape = (groups, 88, 128)
    return pl.pallas_call(
        pair_kernel,
        in_specs=[smem_spec(), vmem_spec(), vmem_spec()],
        out_specs=[vmem_spec()] * 2,
        out_shape=[
            jax.ShapeDtypeStruct((8, 128), jnp.int32),
            jax.ShapeDtypeStruct(shape, jnp.bfloat16),
        ],
        scratch_shapes=[
            pltpu.VMEM((rows, 128), jnp.float32),
            pltpu.VMEM((rows, 128), jnp.float32),
            pltpu.VMEM((coef.shape[0] + MAXBF, 128), jnp.float32),
            pltpu.VMEM((groups, 128), jnp.int32),
            pltpu.VMEM((groups, 128), jnp.float32),
            pltpu.VMEM((groups, 128), jnp.float32),
            pltpu.VMEM((groups, 128), jnp.float32),
            pltpu.SMEM((groups, 128), jnp.int32),
            pltpu.SemaphoreType.DMA,
        ]
        + [pltpu.VMEM((256, 256), jnp.bfloat16), pltpu.VMEM((128, 256), jnp.bfloat16)] * (2 * BATCH),
        compiler_params=limit(40),
        name="pair_sums",
    )(me, coef, got)


def make_slots(scale, asked, places, parts, got):
    def body(*refs):
        slot_kernel(scale, *refs)

    return pl.pallas_call(
        body,
        in_specs=[smem_spec()] * 2 + [vmem_spec()] * 2,
        out_specs=vmem_spec(),
        out_shape=jax.ShapeDtypeStruct((got.shape[0], 2 * MAXBF, 128), jnp.bfloat16),
        scratch_shapes=[pltpu.VMEM((528, 128), jnp.bfloat16)],
        compiler_params=limit(16),
        name="make_slots",
    )(asked, places, parts, got)


def add_gains(table, slots, width, bas_dev):
    return pl.pallas_call(
        gain_kernel,
        in_specs=[smem_spec(), vmem_spec()],
        out_specs=vmem_spec(),
        out_shape=jax.ShapeDtypeStruct((width, bas_dev), jnp.float32),
        scratch_shapes=[
            pltpu.VMEM((bas_dev + MAXBF, 128), jnp.float32),
            pltpu.VMEM(slots.shape, jnp.bfloat16),
        ],
        compiler_params=limit(16),
        name="add_gains",
    )(table, slots)


def pick(hit, values):
    return jnp.sum(jnp.where(hit, values, 0), axis=-1)


def per_device(integrals, coeffs, metric, atom_sizes, pair_device, pair_atom):
    aux_dev, bas_dev, window = integrals.shape
    occ = coeffs.shape[2]
    groups = lax.axis_size("atom")
    aux_count = lax.axis_size("aux")
    occ_part = occ // aux_count
    ref_count = pair_atom.shape[0]
    halo = (window - bas_dev) // 2
    scale = 1.0 / math.sqrt(2 * occ * aux_dev * aux_count * MAXBF)
    me = lax.axis_index("atom")

    own = coeffs.reshape(bas_dev, 2 * occ)
    odd = lax.axis_index("atom") % 2
    inner = range(1, groups - 1)
    far = lax.dynamic_slice_in_dim(own, odd * halo, halo, 0)
    far = lax.ppermute(far, "atom", [(i, i + 1 if i % 2 else i - 1) for i in inner])
    near = lax.dynamic_slice_in_dim(own, (1 - odd) * halo, halo, 0)
    near = lax.ppermute(near, "atom", [(i, i ^ 1) for i in range(groups)])

    part = jnp.full((1,), lax.axis_index("aux"), jnp.int32)
    half, ints, columns, mix, meta, coef_part = stage(
        part, own, integrals, metric, atom_sizes, pair_device.T, pair_atom[None]
    )
    me = jnp.full((1,), lax.axis_index("atom"), jnp.int32)

    targets = pair_device[:, 0]
    order = jnp.arange(ref_count, dtype=jnp.int32)
    earlier = (targets[:, None] == targets[None, :]) & (order[None, :] < order[:, None])
    ranks = jnp.sum(earlier.astype(jnp.int32), axis=1)
    asked = targets * 2 + ranks
    place = (order % 2) * 256 + (order // 2) * MAXBF
    asked_hit = asked[None, :] == jnp.arange(2 * groups, dtype=jnp.int32)[:, None]
    places = 512 + pick(asked_hit, place[None, :] - 512)

    near, far, me, coef_part, asked, places = lax.optimization_barrier(
        (near, far, me, coef_part, asked, places)
    )
    odd = jnp.full((1,), odd, jnp.int32)
    packed = fit(odd, near, far, half, ints, columns, mix, meta)
    got = lax.all_to_all(packed, "atom", split_axis=0, concat_axis=0, tiled=True)
    table, sent = pair_sums(me, coef_part, got)
    owned = lax.all_to_all(sent, "atom", split_axis=0, concat_axis=0, tiled=True)
    own_sums = jnp.sum(owned[:, : 4 * MAXBF].astype(jnp.float32), axis=0).astype(jnp.bfloat16)
    shared = jnp.broadcast_to(own_sums[None], (aux_count,) + own_sums.shape)
    parts = lax.all_to_all(shared, "aux", split_axis=0, concat_axis=0, tiled=True)
    slots = make_slots(scale, asked, places, parts, owned)
    slots = lax.all_to_all(slots, "atom", split_axis=0, concat_axis=0, tiled=True)
    result = add_gains(table, slots, 2 * occ_part, bas_dev)
    return result.reshape(2, occ_part, bas_dev).transpose(2, 0, 1)


def solution(mesh):
    placed = (
        P("aux", "atom", None),
        P("atom", None, None),
        P("aux", None),
        P("atom", None),
        P("atom", None),
        P("atom"),
    )
    return jax.shard_map(
        per_device, mesh=mesh, in_specs=placed, out_specs=P("atom", None, "aux"), check_vma=False
    )
```

```python
import math

import jax
import jax.numpy as jnp
from jax import lax
from jax.experimental import pallas as pl
from jax.experimental.pallas import tpu as pltpu
from jax.sharding import PartitionSpec as P

MAXBF = 16
ROWBLK = 32
PACKED = ROWBLK + ROWBLK // 2
BATCH = 32
MIB = 1 << 20


def iota(shape, dim):
    return lax.broadcasted_iota(jnp.int32, shape, dim)


def dot(a, b):
    return jnp.dot(a, b, preferred_element_type=jnp.float32)


def dot_nt(a, b):
    return lax.dot_general(a, b, (((1,), (1,)), ((), ())), preferred_element_type=jnp.float32)


def dot_tn(a, b):
    return lax.dot_general(a, b, (((0,), (0,)), ((), ())), preferred_element_type=jnp.float32)


def ordered(part_ref, order_ref, window_ref, at):
    rows = part_ref.shape[0]
    half = part_ref.shape[1] // 2
    for t in range(3):
        real = part_ref[:, t * 128 : (t + 1) * 128]
        imag = part_ref[:, half + t * 128 : half + (t + 1) * 128]
        value = dot(jnp.concatenate([real, imag], axis=1), order_ref[t // 2])
        place = pl.ds(at if isinstance(at, int) else pl.multiple_of(at, 64), rows)
        window_ref[place, t * 256 : (t + 1) * 256] = value.astype(jnp.bfloat16)


def stage_kernel(
    part_ref, own_ref, ints_hbm, metric_hbm, size_hbm, dev_hbm, atom_hbm,
    half_ref, ints_ref, order_ref, mix_ref, meta_ref, coef_ref,
    window_ref, metric_ref, size_ref, dev_ref, atom_ref, rows_ref, sem_ref,
):
    sources = (ints_hbm, metric_hbm, size_hbm, dev_hbm, atom_hbm)
    targets = (ints_ref, metric_ref, size_ref, dev_ref, atom_ref)
    fetches = [
        pltpu.make_async_copy(a, b, sem_ref.at[i]) for i, (a, b) in enumerate(zip(sources, targets))
    ]
    for fetch in fetches:
        fetch.start()
    u, v = iota((256, 256), 0), iota((256, 256), 1)
    main_order = u == ((v % 128) // 64) * 128 + (v // 128) * 64 + v % 64
    side_order = u == ((v % 64) // 32) * 128 + (v // 64) * 32 + v % 32
    order_ref[0] = jnp.where(main_order, 1.0, 0.0).astype(jnp.bfloat16)
    order_ref[1] = jnp.where(side_order, 1.0, 0.0).astype(jnp.bfloat16)
    ordered(own_ref, order_ref, window_ref, 0)
    width = own_ref.shape[1]
    part = width // 16
    row, lane = iota((width, 128), 0), iota((width, 128), 1)
    source = part_ref[0] * part + jnp.where(lane < part, lane, lane + width // 2 - part)
    chosen = jnp.where((row == source) & (lane < 2 * part), 1.0, 0.0).astype(jnp.bfloat16)
    coef_ref[...] = dot(own_ref[...], chosen).astype(jnp.bfloat16)
    for fetch in fetches[1:]:
        fetch.wait()
    member = iota((256, 8), 0) // ROWBLK == iota((256, 8), 1)
    member = jnp.where(member, 1.0, 0.0).astype(jnp.bfloat16)
    mix = dot_nt(dot_nt(member, metric_ref[...]).astype(jnp.bfloat16), member)
    mix_ref[...] = jnp.where(u % ROWBLK == v % ROWBLK, mix, 0.0).astype(jnp.bfloat16)
    rows_ref[...] = jnp.zeros(rows_ref.shape, jnp.float32)
    for row, value_ref in enumerate((size_ref, dev_ref, atom_ref)):
        rows_ref[row : row + 1, 0 : value_ref.shape[1]] = value_ref[...].astype(jnp.float32)
    meta_ref[...] = rows_ref[...].astype(jnp.bfloat16)
    fetches[0].wait()
    aux_dev, bas_dev, span = ints_ref.shape
    halo = (span - bas_dev) // 2
    step = bas_dev // 2
    for u in range(2):
        rows = slice(u * step, (u + 1) * step)
        ints = ints_ref[:, rows, halo : halo + bas_dev].reshape(aux_dev * step, bas_dev)
        half_ref[:, rows] = dot(ints, window_ref[...]).reshape(aux_dev, step, -1)


def fit_kernel(
    odd_ref, near_ref, far_ref, rest_ref, half_ref, ints_ref, order_ref, mix_ref, meta_ref, out_ref,
    window_ref,
):
    aux_dev, bas_dev, span = ints_ref.shape
    blocks = bas_dev // ROWBLK
    halo = near_ref.shape[0]
    far_at = odd_ref[0] * halo
    ordered(near_ref, order_ref, window_ref, halo - far_at)
    ordered(far_ref, order_ref, window_ref, far_at)
    ordered(rest_ref, order_ref, window_ref, far_at + halo // 2)
    mix = mix_ref[...]
    left = iota((ROWBLK // 2, 128), 1) < 64
    for u in range(blocks):
        if u % 4 == 0:
            rows = slice(u * ROWBLK, (u + 4) * ROWBLK)
            low, high = ints_ref[:, rows, 0:halo], ints_ref[:, rows, span - halo : span]
            ints = jnp.concatenate([low, high], axis=2).reshape(-1, 2 * halo)
            wide = dot(ints, window_ref[...]) + half_ref[:, rows].reshape(ints.shape[0], -1)
            wide = wide.astype(jnp.bfloat16)
            wide = wide.reshape(aux_dev, 4 * ROWBLK, -1)
        at = (u % 4) * ROWBLK
        half = wide[:, at : at + ROWBLK].reshape(aux_dev * ROWBLK, -1)
        fitted = dot(mix, half)
        main = slice(u * PACKED, u * PACKED + ROWBLK)
        side = slice(u * PACKED + ROWBLK, (u + 1) * PACKED)
        for p in range(aux_dev):
            rows = fitted[p * ROWBLK : (p + 1) * ROWBLK]
            for k in range(4):
                tile = rows[:, k * 128 : (k + 1) * 128]
                out_ref[p * 4 + k, main] = tile.astype(jnp.bfloat16)
            for k in range(2):
                shared = rows[:, 512 + k * 128 : 640 + k * 128]
                top, bottom = shared[: ROWBLK // 2], shared[ROWBLK // 2 :]
                even = jnp.where(left, top, pltpu.roll(bottom, 64, 1))
                odd = jnp.where(left, pltpu.roll(top, 64, 1), bottom)
                out_ref[p * 4 + 2 * k, side] = even.astype(jnp.bfloat16)
                out_ref[p * 4 + 2 * k + 1, side] = odd.astype(jnp.bfloat16)
        if u == blocks - 1:
            for d in range(4 * aux_dev):
                out_ref[d, blocks * PACKED : blocks * PACKED + 8] = meta_ref[...]


def end_table(me, got_ref, size_ref, dev_ref, atom_ref):
    groups, at = got_ref.shape[0], got_ref.shape[1] - 8
    for d in range(groups):
        rows = got_ref[d, at : at + 8].astype(jnp.float32)
        for i, dest in enumerate((size_ref, dev_ref, atom_ref)):
            dest[d : d + 1] = rows[i : i + 1]
    before = jnp.where(iota((128, 128), 0) < iota((128, 128), 1), 1.0, 0.0).astype(jnp.bfloat16)
    sizes = size_ref[...]
    packed = dot(sizes.astype(jnp.bfloat16), before) * 32.0 + sizes
    devices = dev_ref[...].astype(jnp.int32)
    atoms = atom_ref[...].astype(jnp.int32)
    found = jnp.zeros(packed.shape, jnp.float32)
    for d in range(groups):
        row = jnp.broadcast_to(packed[d : d + 1], packed.shape)
        found = jnp.where(devices == d, jnp.take_along_axis(row, atoms, axis=1), found)
    found = found.astype(jnp.int32)
    starts, counts = found // 32, found % 32
    lane = iota(found.shape, 1)
    here = (devices == me) & (lane < 32)
    rank = dot(jnp.where(here, 1.0, 0.0).astype(jnp.bfloat16), before)
    table = jnp.where(lane < 32, devices * 256 + starts, 0)
    for i, value in enumerate((starts, counts)):
        value = value.astype(jnp.float32)
        for r in range(2):
            one = jnp.sum(jnp.where(here & (rank == r), value, 0.0), axis=1, keepdims=True)
            table = jnp.where(lane == 32 + 2 * i + r, one.astype(jnp.int32), table)
    return table


def pair_kernel(
    me_ref, coef_ref, got_ref, slot_ref, out_ref, real_ref, imag_ref, rows_ref, table_ref,
    size_ref, dev_ref, atom_ref, row_ref, table_sem, *sides,
):
    table = end_table(me_ref[0], got_ref, size_ref, dev_ref, atom_ref)
    table_ref[...] = table
    fetch = pltpu.make_async_copy(table_ref, row_ref, table_sem)
    fetch.start()
    groups, blocks = got_ref.shape[0], got_ref.shape[1] // PACKED
    lane = iota((ROWBLK // 2, 128), 1)
    left, valid = lane < 64, lane < 96

    def unpack(b, carry):
        for i in range(blocks):
            base = pl.multiple_of(b * (blocks * ROWBLK) + i * ROWBLK, ROWBLK)
            shared = got_ref[b, i * PACKED + ROWBLK : (i + 1) * PACKED].astype(jnp.float32)
            for h in range(2):
                at = i * PACKED + h * 16
                main = got_ref[b, at : at + 16].astype(jnp.float32)
                real = shared if h else pltpu.roll(shared, 64, 1)
                imag = pltpu.roll(shared, 96 if h else 32, 1)
                real = jnp.where(left, main, jnp.where(valid, real, 0.0))
                imag = jnp.where(left, pltpu.roll(main, 64, 1), jnp.where(valid, imag, 0.0))
                real_ref[pl.ds(base + h * 16, 16)] = real
                imag_ref[pl.ds(base + h * 16, 16)] = imag
        return carry

    lax.fori_loop(0, groups, unpack, 0, unroll=16)
    tail = groups * blocks * ROWBLK
    real_ref[tail : tail + MAXBF] = jnp.zeros((MAXBF, 128), jnp.float32)
    imag_ref[tail : tail + MAXBF] = jnp.zeros((MAXBF, 128), jnp.float32)
    bas_dev = coef_ref.shape[0]
    rows_ref[...] = jnp.zeros(rows_ref.shape, jnp.float32)
    rows_ref[0:bas_dev] = coef_ref[...].astype(jnp.float32)
    row_id = iota((MAXBF, 128), 0)
    lane_pair = lane // MAXBF
    batch = len(sides) // 4
    slot_ref[...] = jnp.zeros(slot_ref.shape, jnp.int32)
    slot_ref[:, 0:groups] = table.astype(jnp.float32).T[32:40].astype(jnp.int32)
    fetch.wait()

    def group(step, carry):
        for u in range(batch):
            g = step * batch + u
            for h in range(2):
                first_ref, second_ref = sides[u * 4 + h * 2], sides[u * 4 + h * 2 + 1]
                for j in range(16):
                    row = pl.ds(row_ref[g, h * 16 + j], 16)
                    place = (j // 2) * MAXBF
                    real, imag = real_ref[row], imag_ref[row]
                    if j % 2:
                        second_ref[place : place + 16, 0:128] = real.astype(jnp.bfloat16)
                        second_ref[place : place + 16, 128:256] = imag.astype(jnp.bfloat16)
                    else:
                        first_ref[place : place + 16, 0:128] = real.astype(jnp.bfloat16)
                        first_ref[place : place + 16, 128:256] = imag.astype(jnp.bfloat16)
                        place += 128
                        first_ref[place : place + 16, 0:128] = imag.astype(jnp.bfloat16)
                        first_ref[place : place + 16, 128:256] = (-real).astype(jnp.bfloat16)
                value = dot_nt(first_ref[...], second_ref[...])
                for c in range(2):
                    part = value[c * 128 : c * 128 + 16]
                    for j in range(1, 8):
                        here = value[c * 128 + j * 16 : c * 128 + j * 16 + 16]
                        part = jnp.where(lane_pair == j, here, part)
                    at = h * 32 + c * 16
                    out_ref[g, at : at + 16] = part.astype(jnp.bfloat16)
            rows = []
            for r in range(2):
                value = rows_ref[pl.ds(row_ref[g, 32 + r], MAXBF)]
                rows.append(jnp.where(row_id < row_ref[g, 34 + r], value, 0.0))
            rest = pltpu.roll(rows[1], 96, 1)
            out_ref[g, 64:80] = jnp.where(valid, rows[0], rest).astype(jnp.bfloat16)
            rest = jnp.where(left[0:8], rest[0:8], pltpu.roll(rest[8:16], 64, 1))
            out_ref[g, 80:88] = rest.astype(jnp.bfloat16)
        return carry

    lax.fori_loop(0, groups // batch, group, 0)


def slot_kernel(scale, asked_ref, place_ref, parts_ref, got_ref, out_ref, tile_ref):
    total = parts_ref[0].astype(jnp.float32)
    for z in range(1, parts_ref.shape[0]):
        total = total + parts_ref[z].astype(jnp.float32)
    kernel = (total * scale).astype(jnp.bfloat16)
    u, v = iota((128, 128), 0), iota((128, 128), 1)
    same = u // MAXBF == v // MAXBF
    folds = [jnp.where(v == 96 + c * 16 + u % 16, 1.0, 0.0).astype(jnp.bfloat16) for c in range(2)]
    u, v = iota((32, 128), 0), iota((32, 128), 1)
    turned = jnp.where(v == 96 + u, jnp.where(u < MAXBF, 1.0, -1.0), 0.0).astype(jnp.bfloat16)

    lane = iota((MAXBF, 128), 1)

    def coef(e):
        source = asked_ref[e] // 2
        rows = got_ref[source, 64:80].astype(jnp.float32)
        rest = got_ref[source, 80:88].astype(jnp.float32)
        rest = jnp.concatenate([rest, pltpu.roll(rest, 64, 1)], axis=0)
        second = jnp.where(lane < 64, rest, jnp.where(lane < 96, 0.0, rows))
        second = pltpu.roll(second, 32, 1)
        first = jnp.where(lane < 96, rows, 0.0)
        return jnp.where(asked_ref[e] % 2 == 1, second, first)

    for h in range(2):
        block = kernel[h * 32 : (h + 1) * 32]
        first = jnp.zeros((128, 128), jnp.float32)
        for c in range(2):
            tile = block[c * MAXBF : (c + 1) * MAXBF].astype(jnp.float32)
            wide = jnp.where(same, jnp.concatenate([tile] * 8, axis=0), 0.0)
            first = first + dot(wide.astype(jnp.bfloat16), folds[c])
        second = dot_tn(block, turned)
        for j in range(8):
            pair, rows = h * 8 + j, slice(j * MAXBF, (j + 1) * MAXBF)
            at = pair * MAXBF
            tile = first[rows] + coef(2 * pair + 1)
            tile_ref[at : at + MAXBF] = tile.astype(jnp.bfloat16)
            tile = second[rows] + coef(2 * pair)
            tile_ref[256 + at : 256 + at + MAXBF] = tile.astype(jnp.bfloat16)
    tile_ref[512:528] = jnp.zeros((MAXBF, 128), jnp.bfloat16)
    for s in range(2 * out_ref.shape[0]):
        rows = tile_ref[pl.ds(pl.multiple_of(place_ref[s], MAXBF), MAXBF)]
        out_ref[s // 2, (s % 2) * MAXBF : (s % 2 + 1) * MAXBF] = rows


def gain_kernel(table_ref, slot_ref, out_ref, sum_ref, turned_ref):
    groups, rows, _ = slot_ref.shape
    width, bas_dev = out_ref.shape
    half = width // 2
    u, v = iota((128, 128), 0), iota((128, 128), 1)
    turn = jnp.where((v < half) & (u == v + half), -1.0, 0.0)
    turn = jnp.where((v >= half) & (v < width) & (u == v - half), 1.0, turn).astype(jnp.bfloat16)
    turned = dot(slot_ref[...].reshape(groups * rows, 128), turn).astype(jnp.bfloat16)
    turned_ref[...] = turned.reshape(groups, rows, 128)
    sum_ref[...] = jnp.zeros(sum_ref.shape, jnp.float32)
    lane, row_id = iota((MAXBF, 128), 1), iota((MAXBF, 128), 0)
    for g in range(groups):
        slots = slot_ref[g]
        wide = slots.astype(jnp.float32)
        tiles = []
        for r in range(2):
            tile = wide[r * MAXBF : (r + 1) * MAXBF]
            real = jnp.where(lane // MAXBF == r, pltpu.roll(tile, 32 + 16 * r, 1), 0.0)
            imag = jnp.where(lane // MAXBF == 2 + r, pltpu.roll(tile, 48 + 16 * r, 1), 0.0)
            tiles.append(real + imag)
        tiles = jnp.concatenate(tiles, axis=0)[:, 0:64].astype(jnp.bfloat16)
        gains = dot(tiles, jnp.concatenate([slots, turned_ref[g]], axis=0))
        for r in range(2):
            part = gains[r * MAXBF : (r + 1) * MAXBF]
            part = jnp.where(row_id < table_ref[2 + r, g], part, 0.0)
            where = pl.ds(table_ref[r, g], MAXBF)
            sum_ref[where] = sum_ref[where] + part
    out_ref[...] = sum_ref[0:bas_dev].T[0:width]


def vmem_spec():
    return pl.BlockSpec(memory_space=pltpu.VMEM)


def smem_spec():
    return pl.BlockSpec(memory_space=pltpu.SMEM)


def limit(mib):
    return pltpu.CompilerParams(vmem_limit_bytes=mib * MIB)


def in_hbm(array):
    return pltpu.with_memory_space_constraint(array, pltpu.HBM)


def stage(part, own, *fetched):
    shapes = [fetched[0].shape, (2, 256, 256), (256, 256), (8, 128), (own.shape[0], 128)]
    half = fetched[0].shape[:2] + own.shape[1:]
    return pl.pallas_call(
        stage_kernel,
        in_specs=[smem_spec(), vmem_spec()]
        + [pl.BlockSpec(memory_space=pltpu.HBM)] * len(fetched),
        out_specs=[vmem_spec()] * (len(shapes) + 1),
        out_shape=[pltpu.VMEM(half, jnp.float32)]
        + [pltpu.VMEM(shape, jnp.bfloat16) for shape in shapes],
        scratch_shapes=[pltpu.VMEM(own.shape, jnp.bfloat16)]
        + [pltpu.VMEM(x.shape, x.dtype) for x in fetched[1:]]
        + [pltpu.VMEM((8, 128), jnp.float32), pltpu.SemaphoreType.DMA((len(fetched),))],
        compiler_params=limit(24),
        cost_estimate=pl.CostEstimate(flops=1 << 28, bytes_accessed=5 * MIB, transcendentals=0),
        name="stage",
    )(part, own, *[in_hbm(x) for x in fetched])


def fit(odd, near, far, rest, half, ints, order, mix, meta):
    aux_dev, bas_dev, window = ints.shape
    width = near.shape[1]
    blocks = bas_dev // ROWBLK
    shape = (4 * aux_dev, blocks * PACKED + 8, 128)
    return pl.pallas_call(
        fit_kernel,
        in_specs=[smem_spec()] + [vmem_spec()] * 8,
        out_specs=vmem_spec(),
        out_shape=jax.ShapeDtypeStruct(shape, jnp.bfloat16),
        scratch_shapes=[pltpu.VMEM((window - bas_dev, width), jnp.bfloat16)],
        compiler_params=limit(32),
        cost_estimate=pl.CostEstimate(
            flops=2 * aux_dev * bas_dev * width * (window + 256),
            bytes_accessed=6 * MIB,
            transcendentals=0,
        ),
        name="fit",
    )(odd, near, far, rest, half, ints, order, mix, meta)


def pair_sums(me, coef, got):
    groups = got.shape[0]
    rows = groups * (got.shape[1] // PACKED) * ROWBLK + MAXBF
    shape = (groups, 88, 128)
    return pl.pallas_call(
        pair_kernel,
        in_specs=[smem_spec(), vmem_spec(), vmem_spec()],
        out_specs=[vmem_spec()] * 2,
        out_shape=[
            jax.ShapeDtypeStruct((8, 128), jnp.int32),
            jax.ShapeDtypeStruct(shape, jnp.bfloat16),
        ],
        scratch_shapes=[
            pltpu.VMEM((rows, 128), jnp.float32),
            pltpu.VMEM((rows, 128), jnp.float32),
            pltpu.VMEM((coef.shape[0] + MAXBF, 128), jnp.float32),
            pltpu.VMEM((groups, 128), jnp.int32),
            pltpu.VMEM((groups, 128), jnp.float32),
            pltpu.VMEM((groups, 128), jnp.float32),
            pltpu.VMEM((groups, 128), jnp.float32),
            pltpu.SMEM((groups, 128), jnp.int32),
            pltpu.SemaphoreType.DMA,
        ]
        + [pltpu.VMEM((256, 256), jnp.bfloat16), pltpu.VMEM((128, 256), jnp.bfloat16)] * (2 * BATCH),
        compiler_params=limit(40),
        name="pair_sums",
    )(me, coef, got)


def make_slots(scale, asked, places, parts, got):
    def body(*refs):
        slot_kernel(scale, *refs)

    return pl.pallas_call(
        body,
        in_specs=[smem_spec()] * 2 + [vmem_spec()] * 2,
        out_specs=vmem_spec(),
        out_shape=jax.ShapeDtypeStruct((got.shape[0], 2 * MAXBF, 128), jnp.bfloat16),
        scratch_shapes=[pltpu.VMEM((528, 128), jnp.bfloat16)],
        compiler_params=limit(16),
        name="make_slots",
    )(asked, places, parts, got)


def add_gains(table, slots, width, bas_dev):
    return pl.pallas_call(
        gain_kernel,
        in_specs=[smem_spec(), vmem_spec()],
        out_specs=vmem_spec(),
        out_shape=jax.ShapeDtypeStruct((width, bas_dev), jnp.float32),
        scratch_shapes=[
            pltpu.VMEM((bas_dev + MAXBF, 128), jnp.float32),
            pltpu.VMEM(slots.shape, jnp.bfloat16),
        ],
        compiler_params=limit(16),
        name="add_gains",
    )(table, slots)


def pick(hit, values):
    return jnp.sum(jnp.where(hit, values, 0), axis=-1)


def per_device(integrals, coeffs, metric, atom_sizes, pair_device, pair_atom):
    aux_dev, bas_dev, window = integrals.shape
    occ = coeffs.shape[2]
    groups = lax.axis_size("atom")
    aux_count = lax.axis_size("aux")
    occ_part = occ // aux_count
    ref_count = pair_atom.shape[0]
    halo = (window - bas_dev) // 2
    scale = 1.0 / math.sqrt(2 * occ * aux_dev * aux_count * MAXBF)
    me = lax.axis_index("atom")

    own = coeffs.reshape(bas_dev, 2 * occ)
    odd = lax.axis_index("atom") % 2
    inner = range(1, groups - 1)
    far = lax.dynamic_slice_in_dim(own, odd * halo, halo, 0)
    across = [(i, i + 1 if i % 2 else i - 1) for i in inner]
    rest = lax.ppermute(far[halo // 2 :], "atom", across)
    far = lax.ppermute(far[: halo // 2], "atom", across)
    near = lax.dynamic_slice_in_dim(own, (1 - odd) * halo, halo, 0)
    near = lax.ppermute(near, "atom", [(i, i ^ 1) for i in range(groups)])

    part = jnp.full((1,), lax.axis_index("aux"), jnp.int32)
    half, ints, columns, mix, meta, coef_part = stage(
        part, own, integrals, metric, atom_sizes, pair_device.T, pair_atom[None]
    )
    me = jnp.full((1,), lax.axis_index("atom"), jnp.int32)

    targets = pair_device[:, 0]
    order = jnp.arange(ref_count, dtype=jnp.int32)
    earlier = (targets[:, None] == targets[None, :]) & (order[None, :] < order[:, None])
    ranks = jnp.sum(earlier.astype(jnp.int32), axis=1)
    asked = targets * 2 + ranks
    place = (order % 2) * 256 + (order // 2) * MAXBF
    asked_hit = asked[None, :] == jnp.arange(2 * groups, dtype=jnp.int32)[:, None]
    places = 512 + pick(asked_hit, place[None, :] - 512)

    near, far, rest, me, coef_part, asked, places = lax.optimization_barrier(
        (near, far, rest, me, coef_part, asked, places)
    )
    odd = jnp.full((1,), odd, jnp.int32)
    packed = fit(odd, near, far, rest, half, ints, columns, mix, meta)
    got = lax.all_to_all(packed, "atom", split_axis=0, concat_axis=0, tiled=True)
    table, sent = pair_sums(me, coef_part, got)
    owned = lax.all_to_all(sent, "atom", split_axis=0, concat_axis=0, tiled=True)
    own_sums = jnp.sum(owned[:, : 4 * MAXBF].astype(jnp.float32), axis=0).astype(jnp.bfloat16)
    shared = jnp.broadcast_to(own_sums[None], (aux_count,) + own_sums.shape)
    parts = lax.all_to_all(shared, "aux", split_axis=0, concat_axis=0, tiled=True)
    slots = make_slots(scale, asked, places, parts, owned)
    slots = lax.all_to_all(slots, "atom", split_axis=0, concat_axis=0, tiled=True)
    result = add_gains(table, slots, 2 * occ_part, bas_dev)
    return result.reshape(2, occ_part, bas_dev).transpose(2, 0, 1)


def solution(mesh):
    placed = (
        P("aux", "atom", None),
        P("atom", None, None),
        P("aux", None),
        P("atom", None),
        P("atom", None),
        P("atom"),
    )
    return jax.shard_map(
        per_device, mesh=mesh, in_specs=placed, out_specs=P("atom", None, "aux"), check_vma=False
    )
```

```python
import math

import jax
import jax.numpy as jnp
from jax import lax
from jax.experimental import pallas as pl
from jax.experimental.pallas import tpu as pltpu
from jax.sharding import PartitionSpec as P

MAXBF = 16
ROWBLK = 32
PACKED = ROWBLK + ROWBLK // 2
BATCH = 32
MIB = 1 << 20


def iota(shape, dim):
    return lax.broadcasted_iota(jnp.int32, shape, dim)


def dot(a, b):
    return jnp.dot(a, b, preferred_element_type=jnp.float32)


def dot_nt(a, b):
    return lax.dot_general(a, b, (((1,), (1,)), ((), ())), preferred_element_type=jnp.float32)


def dot_tn(a, b):
    return lax.dot_general(a, b, (((0,), (0,)), ((), ())), preferred_element_type=jnp.float32)


def ordered(part_ref, order_ref, window_ref, at):
    rows = part_ref.shape[0]
    half = part_ref.shape[1] // 2
    for t in range(3):
        real = part_ref[:, t * 128 : (t + 1) * 128]
        imag = part_ref[:, half + t * 128 : half + (t + 1) * 128]
        value = dot(jnp.concatenate([real, imag], axis=1), order_ref[t // 2])
        place = pl.ds(at if isinstance(at, int) else pl.multiple_of(at, 128), rows)
        window_ref[place, t * 256 : (t + 1) * 256] = value.astype(jnp.bfloat16)


def stage_kernel(
    part_ref, own_ref, ints_hbm, metric_hbm, size_hbm, dev_hbm, atom_hbm,
    half_ref, ints_ref, order_ref, mix_ref, meta_ref, coef_ref,
    window_ref, metric_ref, size_ref, dev_ref, atom_ref, rows_ref, sem_ref,
):
    sources = (ints_hbm, metric_hbm, size_hbm, dev_hbm, atom_hbm)
    targets = (ints_ref, metric_ref, size_ref, dev_ref, atom_ref)
    fetches = [
        pltpu.make_async_copy(a, b, sem_ref.at[i]) for i, (a, b) in enumerate(zip(sources, targets))
    ]
    for fetch in fetches:
        fetch.start()
    u, v = iota((256, 256), 0), iota((256, 256), 1)
    main_order = u == ((v % 128) // 64) * 128 + (v // 128) * 64 + v % 64
    side_order = u == ((v % 64) // 32) * 128 + (v // 64) * 32 + v % 32
    order_ref[0] = jnp.where(main_order, 1.0, 0.0).astype(jnp.bfloat16)
    order_ref[1] = jnp.where(side_order, 1.0, 0.0).astype(jnp.bfloat16)
    ordered(own_ref, order_ref, window_ref, 0)
    width = own_ref.shape[1]
    part = width // 16
    row, lane = iota((width, 128), 0), iota((width, 128), 1)
    source = part_ref[0] * part + jnp.where(lane < part, lane, lane + width // 2 - part)
    chosen = jnp.where((row == source) & (lane < 2 * part), 1.0, 0.0).astype(jnp.bfloat16)
    coef_ref[...] = dot(own_ref[...], chosen).astype(jnp.bfloat16)
    for fetch in fetches[1:]:
        fetch.wait()
    member = iota((256, 8), 0) // ROWBLK == iota((256, 8), 1)
    member = jnp.where(member, 1.0, 0.0).astype(jnp.bfloat16)
    mix = dot_nt(dot_nt(member, metric_ref[...]).astype(jnp.bfloat16), member)
    mix_ref[...] = jnp.where(u % ROWBLK == v % ROWBLK, mix, 0.0).astype(jnp.bfloat16)
    rows_ref[...] = jnp.zeros(rows_ref.shape, jnp.float32)
    for row, value_ref in enumerate((size_ref, dev_ref, atom_ref)):
        rows_ref[row : row + 1, 0 : value_ref.shape[1]] = value_ref[...].astype(jnp.float32)
    meta_ref[...] = rows_ref[...].astype(jnp.bfloat16)
    fetches[0].wait()
    aux_dev, bas_dev, span = ints_ref.shape
    halo = (span - bas_dev) // 2
    step = bas_dev // 2
    for u in range(2):
        rows = slice(u * step, (u + 1) * step)
        ints = ints_ref[:, rows, halo : halo + bas_dev].reshape(aux_dev * step, bas_dev)
        half_ref[:, rows] = dot(ints, window_ref[...]).reshape(aux_dev, step, -1)


def fit_kernel(
    odd_ref, near_ref, far_ref, half_ref, ints_ref, order_ref, mix_ref, meta_ref, out_ref,
    window_ref,
):
    aux_dev, bas_dev, span = ints_ref.shape
    blocks = bas_dev // ROWBLK
    halo = near_ref.shape[0]
    far_at = odd_ref[0] * halo
    ordered(near_ref, order_ref, window_ref, halo - far_at)
    ordered(far_ref, order_ref, window_ref, far_at)
    mix = mix_ref[...]
    left = iota((ROWBLK // 2, 128), 1) < 64
    for u in range(blocks):
        if u % 4 == 0:
            rows = slice(u * ROWBLK, (u + 4) * ROWBLK)
            low, high = ints_ref[:, rows, 0:halo], ints_ref[:, rows, span - halo : span]
            ints = jnp.concatenate([low, high], axis=2).reshape(-1, 2 * halo)
            wide = dot(ints, window_ref[...]) + half_ref[:, rows].reshape(ints.shape[0], -1)
            wide = wide.astype(jnp.bfloat16)
            wide = wide.reshape(aux_dev, 4 * ROWBLK, -1)
        at = (u % 4) * ROWBLK
        half = wide[:, at : at + ROWBLK].reshape(aux_dev * ROWBLK, -1)
        fitted = dot(mix, half)
        main = slice(u * PACKED, u * PACKED + ROWBLK)
        side = slice(u * PACKED + ROWBLK, (u + 1) * PACKED)
        for p in range(aux_dev):
            rows = fitted[p * ROWBLK : (p + 1) * ROWBLK]
            for k in range(4):
                tile = rows[:, k * 128 : (k + 1) * 128]
                out_ref[p * 4 + k, main] = tile.astype(jnp.bfloat16)
            for k in range(2):
                shared = rows[:, 512 + k * 128 : 640 + k * 128]
                top, bottom = shared[: ROWBLK // 2], shared[ROWBLK // 2 :]
                even = jnp.where(left, top, pltpu.roll(bottom, 64, 1))
                odd = jnp.where(left, pltpu.roll(top, 64, 1), bottom)
                out_ref[p * 4 + 2 * k, side] = even.astype(jnp.bfloat16)
                out_ref[p * 4 + 2 * k + 1, side] = odd.astype(jnp.bfloat16)
        if u == blocks - 1:
            for d in range(4 * aux_dev):
                out_ref[d, blocks * PACKED : blocks * PACKED + 8] = meta_ref[...]


def end_table(me, got_ref, size_ref, dev_ref, atom_ref):
    groups, at = got_ref.shape[0], got_ref.shape[1] - 8
    for d in range(groups):
        rows = got_ref[d, at : at + 8].astype(jnp.float32)
        for i, dest in enumerate((size_ref, dev_ref, atom_ref)):
            dest[d : d + 1] = rows[i : i + 1]
    before = jnp.where(iota((128, 128), 0) < iota((128, 128), 1), 1.0, 0.0).astype(jnp.bfloat16)
    sizes = size_ref[...]
    packed = dot(sizes.astype(jnp.bfloat16), before) * 32.0 + sizes
    devices = dev_ref[...].astype(jnp.int32)
    atoms = atom_ref[...].astype(jnp.int32)
    found = jnp.zeros(packed.shape, jnp.float32)
    for d in range(groups):
        row = jnp.broadcast_to(packed[d : d + 1], packed.shape)
        found = jnp.where(devices == d, jnp.take_along_axis(row, atoms, axis=1), found)
    found = found.astype(jnp.int32)
    starts, counts = found // 32, found % 32
    lane = iota(found.shape, 1)
    here = (devices == me) & (lane < 32)
    rank = dot(jnp.where(here, 1.0, 0.0).astype(jnp.bfloat16), before)
    table = jnp.where(lane < 32, devices * 256 + starts, 0)
    for i, value in enumerate((starts, counts)):
        value = value.astype(jnp.float32)
        for r in range(2):
            one = jnp.sum(jnp.where(here & (rank == r), value, 0.0), axis=1, keepdims=True)
            table = jnp.where(lane == 32 + 2 * i + r, one.astype(jnp.int32), table)
    return table


def pair_kernel(
    me_ref, coef_ref, got_ref, slot_ref, out_ref, real_ref, imag_ref, rows_ref, table_ref,
    size_ref, dev_ref, atom_ref, row_ref, table_sem, *sides,
):
    table = end_table(me_ref[0], got_ref, size_ref, dev_ref, atom_ref)
    table_ref[...] = table
    fetch = pltpu.make_async_copy(table_ref, row_ref, table_sem)
    fetch.start()
    groups, blocks = got_ref.shape[0], got_ref.shape[1] // PACKED
    lane = iota((ROWBLK // 2, 128), 1)
    left, valid = lane < 64, lane < 96

    def unpack(b, carry):
        for i in range(blocks):
            base = pl.multiple_of(b * (blocks * ROWBLK) + i * ROWBLK, ROWBLK)
            shared = got_ref[b, i * PACKED + ROWBLK : (i + 1) * PACKED].astype(jnp.float32)
            for h in range(2):
                at = i * PACKED + h * 16
                main = got_ref[b, at : at + 16].astype(jnp.float32)
                real = shared if h else pltpu.roll(shared, 64, 1)
                imag = pltpu.roll(shared, 96 if h else 32, 1)
                real = jnp.where(left, main, jnp.where(valid, real, 0.0))
                imag = jnp.where(left, pltpu.roll(main, 64, 1), jnp.where(valid, imag, 0.0))
                real_ref[pl.ds(base + h * 16, 16)] = real
                imag_ref[pl.ds(base + h * 16, 16)] = imag
        return carry

    lax.fori_loop(0, groups, unpack, 0, unroll=16)
    tail = groups * blocks * ROWBLK
    real_ref[tail : tail + MAXBF] = jnp.zeros((MAXBF, 128), jnp.float32)
    imag_ref[tail : tail + MAXBF] = jnp.zeros((MAXBF, 128), jnp.float32)
    bas_dev = coef_ref.shape[0]
    rows_ref[...] = jnp.zeros(rows_ref.shape, jnp.float32)
    rows_ref[0:bas_dev] = coef_ref[...].astype(jnp.float32)
    row_id = iota((MAXBF, 128), 0)
    lane_pair = lane // MAXBF
    batch = len(sides) // 4
    slot_ref[...] = jnp.zeros(slot_ref.shape, jnp.int32)
    slot_ref[:, 0:groups] = table.astype(jnp.float32).T[32:40].astype(jnp.int32)
    fetch.wait()

    def group(step, carry):
        for u in range(batch):
            g = step * batch + u
            for h in range(2):
                first_ref, second_ref = sides[u * 4 + h * 2], sides[u * 4 + h * 2 + 1]
                for j in range(16):
                    row = pl.ds(row_ref[g, h * 16 + j], 16)
                    place = (j // 2) * MAXBF
                    real, imag = real_ref[row], imag_ref[row]
                    if j % 2:
                        second_ref[place : place + 16, 0:128] = real.astype(jnp.bfloat16)
                        second_ref[place : place + 16, 128:256] = imag.astype(jnp.bfloat16)
                    else:
                        first_ref[place : place + 16, 0:128] = real.astype(jnp.bfloat16)
                        first_ref[place : place + 16, 128:256] = imag.astype(jnp.bfloat16)
                        place += 128
                        first_ref[place : place + 16, 0:128] = imag.astype(jnp.bfloat16)
                        first_ref[place : place + 16, 128:256] = (-real).astype(jnp.bfloat16)
                value = dot_nt(first_ref[...], second_ref[...])
                for c in range(2):
                    part = value[c * 128 : c * 128 + 16]
                    for j in range(1, 8):
                        here = value[c * 128 + j * 16 : c * 128 + j * 16 + 16]
                        part = jnp.where(lane_pair == j, here, part)
                    at = h * 32 + c * 16
                    out_ref[g, at : at + 16] = part.astype(jnp.bfloat16)
            rows = []
            for r in range(2):
                value = rows_ref[pl.ds(row_ref[g, 32 + r], MAXBF)]
                rows.append(jnp.where(row_id < row_ref[g, 34 + r], value, 0.0))
            rest = pltpu.roll(rows[1], 96, 1)
            out_ref[g, 64:80] = jnp.where(valid, rows[0], rest).astype(jnp.bfloat16)
            rest = jnp.where(left[0:8], rest[0:8], pltpu.roll(rest[8:16], 64, 1))
            out_ref[g, 80:88] = rest.astype(jnp.bfloat16)
        return carry

    lax.fori_loop(0, groups // batch, group, 0)


def slot_kernel(scale, asked_ref, place_ref, parts_ref, got_ref, out_ref, tile_ref):
    total = parts_ref[0].astype(jnp.float32)
    for z in range(1, parts_ref.shape[0]):
        total = total + parts_ref[z].astype(jnp.float32)
    kernel = (total * scale).astype(jnp.bfloat16)
    u, v = iota((128, 128), 0), iota((128, 128), 1)
    same = u // MAXBF == v // MAXBF
    folds = [jnp.where(v == 96 + c * 16 + u % 16, 1.0, 0.0).astype(jnp.bfloat16) for c in range(2)]
    u, v = iota((32, 128), 0), iota((32, 128), 1)
    turned = jnp.where(v == 96 + u, jnp.where(u < MAXBF, 1.0, -1.0), 0.0).astype(jnp.bfloat16)

    lane = iota((MAXBF, 128), 1)

    def coef(e):
        source = asked_ref[e] // 2
        rows = got_ref[source, 64:80].astype(jnp.float32)
        rest = got_ref[source, 80:88].astype(jnp.float32)
        rest = jnp.concatenate([rest, pltpu.roll(rest, 64, 1)], axis=0)
        second = jnp.where(lane < 64, rest, jnp.where(lane < 96, 0.0, rows))
        second = pltpu.roll(second, 32, 1)
        first = jnp.where(lane < 96, rows, 0.0)
        return jnp.where(asked_ref[e] % 2 == 1, second, first)

    for h in range(2):
        block = kernel[h * 32 : (h + 1) * 32]
        first = jnp.zeros((128, 128), jnp.float32)
        for c in range(2):
            tile = block[c * MAXBF : (c + 1) * MAXBF].astype(jnp.float32)
            wide = jnp.where(same, jnp.concatenate([tile] * 8, axis=0), 0.0)
            first = first + dot(wide.astype(jnp.bfloat16), folds[c])
        second = dot_tn(block, turned)
        for j in range(8):
            pair, rows = h * 8 + j, slice(j * MAXBF, (j + 1) * MAXBF)
            at = pair * MAXBF
            tile = first[rows] + coef(2 * pair + 1)
            tile_ref[at : at + MAXBF] = tile.astype(jnp.bfloat16)
            tile = second[rows] + coef(2 * pair)
            tile_ref[256 + at : 256 + at + MAXBF] = tile.astype(jnp.bfloat16)
    tile_ref[512:528] = jnp.zeros((MAXBF, 128), jnp.bfloat16)
    for s in range(2 * out_ref.shape[0]):
        rows = tile_ref[pl.ds(pl.multiple_of(place_ref[s], MAXBF), MAXBF)]
        out_ref[s // 2, (s % 2) * MAXBF : (s % 2 + 1) * MAXBF] = rows


def gain_kernel(table_ref, slot_ref, out_ref, sum_ref, turned_ref):
    groups, rows, _ = slot_ref.shape
    width, bas_dev = out_ref.shape
    half = width // 2
    u, v = iota((128, 128), 0), iota((128, 128), 1)
    turn = jnp.where((v < half) & (u == v + half), -1.0, 0.0)
    turn = jnp.where((v >= half) & (v < width) & (u == v - half), 1.0, turn).astype(jnp.bfloat16)
    turned = dot(slot_ref[...].reshape(groups * rows, 128), turn).astype(jnp.bfloat16)
    turned_ref[...] = turned.reshape(groups, rows, 128)
    sum_ref[...] = jnp.zeros(sum_ref.shape, jnp.float32)
    lane, row_id = iota((MAXBF, 128), 1), iota((MAXBF, 128), 0)
    for g in range(groups):
        slots = slot_ref[g]
        wide = slots.astype(jnp.float32)
        tiles = []
        for r in range(2):
            tile = wide[r * MAXBF : (r + 1) * MAXBF]
            real = jnp.where(lane // MAXBF == r, pltpu.roll(tile, 32 + 16 * r, 1), 0.0)
            imag = jnp.where(lane // MAXBF == 2 + r, pltpu.roll(tile, 48 + 16 * r, 1), 0.0)
            tiles.append(real + imag)
        tiles = jnp.concatenate(tiles, axis=0)[:, 0:64].astype(jnp.bfloat16)
        gains = dot(tiles, jnp.concatenate([slots, turned_ref[g]], axis=0))
        for r in range(2):
            part = gains[r * MAXBF : (r + 1) * MAXBF]
            part = jnp.where(row_id < table_ref[2 + r, g], part, 0.0)
            where = pl.ds(table_ref[r, g], MAXBF)
            sum_ref[where] = sum_ref[where] + part
    out_ref[...] = sum_ref[0:bas_dev].T[0:width]


def vmem_spec():
    return pl.BlockSpec(memory_space=pltpu.VMEM)


def smem_spec():
    return pl.BlockSpec(memory_space=pltpu.SMEM)


def limit(mib):
    return pltpu.CompilerParams(vmem_limit_bytes=mib * MIB)


def in_hbm(array):
    return pltpu.with_memory_space_constraint(array, pltpu.HBM)


def stage(part, own, *fetched):
    shapes = [fetched[0].shape, (2, 256, 256), (256, 256), (8, 128), (own.shape[0], 128)]
    half = fetched[0].shape[:2] + own.shape[1:]
    return pl.pallas_call(
        stage_kernel,
        in_specs=[smem_spec(), vmem_spec()]
        + [pl.BlockSpec(memory_space=pltpu.HBM)] * len(fetched),
        out_specs=[vmem_spec()] * (len(shapes) + 1),
        out_shape=[pltpu.VMEM(half, jnp.float32)]
        + [pltpu.VMEM(shape, jnp.bfloat16) for shape in shapes],
        scratch_shapes=[pltpu.VMEM(own.shape, jnp.bfloat16)]
        + [pltpu.VMEM(x.shape, x.dtype) for x in fetched[1:]]
        + [pltpu.VMEM((8, 128), jnp.float32), pltpu.SemaphoreType.DMA((len(fetched),))],
        compiler_params=limit(24),
        cost_estimate=pl.CostEstimate(flops=1 << 28, bytes_accessed=5 * MIB, transcendentals=0),
        name="stage",
    )(part, own, *[in_hbm(x) for x in fetched])


def fit(odd, near, far, half, ints, order, mix, meta):
    aux_dev, bas_dev, window = ints.shape
    width = near.shape[1]
    blocks = bas_dev // ROWBLK
    shape = (4 * aux_dev, blocks * PACKED + 8, 128)
    return pl.pallas_call(
        fit_kernel,
        in_specs=[smem_spec()] + [vmem_spec()] * 7,
        out_specs=vmem_spec(),
        out_shape=jax.ShapeDtypeStruct(shape, jnp.bfloat16),
        scratch_shapes=[pltpu.VMEM((window - bas_dev, width), jnp.bfloat16)],
        compiler_params=limit(32),
        cost_estimate=pl.CostEstimate(
            flops=2 * aux_dev * bas_dev * width * (window + 256),
            bytes_accessed=6 * MIB,
            transcendentals=0,
        ),
        name="fit",
    )(odd, near, far, half, ints, order, mix, meta)


def pair_sums(me, coef, got):
    groups = got.shape[0]
    rows = groups * (got.shape[1] // PACKED) * ROWBLK + MAXBF
    shape = (groups, 88, 128)
    return pl.pallas_call(
        pair_kernel,
        in_specs=[smem_spec(), vmem_spec(), vmem_spec()],
        out_specs=[vmem_spec()] * 2,
        out_shape=[
            jax.ShapeDtypeStruct((8, 128), jnp.int32),
            jax.ShapeDtypeStruct(shape, jnp.bfloat16),
        ],
        scratch_shapes=[
            pltpu.VMEM((rows, 128), jnp.float32),
            pltpu.VMEM((rows, 128), jnp.float32),
            pltpu.VMEM((coef.shape[0] + MAXBF, 128), jnp.float32),
            pltpu.VMEM((groups, 128), jnp.int32),
            pltpu.VMEM((groups, 128), jnp.float32),
            pltpu.VMEM((groups, 128), jnp.float32),
            pltpu.VMEM((groups, 128), jnp.float32),
            pltpu.SMEM((groups, 128), jnp.int32),
            pltpu.SemaphoreType.DMA,
        ]
        + [pltpu.VMEM((256, 256), jnp.bfloat16), pltpu.VMEM((128, 256), jnp.bfloat16)] * (2 * BATCH),
        compiler_params=limit(40),
        name="pair_sums",
    )(me, coef, got)


def make_slots(scale, asked, places, parts, got):
    def body(*refs):
        slot_kernel(scale, *refs)

    return pl.pallas_call(
        body,
        in_specs=[smem_spec()] * 2 + [vmem_spec()] * 2,
        out_specs=vmem_spec(),
        out_shape=jax.ShapeDtypeStruct((got.shape[0], 2 * MAXBF, 128), jnp.bfloat16),
        scratch_shapes=[pltpu.VMEM((528, 128), jnp.bfloat16)],
        compiler_params=limit(16),
        name="make_slots",
    )(asked, places, parts, got)


def add_gains(table, slots, width, bas_dev):
    return pl.pallas_call(
        gain_kernel,
        in_specs=[smem_spec(), vmem_spec()],
        out_specs=vmem_spec(),
        out_shape=jax.ShapeDtypeStruct((width, bas_dev), jnp.float32),
        scratch_shapes=[
            pltpu.VMEM((bas_dev + MAXBF, 128), jnp.float32),
            pltpu.VMEM(slots.shape, jnp.bfloat16),
        ],
        compiler_params=limit(16),
        name="add_gains",
    )(table, slots)


def pick(hit, values):
    return jnp.sum(jnp.where(hit, values, 0), axis=-1)


def per_device(integrals, coeffs, metric, atom_sizes, pair_device, pair_atom):
    aux_dev, bas_dev, window = integrals.shape
    occ = coeffs.shape[2]
    groups = lax.axis_size("atom")
    aux_count = lax.axis_size("aux")
    occ_part = occ // aux_count
    ref_count = pair_atom.shape[0]
    halo = (window - bas_dev) // 2
    scale = 1.0 / math.sqrt(2 * occ * aux_dev * aux_count * MAXBF)
    me = lax.axis_index("atom")

    own = coeffs.reshape(bas_dev, 2 * occ)
    odd = lax.axis_index("atom") % 2
    inner = range(1, groups - 1)
    far = lax.dynamic_slice_in_dim(own, odd * halo, halo, 0)
    far = lax.ppermute(far, "atom", [(i, i + 1 if i % 2 else i - 1) for i in inner])
    near = lax.dynamic_slice_in_dim(own, (1 - odd) * halo, halo, 0)
    near = lax.ppermute(near, "atom", [(i, i ^ 1) for i in range(groups)])

    part = jnp.full((1,), lax.axis_index("aux"), jnp.int32)
    half, ints, columns, mix, meta, coef_part = stage(
        part, own, integrals, metric, atom_sizes, pair_device.T, pair_atom[None]
    )
    me = jnp.full((1,), lax.axis_index("atom"), jnp.int32)

    targets = pair_device[:, 0]
    order = jnp.arange(ref_count, dtype=jnp.int32)
    earlier = (targets[:, None] == targets[None, :]) & (order[None, :] < order[:, None])
    own_block = jnp.where(order[None, :] == order[:, None], 2 * targets[None, :], 0)
    asked = jnp.sum(earlier.astype(jnp.int32) + own_block, axis=1)
    place = (order % 2) * 256 + (order // 2) * MAXBF
    asked_hit = asked[None, :] == jnp.arange(2 * groups, dtype=jnp.int32)[:, None]
    places = 512 + pick(asked_hit, place[None, :] - 512)

    near, far, me, coef_part, asked, places = lax.optimization_barrier(
        (near, far, me, coef_part, asked, places)
    )
    odd = jnp.full((1,), odd, jnp.int32)
    packed = fit(odd, near, far, half, ints, columns, mix, meta)
    got = lax.all_to_all(packed, "atom", split_axis=0, concat_axis=0, tiled=True)
    table, sent = pair_sums(me, coef_part, got)
    owned = lax.all_to_all(sent, "atom", split_axis=0, concat_axis=0, tiled=True)
    own_sums = jnp.sum(owned[:, : 4 * MAXBF].astype(jnp.float32), axis=0).astype(jnp.bfloat16)
    shared = jnp.broadcast_to(own_sums[None], (aux_count,) + own_sums.shape)
    parts = lax.all_to_all(shared, "aux", split_axis=0, concat_axis=0, tiled=True)
    slots = make_slots(scale, asked, places, parts, owned)
    slots = lax.all_to_all(slots, "atom", split_axis=0, concat_axis=0, tiled=True)
    result = add_gains(table, slots, 2 * occ_part, bas_dev)
    return result.reshape(2, occ_part, bas_dev).transpose(2, 0, 1)


def solution(mesh):
    placed = (
        P("aux", "atom", None),
        P("atom", None, None),
        P("aux", None),
        P("atom", None),
        P("atom", None),
        P("atom"),
    )
    return jax.shard_map(
        per_device, mesh=mesh, in_specs=placed, out_specs=P("atom", None, "aux"), check_vma=False
    )
```
